32 devices in a mesh: dp: 8 (over y, x, core), tensor: 4 (over z).
Axes of the slice: x: 2, y: 2, z: 4, core: 2. Of those that a mesh axis runs over, the one named last changes fastest.
Arguments:
- block_input: bfloat16 [8, 1024, 1024], P('dp', 'tensor'), may hold values from -6 to 6
- piece_starts: int32 [8, 2], P('dp'), may hold values from 0 to 768
- attn_gain: bfloat16 [1024], P('dp'), may hold values from 0.5 to 1.5
- q_gain: bfloat16 [128], P('dp'), may hold values from 0.5 to 1.5
- k_gain: bfloat16 [128], P('dp'), may hold values from 0.5 to 1.5
- w_query: bfloat16 [1024, 2048], P('dp', 'tensor'), may hold values from -0.1875 to 0.1875
- key_projection_weight: bfloat16 [1024, 1024], P('dp', 'tensor'), may hold values from -0.1875 to 0.1875
- value_projection_weight: bfloat16 [1024, 1024], P('dp', 'tensor'), may hold values from -0.1875 to 0.1875
- w_out: bfloat16 [2048, 1024], P('tensor', 'dp'), may hold values from -3 to 3
- mlp_gain: bfloat16 [1024], P('dp'), may hold values from 0.5 to 1.5
- w_gate: bfloat16 [1024, 3072], P('dp', 'tensor'), may hold values from -0.1875 to 0.1875
- w_up: bfloat16 [1024, 3072], P('dp', 'tensor'), may hold values from -0.1875 to 0.1875
- w_down: bfloat16 [3072, 1024], P('tensor', 'dp'), may hold values from -0.109375 to 0.109375
- cotangent: bfloat16 [8, 1024, 1024], P('dp', 'tensor'), may hold values from -6 to 6
Outputs:
- block_output: bfloat16 [8, 1024, 1024], P('dp', 'tensor')
- input_grad: float32 [8, 1024, 1024], P('dp', 'tensor')
- grad_attn_gain: float32 [1024], P('dp')
- grad_q_gain: float32 [128], P('dp')
- grad_k_gain: float32 [128], P('dp')
- grad_query: float32 [1024, 2048], P('dp', 'tensor')
- grad_key: float32 [1024, 1024], P('dp', 'tensor')
- grad_value: float32 [1024, 1024], P('dp', 'tensor')
- grad_out: float32 [2048, 1024], P('tensor', 'dp')
- grad_mlp_gain: float32 [1024], P('dp')
- grad_gate: float32 [1024, 3072], P('dp', 'tensor')
- grad_up: float32 [1024, 3072], P('dp', 'tensor')
- grad_down: float32 [3072, 1024], P('tensor', 'dp')
The draws below stay inside these ranges and needn't reach their ends.
Inputs may be any that keep to these rules, and one draw needn't show every extreme that they name: piece_starts gives the first position of each of the 2 picture pieces of a sequence; a piece covers 256 positions, and pieces may intersect.
All inputs are finite; a program needn't handle non-finite values.
Results may differ from the reference program's by a relative error of at most 0.015.
Values may be sent and summed in bfloat16 or wider, within the bound.
A program may use at most 128 MiB of HBM per device.

```python
import jax
import jax.numpy as jnp
from jax import lax

MODEL_WIDTH = 1024
QUERY_HEADS = 16
KEY_VALUE_HEADS = 8
HEAD_SIZE = 128
FF = 3072
LEN = 1024
SCORE_BLOCK_ROWS = 512
PIECE = 256
NPIC = 2
SEQS = 8


def set_ends(values, key, least, largest):
    longest = values.shape.index(max(values.shape))
    spots = []
    for shift in (0, 1):
        where = [jax.random.randint(jax.random.fold_in(key, axis), (), 0, length) for axis, length in enumerate(values.shape)]
        where[longest] = (where[longest] + shift) % values.shape[longest]
        spots.append(tuple(where))
    return values.at[spots[0]].set(least).at[spots[1]].set(largest)


def levels(key, shape, shards, smallest, largest):
    loudness = 1.0
    for dim, blocks in shards:
        steps = jax.random.uniform(jax.random.fold_in(jax.random.fold_in(key, 6), dim), (blocks,), jnp.float32, smallest / len(shards), largest / len(shards))
        loudness = loudness * jnp.repeat(jnp.exp(steps), shape[dim] // blocks).reshape((-1,) + (1,) * (len(shape) - 1 - dim))
    return loudness


def noise(rng, extent, scale, reach, cuts=(), kind=jnp.bfloat16):
    gain = levels(rng, extent, cuts, -0.22, 0.18) if cuts else 1.0
    entries = jax.random.normal(rng, extent, jnp.float32) * scale * gain
    return jnp.minimum(jnp.maximum(entries, -reach), reach).astype(kind)


def setup_inputs(seed: int = 0) -> dict:
    keys = jax.random.split(jax.random.key(seed), 15)
    block_input = noise(keys[0], (SEQS, LEN, MODEL_WIDTH), 1.0, 6.0, ((0, 8), (1, 4)))
    piece_starts = set_ends(jax.random.randint(keys[1], (SEQS, NPIC), 0, LEN - PIECE + 1), jax.random.fold_in(keys[1], 1), 0, LEN - PIECE).astype(jnp.int32)
    attn_gain = jnp.clip(1.0 + 0.1 * jax.random.normal(keys[2], (MODEL_WIDTH,), jnp.float32), 0.5, 1.5).astype(jnp.bfloat16)
    q_gain = jnp.clip(1.0 + 0.1 * jax.random.normal(keys[3], (HEAD_SIZE,), jnp.float32), 0.5, 1.5).astype(jnp.bfloat16)
    k_gain = jnp.clip(1.0 + 0.1 * jax.random.normal(keys[4], (HEAD_SIZE,), jnp.float32), 0.5, 1.5).astype(jnp.bfloat16)
    w_query = noise(keys[5], (MODEL_WIDTH, QUERY_HEADS * HEAD_SIZE), MODEL_WIDTH ** -0.5, 0.1875, ((0, 8), (1, 4)))
    key_projection_weight = noise(keys[6], (MODEL_WIDTH, KEY_VALUE_HEADS * HEAD_SIZE), MODEL_WIDTH ** -0.5, 0.1875, ((0, 8), (1, 4)))
    value_projection_weight = noise(keys[7], (MODEL_WIDTH, KEY_VALUE_HEADS * HEAD_SIZE), MODEL_WIDTH ** -0.5, 0.1875, ((0, 8), (1, 4)))
    w_out = noise(keys[8], (QUERY_HEADS * HEAD_SIZE, MODEL_WIDTH), (max(1, QUERY_HEADS * HEAD_SIZE * 2 // LEN)) ** -0.5, 3.0, ((0, 4), (1, 8)))
    mlp_gain = jnp.clip(1.0 + 0.1 * jax.random.normal(keys[9], (MODEL_WIDTH,), jnp.float32), 0.5, 1.5).astype(jnp.bfloat16)
    w_gate = noise(keys[10], (MODEL_WIDTH, FF), MODEL_WIDTH ** -0.5, 0.1875, ((0, 8), (1, 4)))
    w_up = noise(keys[11], (MODEL_WIDTH, FF), MODEL_WIDTH ** -0.5, 0.1875, ((0, 8), (1, 4)))
    w_down = noise(keys[12], (FF, MODEL_WIDTH), FF ** -0.5, 0.109375, ((0, 4), (1, 8)))
    cotangent = noise(keys[13], (SEQS, LEN, MODEL_WIDTH), 1.0, 6.0, ((0, 8), (1, 4)))
    return {"block_input": block_input, "piece_starts": piece_starts, "attn_gain": attn_gain, "q_gain": q_gain, "k_gain": k_gain, "w_query": w_query, "key_projection_weight": key_projection_weight, "value_projection_weight": value_projection_weight, "w_out": w_out, "mlp_gain": mlp_gain, "w_gate": w_gate, "w_up": w_up, "w_down": w_down, "cotangent": cotangent}


@jax.custom_vjp
def lower_precision(v):
    return lax.optimization_barrier(v.astype(jnp.bfloat16)).astype(jnp.float32)

@jax.custom_vjp
def lower_backward(v):
    return v

def low_keep(v):
    return (lower_precision(v), None)

def low_pass(kept, grad):
    return (grad,)

def back_keep(v):
    return (v, None)

def back_low(kept, grad):
    return (lower_precision(grad),)
lower_precision.defvjp(low_keep, low_pass)
lower_backward.defvjp(back_keep, back_low)
eps = 1e-06
theta = 1000000.0
neg_big = -1e+30
highest_precision = lax.Precision.HIGHEST

def rotary_tables(sequence_length, width):
    half_width = width // 2
    frequency = theta ** (-(jnp.arange(half_width, dtype=jnp.float32) * 2.0) / width)
    angles = jnp.arange(sequence_length, dtype=jnp.float32)[:, None] * frequency[None, :]
    return (jnp.cos(angles)[:, None, :], jnp.sin(angles)[:, None, :])

def rotate(vectors, cosine, sine_table):
    half_width = vectors.shape[-1] // 2
    first_half = vectors[..., :half_width]
    second_half = vectors[..., half_width:]
    return jnp.concatenate([first_half * cosine - second_half * sine_table, second_half * cosine + first_half * sine_table], axis=-1)

def piece_table(positions, starts):
    inside = (positions[:, None] >= starts[None, :]) & (positions[:, None] < starts[None, :] + PIECE)
    return inside.astype(jnp.float32)

def allowed_keys(block_index, sequence_length, starts):
    key_pos = jnp.arange(sequence_length, dtype=jnp.int32)
    query_pos = block_index * SCORE_BLOCK_ROWS + jnp.arange(SCORE_BLOCK_ROWS, dtype=jnp.int32)
    shared = jnp.dot(piece_table(query_pos, starts), piece_table(key_pos, starts).T) > 0.5
    return (key_pos[None, :] <= query_pos[:, None]) | shared

def rms_scale(vectors):
    return lax.rsqrt(lax.optimization_barrier(jnp.mean(vectors * vectors, axis=-1, keepdims=True)) + eps)

def decoder_layer(inputs, starts, weights):
    attn_gain, q_gain, k_gain, w_query, key_projection_weight, value_projection_weight, w_out, mlp_gain, w_gate, w_up, w_down = weights
    sequence_length = inputs.shape[0]
    first_normed = lower_precision(inputs * rms_scale(inputs) * attn_gain)
    query_pre = lower_backward(jnp.dot(first_normed, w_query, precision=highest_precision)).reshape(sequence_length, QUERY_HEADS, HEAD_SIZE)
    key_before_norm = lower_backward(jnp.dot(first_normed, key_projection_weight, precision=highest_precision)).reshape(sequence_length, KEY_VALUE_HEADS, HEAD_SIZE)
    value_row_set = lower_backward(lower_precision(jnp.dot(first_normed, value_projection_weight, precision=highest_precision))).reshape(sequence_length, KEY_VALUE_HEADS, HEAD_SIZE)
    cosine, sine_table = rotary_tables(sequence_length, HEAD_SIZE)
    query_matrix = lower_precision(rotate(query_pre * rms_scale(query_pre) * q_gain, cosine, sine_table))
    key_rows = lower_precision(rotate(key_before_norm * rms_scale(key_before_norm) * k_gain, cosine, sine_table))
    block_list = query_matrix.reshape(sequence_length // SCORE_BLOCK_ROWS, SCORE_BLOCK_ROWS, KEY_VALUE_HEADS, QUERY_HEADS // KEY_VALUE_HEADS, HEAD_SIZE)
    score_scale = HEAD_SIZE ** (-0.5)

    def attend(element):
        query_block, block_index = element
        scores = jnp.einsum('ikrd,jkd->krij', query_block, key_rows, precision=highest_precision) * score_scale
        scores = jnp.where(allowed_keys(block_index, sequence_length, starts)[None, None], scores, neg_big)
        scores = lower_backward(scores)
        row_top = lax.optimization_barrier(jnp.max(scores, axis=-1, keepdims=True))
        exponent = jnp.exp(scores - row_top)
        probability = exponent / lax.optimization_barrier(jnp.sum(exponent, axis=-1, keepdims=True))
        return jnp.einsum('krij,jkd->ikrd', lower_precision(probability), value_row_set, precision=highest_precision)
    mixed_rows = lax.map(jax.checkpoint(attend), (block_list, jnp.arange(sequence_length // SCORE_BLOCK_ROWS, dtype=jnp.int32)))
    mixed_rows = lower_backward(lower_precision(mixed_rows.reshape(sequence_length, QUERY_HEADS * HEAD_SIZE)))
    hidden_one = inputs + lower_backward(jnp.dot(mixed_rows, w_out, precision=highest_precision))
    normed_two = lower_precision(hidden_one * rms_scale(hidden_one) * mlp_gain)
    gate_pre = lower_backward(jnp.dot(normed_two, w_gate, precision=highest_precision))
    upward = lower_backward(jnp.dot(normed_two, w_up, precision=highest_precision))
    hidden = lower_precision(gate_pre * jax.nn.sigmoid(gate_pre) * upward)
    return hidden_one + lower_backward(jnp.dot(hidden, w_down, precision=highest_precision))

def reference(block_input, piece_starts, attn_gain, q_gain, k_gain, w_query, key_projection_weight, value_projection_weight, w_out, mlp_gain, w_gate, w_up, w_down, cotangent):
    weights = tuple((weight.astype(jnp.float32) for weight in (attn_gain, q_gain, k_gain, w_query, key_projection_weight, value_projection_weight, w_out, mlp_gain, w_gate, w_up, w_down)))

    def per_sequence(running, element):
        sequence, starts, sequence_grad = element

        def forward(inputs, weight_set):
            return decoder_layer(inputs, starts, weight_set)
        result, pullback = jax.vjp(forward, sequence.astype(jnp.float32), weights)
        input_part, weight_parts = pullback(sequence_grad.astype(jnp.float32))
        running = tuple((summed + part for summed, part in zip(running, weight_parts)))
        return (running, (result.astype(jnp.bfloat16), input_part))
    zeros_start = tuple((jnp.zeros_like(weight) for weight in weights))
    running, (outputs, input_grads) = lax.scan(per_sequence, zeros_start, (block_input, piece_starts, cotangent))
    return (outputs, input_grads, running[0], running[1], running[2], running[3], running[4], running[5], running[6], running[7], running[8], running[9], running[10])
```

```python
import functools
import math

import jax
import jax.numpy as jnp
import numpy as np
from jax import lax
from jax.experimental import pallas as pl
from jax.experimental.pallas import tpu as pltpu
from jax.sharding import PartitionSpec as P

HEAD = 128
PIECE = 256
EPS = 1e-06
THETA = 1000000.0
SCALE = HEAD**-0.5
LOG2E = math.log2(math.e)
MESH = pl.DeviceIdType.MESH
F32 = jnp.float32
BF16 = jnp.bfloat16
VMEM_LIMIT = 60 * 2**20


def nt(x, y):
    return lax.dot_general(x, y, (((1,), (1,)), ((), ())), preferred_element_type=F32)


def nn(x, y):
    return lax.dot_general(x, y, (((1,), (0,)), ((), ())), preferred_element_type=F32)


def tn(x, y):
    return lax.dot_general(x, y, (((0,), (0,)), ((), ())), preferred_element_type=F32)


def start(copy):
    copy.start()


def wait(copy):
    copy.wait()


def wait_send(copy):
    copy.wait_send()


class Place:
    def __init__(self, dp, tensor):
        self.dp, self.tensor, self.columns = dp, tensor, dp // 2
        self.d = lax.axis_index("dp")
        self.t = lax.axis_index("tensor")
        self.col, self.c = lax.div(self.d, 2), lax.rem(self.d, 2)
        self.a, self.b = lax.div(self.t, 2), lax.rem(self.t, 2)
        self.sibling = self.d + 1 - 2 * self.c
        self.near = self.t + 1 - 2 * self.b
        self.far = self.t + 2 - 4 * self.a

    def barrier(self):
        semaphore = pltpu.get_barrier_semaphore()
        for k in range(1, self.dp):
            pl.semaphore_signal(
                semaphore, 1, device_id=(lax.rem(self.d + k, self.dp), self.t), device_id_type=MESH
            )
        for k in range(1, self.tensor):
            pl.semaphore_signal(
                semaphore,
                1,
                device_id=(self.d, lax.rem(self.t + k, self.tensor)),
                device_id_type=MESH,
            )
        pl.semaphore_wait(semaphore, self.dp + self.tensor - 2)

    def plane(self, bits_a, bits_b):
        first = self.a + bits_a - 2 * self.a * bits_a
        second = self.b + bits_b - 2 * self.b * bits_b
        return 2 * first + second


def remote(source, target, send, receive, device):
    return pltpu.make_async_remote_copy(
        src_ref=source,
        dst_ref=target,
        send_sem=send,
        recv_sem=receive,
        device_id=device,
        device_id_type=MESH,
    )


class Spread:
    def __init__(self, place, shard, stage, whole, send, receive, cross):
        self.p, self.shard, self.stage, self.whole = place, shard, stage, whole
        self.send, self.receive, self.cross = send, receive, cross
        self.rows = shard.shape[0]

    def slot(self, index):
        return self.whole.at[pl.ds(pl.multiple_of(index * self.rows, self.rows), self.rows)]

    def crossing(self):
        p = self.p
        return remote(self.shard, self.stage, self.cross.at[0], self.cross.at[1], (p.d, p.far))

    def each(self, phase, act_remote, act_local):
        p = self.p
        source = self.shard if phase == 0 else self.stage
        core = p.a if phase == 0 else 1 - p.a
        for j in range(p.columns):
            device = (2 * lax.rem(p.col + j, p.columns) + core, p.t)
            send = self.send.at[phase, j]

            def to_other():
                act_remote(remote(source, self.slot(p.d), send, self.receive.at[p.d], device))

            def to_self():
                act_local(pltpu.make_async_copy(source, self.slot(p.d), send))

            if j == 0 and act_local:
                pl.when(core == p.c)(to_self)
            if act_remote:
                if j:
                    to_other()
                else:
                    pl.when(core != p.c)(to_other)

    def start(self, phase):
        self.each(phase, start, start)

    def cross_start(self):
        self.crossing().start()

    def cross_wait(self):
        self.crossing().wait_recv()

    def wait_whole(self):
        p = self.p
        self.each(0, None, wait)
        self.each(1, None, wait)
        for k in range(1, p.dp):
            source = lax.rem(p.d + k, p.dp)
            remote(
                self.shard, self.slot(source), self.send.at[0, 0], self.receive.at[source], (p.d, p.t)
            ).wait_recv()

    def wait_sends(self):
        self.crossing().wait_send()
        self.each(0, wait_send, None)
        self.each(1, wait_send, None)


def spread_scratch(dp, rows, columns):
    return [
        pltpu.VMEM((rows, columns), BF16),
        pltpu.SemaphoreType.DMA((2, dp // 2)),
        pltpu.SemaphoreType.DMA((dp,)),
        pltpu.SemaphoreType.DMA((2,)),
    ]


class Fan:
    def __init__(self, place, block, whole, send, receive, onward):
        self.p, self.block, self.whole = place, block, whole
        self.send, self.receive, self.onward = send, receive, onward

    def sends(self, act):
        p = self.p
        for i in range(2):
            plane = 2 * p.c + i

            @pl.when(plane != p.t)
            def _():
                act(
                    remote(
                        self.block,
                        self.whole.at[p.t],
                        self.send.at[i],
                        self.receive.at[p.t],
                        (p.d, plane),
                    )
                )

    def start(self):
        p = self.p
        self.sends(start)

        @pl.when(p.a == p.c)
        def _():
            self.whole[p.t] = self.block[...]

    def pass_on(self, index, slot):
        p = self.p
        return remote(
            self.whole.at[slot],
            self.whole.at[slot],
            self.onward.at[index],
            self.receive.at[slot],
            (p.sibling, p.t),
        )

    def take(self, index, slot, own):
        p = self.p
        if own:
            pl.when(p.a != p.c)(lambda: self.pass_on(index, slot).wait_recv())
        else:
            self.pass_on(index, slot).wait_recv()
        pl.when(p.a == p.c)(lambda: self.pass_on(index, slot).start())

    def finish(self, slots):
        p = self.p
        self.sends(wait_send)

        @pl.when(p.a == p.c)
        def _():
            for index, slot in enumerate(slots):
                self.pass_on(index, slot).wait_send()


FAN_SEMAPHORES = [
    pltpu.SemaphoreType.DMA((2,)),
    pltpu.SemaphoreType.DMA((4,)),
    pltpu.SemaphoreType.DMA((4,)),
]


def gains_rows(total):
    one = jnp.concatenate([total[i : i + 1] for i in range(8)], axis=1)
    two = jnp.concatenate([total[i : i + 1] for i in range(8, 16)], axis=1)
    return one, two, total[16:17], total[17:18]


def unit_of(values):
    scale = lax.rsqrt(jnp.mean(values * values, axis=-1, keepdims=True) + EPS)
    return values * scale, scale


def first_kernel(
    dp,
    tensor,
    x_ref,
    wq_ref,
    wk_ref,
    wv_ref,
    pack_ref,
    cos_ref,
    sin_ref,
    normed_ref,
    q_ref,
    k_ref,
    v_ref,
    q_pre_ref,
    k_pre_ref,
    weights_ref,
    gains_ref,
    gain_slots,
    block,
    shard,
    gain_send,
    gain_receive,
    fan_send,
    fan_receive,
    fan_onward,
    stage,
    spread_send,
    spread_receive,
    spread_cross,
):
    p = Place(dp, tensor)
    p.barrier()

    def gain_copy(k, slot):
        return remote(
            pack_ref,
            gain_slots.at[slot],
            gain_send.at[k],
            gain_receive.at[slot],
            (lax.rem(p.d + k, dp), p.t),
        )

    for k in range(1, dp):
        gain_copy(k, p.d).start()
    gain_slots[p.d] = pack_ref[...]
    nq, nk = wq_ref.shape[1], wk_ref.shape[1]
    shard[:, :nq] = wq_ref[...]
    shard[:, nq : nq + nk] = wk_ref[...]
    shard[:, nq + nk :] = wv_ref[...]
    spread = Spread(p, shard, stage, weights_ref, spread_send, spread_receive, spread_cross)
    spread.cross_start()
    spread.start(0)
    unit, _ = unit_of(x_ref[...].astype(F32))
    for k in range(1, dp):
        gain_copy(k, lax.rem(p.d + k, dp)).wait_recv()
    total = lax.fori_loop(
        1, dp, lambda i, s: s + gain_slots[i].astype(F32), gain_slots[0].astype(F32)
    )
    gains_ref[...] = total
    gain_one, _, q_gain, k_gain = gains_rows(total)
    block[...] = (unit * gain_one).astype(BF16)
    fan = Fan(p, block, normed_ref, fan_send, fan_receive, fan_onward)
    fan.start()
    slots = [p.plane(k // 2, k % 2) for k in range(4)]
    fan.take(0, slots[0], True)
    spread.cross_wait()
    spread.start(1)
    fan.take(1, slots[1], False)
    spread.wait_whole()
    rows = x_ref.shape[0]

    def project(k, _):
        slot = p.plane(lax.div(k, 2), lax.rem(k, 2))
        pl.when(k >= 2)(lambda: fan.take(k, slot, False))
        tokens = normed_ref[slot]
        at = pl.ds(pl.multiple_of(slot * rows, rows), rows)
        cosine, sine = cos_ref[slot], sin_ref[slot]

        def rotated(values, gain):
            unit_values, _ = unit_of(values)
            scaled = unit_values * gain
            return (scaled * cosine + pltpu.roll(scaled, 64, 1) * sine).astype(BF16)

        for tile in range((nq + 2 * nk) // 256):
            product = nn(tokens, weights_ref[:, tile * 256 : (tile + 1) * 256])
            for half in range(2):
                column = tile * 256 + half * HEAD
                values = product[:, half * HEAD : (half + 1) * HEAD]
                if column < nq:
                    head = column // HEAD
                    q_pre_ref[head, at] = values
                    q_ref[head, at] = rotated(values, q_gain)
                elif column < nq + nk:
                    head = (column - nq) // HEAD
                    k_pre_ref[head, at] = values
                    k_ref[head, at] = rotated(values, k_gain)
                else:
                    v_ref[(column - nq - nk) // HEAD, at] = values.astype(BF16)
        return 0

    lax.fori_loop(0, 4, project, 0)
    for k in range(1, dp):
        gain_copy(k, p.d).wait_send()
    fan.finish(slots)
    spread.wait_sends()


class Home:
    def __init__(self, place, kept, given, taken, summed, landed, semaphores):
        self.p = place
        self.kept, self.given, self.taken, self.summed, self.landed = kept, given, taken, summed, landed
        self.given_send, self.taken_receive, self.summed_send, self.landed_receive = semaphores

    def block(self, k):
        k = 3 - k
        return self.p.plane(k // 2, k % 2)

    def mine(self, k):
        return self.p.c == (self.p.b if k % 2 else 1 - self.p.b)

    def give(self, slot):
        return remote(
            self.given.at[slot],
            self.taken.at[slot],
            self.given_send.at[slot],
            self.taken_receive.at[slot],
            (self.p.sibling, self.p.t),
        )

    def send(self, k):
        p = self.p
        return remote(
            self.summed.at[k // 2],
            self.landed.at[p.b],
            self.summed_send.at[k // 2],
            self.landed_receive.at[p.b],
            (2 * p.col + p.a, self.block(k)),
        )

    def add(self, k, parts):
        @pl.when(self.mine(k))
        def _():
            for i, part in enumerate(parts):
                self.kept[:, i * 256 : (i + 1) * 256] = part()

        @pl.when(jnp.logical_not(self.mine(k)))
        def _():
            for i, part in enumerate(parts):
                self.given[k // 2, :, i * 256 : (i + 1) * 256] = part().astype(BF16)
            self.give(k // 2).start()

    def stays(self, k):
        return jnp.logical_and(self.p.a == self.p.c, k == 3)

    def settle(self, k):
        p = self.p

        @pl.when(self.mine(k))
        def _():
            self.give(k // 2).wait_recv()
            total = (self.kept[...] + self.taken[k // 2].astype(F32)).astype(BF16)
            if k == 3:

                @pl.when(p.a == p.c)
                def _():
                    self.landed[p.b] = total

                @pl.when(p.a != p.c)
                def _():
                    self.summed[k // 2] = total
                    self.send(k).start()
            else:
                self.summed[k // 2] = total
                self.send(k).start()

    def result(self):
        p = self.p

        def arrived(slot):
            remote(
                self.summed.at[0],
                self.landed.at[slot],
                self.summed_send.at[0],
                self.landed_receive.at[slot],
                (p.d, p.t),
            ).wait_recv()

        arrived(1 - p.b)
        here = jnp.logical_and(p.c == p.b, p.a == p.c)
        pl.when(jnp.logical_not(here))(lambda: arrived(p.b))
        return self.landed[0].astype(F32) + self.landed[1].astype(F32)

    def finish(self):
        for k in range(4):

            @pl.when(jnp.logical_not(self.mine(k)))
            def _():
                self.give(k // 2).wait_send()

            sent = self.mine(k)
            if k == 3:
                sent = jnp.logical_and(sent, self.p.a != self.p.c)

            @pl.when(sent)
            def _():
                self.send(k).wait_send()


def home_scratch(rows, width):
    return [
        pltpu.VMEM((rows, width), F32),
        pltpu.VMEM((2, rows, width), BF16),
        pltpu.VMEM((2, rows, width), BF16),
        pltpu.VMEM((2, rows, width), BF16),
        pltpu.VMEM((2, rows, width), BF16),
        *[pltpu.SemaphoreType.DMA((2,))] * 4,
    ]


class Quad:
    def __init__(self, place, block, whole, send, receive):
        self.p, self.whole_block, self.whole, self.sent, self.receive = place, block, whole, send, receive
        b, c = place.b, place.c
        self.slots = [2 * b + c, 2 * b + 1 - c, 2 * (1 - b) + c, 2 * (1 - b) + 1 - c]

    def copy(self, index, source, slot, device):
        return remote(
            source, self.whole.at[slot], self.sent.at[index], self.receive.at[slot], device
        )

    def near(self):
        p = self.p
        return self.copy(0, self.whole_block, self.slots[0], (p.d, p.near))

    def beside(self):
        p = self.p
        return self.copy(1, self.whole_block, self.slots[0], (p.sibling, p.t))

    def onward(self):
        p = self.p
        return self.copy(2, self.whole.at[self.slots[2]], self.slots[2], (p.sibling, p.t))

    def start(self):
        self.near().start()
        self.beside().start()
        self.whole[self.slots[0]] = self.whole_block[...]

    def take(self, index):
        slot = self.slots[index]
        self.copy(0, self.whole_block, slot, (self.p.d, self.p.near)).wait_recv()
        if index == 2:
            self.onward().start()

    def finish(self):
        self.near().wait_send()
        self.beside().wait_send()
        self.onward().wait_send()


QUAD_SEMAPHORES = [pltpu.SemaphoreType.DMA((3,)), pltpu.SemaphoreType.DMA((4,))]


class PairSum:
    def __init__(self, place, kept, given, taken, summed, landed, given_send, taken_receive, across):
        self.p = place
        self.kept, self.given, self.taken, self.summed, self.landed = kept, given, taken, summed, landed
        self.given_send, self.taken_receive, self.across = given_send, taken_receive, across

    def give(self, half):
        return remote(
            self.given.at[half],
            self.taken.at[half],
            self.given_send.at[half],
            self.taken_receive.at[half],
            (self.p.sibling, self.p.t),
        )

    def send(self):
        p = self.p
        return remote(self.summed, self.landed, self.across.at[0], self.across.at[1], (p.d, p.near))

    def relay(self):
        self.give(1).wait_recv()
        self.summed[...] = (self.kept[1] + self.taken[1].astype(F32)).astype(BF16)
        self.send().start()

    def result(self):
        self.give(0).wait_recv()
        self.send().wait_recv()
        return self.kept[0] + self.taken[0].astype(F32) + self.landed[...].astype(F32)

    def finish(self):
        self.give(0).wait_send()
        self.give(1).wait_send()
        self.send().wait_send()


def pair_scratch(rows, width):
    return [
        pltpu.VMEM((2, rows, width), F32),
        pltpu.VMEM((2, rows, width), BF16),
        pltpu.VMEM((2, rows, width), BF16),
        pltpu.VMEM((rows, width), BF16),
        pltpu.VMEM((rows, width), BF16),
        *[pltpu.SemaphoreType.DMA((2,))] * 3,
    ]


def vmem(count):
    return [pl.BlockSpec(memory_space=pltpu.VMEM)] * count


def params(identity):
    return pltpu.CompilerParams(
        collective_id=identity, has_side_effects=True, vmem_limit_bytes=VMEM_LIMIT
    )


def first(dp, tensor, x, wq, wk, wv, pack, cosine, sine):
    rows, width = x.shape
    tokens = rows * tensor
    shard_rows, nq = wq.shape
    nk = wk.shape[1]
    shapes = [
        ((4, rows, width), BF16),
        ((nq // HEAD, tokens, HEAD), BF16),
        ((nk // HEAD, tokens, HEAD), BF16),
        ((nk // HEAD, tokens, HEAD), BF16),
        ((nq // HEAD, tokens, HEAD), F32),
        ((nk // HEAD, tokens, HEAD), F32),
        ((width, nq + 2 * nk), BF16),
        ((32, 128), F32),
    ]
    return pl.pallas_call(
        functools.partial(first_kernel, dp, tensor),
        out_shape=[jax.ShapeDtypeStruct(*s) for s in shapes],
        in_specs=vmem(7),
        out_specs=vmem(len(shapes)),
        scratch_shapes=[
            pltpu.VMEM((dp, 32, 128), BF16),
            pltpu.VMEM((rows, width), BF16),
            pltpu.VMEM((shard_rows, nq + 2 * nk), BF16),
            pltpu.SemaphoreType.DMA((dp,)),
            pltpu.SemaphoreType.DMA((dp,)),
            *FAN_SEMAPHORES,
            *spread_scratch(dp, shard_rows, nq + 2 * nk),
        ],
        compiler_params=params(1),
    )(x, wq, wk, wv, pack, cosine, sine)


def rotary(tokens):
    frequency = np.float32(THETA) ** (
        -(np.arange(HEAD // 2, dtype=np.float32) * np.float32(2.0)) / np.float32(HEAD)
    )
    angles = np.arange(tokens, dtype=np.float32)[:, None] * frequency.astype(np.float32)[None, :]
    cosine, sine = np.cos(angles), np.sin(angles)
    return (
        np.concatenate([cosine, cosine], axis=1).astype(np.float32),
        np.concatenate([-sine, sine], axis=1).astype(np.float32),
    )


def small_pack(dp, attn_gain, mlp_gain, q_gain, k_gain, starts):
    d = lax.axis_index("dp")

    def placed(values, copies):
        size = values.shape[0]
        return jnp.where(lax.div(jnp.arange(size * copies), size) == d, jnp.tile(values, copies), 0)

    lane = jnp.arange(128) == d
    eighths = lax.div(starts[0], 8)
    rest = starts[0] - 8 * eighths
    rows = [placed(v, dp) for v in (attn_gain, mlp_gain, q_gain, k_gain)]
    for piece in range(2):
        for number in (eighths[piece], rest[piece]):
            rows.append(jnp.where(lane, number.astype(BF16), 0))
    flat = jnp.concatenate([r.astype(BF16) for r in rows])
    return jnp.pad(flat, (0, 32 * 128 - flat.shape[0])).reshape(32, 128)


def allowed_mask(place, gains, base, rows, keys, transposed):
    lane = lax.broadcasted_iota(jnp.int32, (1, 128), 1)
    chosen = (lane == 2 * place.col + place.a).astype(F32)
    shape = (keys, rows) if transposed else (rows, keys)
    query_dim, key_dim = (1, 0) if transposed else (0, 1)
    line = lambda dim: tuple(n if i == dim else 1 for i, n in enumerate(shape))
    query = lax.broadcasted_iota(jnp.int32, shape, query_dim)
    key = lax.broadcasted_iota(jnp.int32, shape, key_dim)
    mask = (key <= query).astype(F32)
    for piece in range(2):
        row = 18 + 2 * piece
        numbers = 8.0 * gains[row : row + 1] + gains[row + 1 : row + 2]
        first_position = jnp.sum(numbers * chosen, axis=1, keepdims=True) - base.astype(F32)

        def inside(position):
            position = position.astype(F32)
            return jnp.logical_and(
                position >= first_position, position < first_position + PIECE
            ).astype(F32)

        in_query = inside(lax.broadcasted_iota(jnp.int32, line(query_dim), query_dim))
        in_key = inside(lax.broadcasted_iota(jnp.int32, line(key_dim), key_dim))
        mask = jnp.maximum(mask, in_query * in_key)
    return mask


def second_kernel(
    dp,
    tensor,
    q_ref,
    k_ref,
    v_ref,
    gains_ref,
    x_ref,
    wo_ref,
    wm_ref,
    ct_ref,
    mixed_ref,
    lse_ref,
    hidden_ref,
    wo_whole_ref,
    wm_whole_ref,
    ct_whole_ref,
    v_wide,
    mask,
    *scratch,
):
    p = Place(dp, tensor)
    home = Home(p, *scratch[:5], scratch[5:9])
    spread_o = Spread(p, wo_ref, scratch[9], wo_whole_ref, *scratch[10:13])
    spread_m = Spread(p, wm_ref, scratch[13], wm_whole_ref, *scratch[14:17])
    quad = Quad(p, ct_ref, ct_whole_ref, *scratch[17:19])
    p.barrier()
    spread_o.cross_start()
    spread_o.start(0)
    spread_m.cross_start()
    spread_m.start(0)
    quad.start()
    heads, blocks = q_ref.shape[0], 4
    rows = x_ref.shape[0]
    kv_heads = k_ref.shape[0]
    repeat = heads // kv_heads
    v_wide[:, :, :HEAD] = v_ref[...]
    v_wide[:, :, HEAD:] = jnp.ones_like(v_ref)

    def attend(k):
        block = home.block(k)
        mask[...] = allowed_mask(p, gains_ref[...], block * rows, rows, 2 * rows, False)
        for number in range(blocks):

            @pl.when(block == number)
            def _():
                at = slice(number * rows, (number + 1) * rows)

                def group(g, _):
                    queries = q_ref[pl.ds(g * repeat, repeat), at].reshape(repeat * rows, HEAD)
                    total = jnp.zeros((repeat * rows, 2 * HEAD), F32)
                    for kb in range(min(number + 2, blocks)):
                        keys = slice(kb * rows, (kb + 1) * rows)
                        weight = jnp.exp2(nt(queries, k_ref[g, keys]) * (SCALE * LOG2E))
                        if kb >= number:
                            part = mask[:, (kb - number) * rows : (kb - number + 1) * rows]
                            weight = weight * jnp.concatenate([part] * repeat, axis=0)
                        total = total + nn(weight.astype(BF16), v_wide[g, keys])
                    summed = total[:, HEAD:]
                    result = (total[:, :HEAD] / summed).astype(BF16)
                    result = jnp.concatenate(
                        [result[i * rows : (i + 1) * rows] for i in range(repeat)], axis=1
                    )
                    width = repeat * HEAD
                    mixed_ref[at, pl.ds(pl.multiple_of(g * width, width), width)] = result
                    logs = jnp.log2(summed)
                    for i in range(repeat):
                        turned = logs[i * rows : (i + 1) * rows].T
                        lse_ref[g * repeat + i, :, at] = turned[0:1]
                    return 0

                lax.fori_loop(0, kv_heads, group, 0)

    def project(k):
        at = pl.ds(pl.multiple_of(home.block(k) * rows, rows), rows)

        def part(i):
            return lambda: nt(mixed_ref[at], wo_whole_ref[i * 256 : (i + 1) * 256])

        home.add(k, [part(i) for i in range(x_ref.shape[1] // 256)])

    attend(0)
    spread_o.cross_wait()
    spread_o.start(1)
    attend(1)
    spread_o.wait_whole()
    project(0)
    project(1)
    home.settle(0)
    attend(2)
    home.settle(1)
    project(2)
    attend(3)
    home.settle(2)
    project(3)
    quad.take(1)
    quad.take(2)
    home.settle(3)
    spread_m.cross_wait()
    spread_m.start(1)
    hidden_ref[...] = x_ref[...].astype(F32) + home.result()
    quad.take(3)
    spread_m.wait_whole()
    home.finish()
    quad.finish()
    spread_o.wait_sends()
    spread_m.wait_sends()


def second(dp, tensor, q, k, v, gains, x, wo, wm, ct):
    rows, width = x.shape
    tokens = rows * tensor
    heads = q.shape[0]
    shapes = [
        ((tokens, heads * HEAD), BF16),
        ((heads, 1, tokens), F32),
        ((rows, width), F32),
        ((width, wo.shape[1]), BF16),
        ((width, wm.shape[1]), BF16),
        ((4, rows, width), BF16),
    ]
    return pl.pallas_call(
        functools.partial(second_kernel, dp, tensor),
        out_shape=[jax.ShapeDtypeStruct(*s) for s in shapes],
        in_specs=vmem(8),
        out_specs=vmem(len(shapes)),
        scratch_shapes=[
            pltpu.VMEM((k.shape[0], tokens, 2 * HEAD), BF16),
            pltpu.VMEM((rows, 2 * rows), F32),
            *home_scratch(rows, width),
            *spread_scratch(dp, *wo.shape),
            *spread_scratch(dp, *wm.shape),
            *QUAD_SEMAPHORES,
        ],
        compiler_params=params(2),
    )(q, k, v, gains, x, wo, wm, ct)


def third_kernel(
    dp,
    tensor,
    hidden_ref,
    gains_ref,
    wm_ref,
    ct_ref,
    output_ref,
    grad_ref,
    branch_ref,
    gain_ref,
    grads_ref,
    block,
    normed,
    unit_ref,
    active,
    grad_gate,
    grad_up,
    *scratch,
):
    p = Place(dp, tensor)
    quad = Quad(p, block, normed, *scratch[:2])
    down = PairSum(p, *scratch[2:10])
    back = PairSum(p, *scratch[10:18])
    rows, width = hidden_ref.shape
    units = wm_ref.shape[1] // 3
    gain = gains_rows(gains_ref[...])[1]
    unit, scale = unit_of(hidden_ref[...])
    unit_ref[...] = unit
    block[...] = (unit * gain).astype(BF16)
    p.barrier()
    quad.start()

    def work(slot, keep, half):
        tokens, cotangent = normed[slot], ct_ref[slot]
        at = pl.ds(pl.multiple_of(slot * rows, rows), rows)
        for i in range(units // 256):
            here = slice(i * 256, (i + 1) * 256)
            gate = nn(tokens, wm_ref[:, i * 256 : (i + 1) * 256])
            upward = nn(tokens, wm_ref[:, units + i * 256 : units + (i + 1) * 256])
            grad = nn(cotangent, wm_ref[:, 2 * units + i * 256 : 2 * units + (i + 1) * 256])
            sigmoid = 1.0 / (1.0 + jnp.exp2(gate * -LOG2E))
            silu = gate * sigmoid
            active[at, here] = (silu * upward).astype(BF16)
            grad_gate[at, here] = (
                grad * upward * sigmoid * (1.0 + gate * (1.0 - sigmoid))
            ).astype(BF16)
            grad_up[at, here] = (grad * silu).astype(BF16)
        for i in range(width // 256):
            here = slice(i * 256, (i + 1) * 256)
            out = nt(grad_gate[at], wm_ref[here, :units]) + nt(
                grad_up[at], wm_ref[here, units : 2 * units]
            )
            if keep:
                back.kept[half, :, here] = out
            else:
                back.given[half, :, here] = out.astype(BF16)
        if not keep:
            back.give(half).start()
        for i in range(width // 256):
            here = slice(i * 256, (i + 1) * 256)
            out = nt(active[at], wm_ref[here, 2 * units :])
            if keep:
                down.kept[half, :, here] = out
            else:
                down.given[half, :, here] = out.astype(BF16)
        if not keep:
            down.give(half).start()

    def both(half, _):
        other = lax.select(half == 1, 1 - p.b, p.b)
        pl.when(half == 1)(lambda: quad.take(2))
        work(2 * other + p.c, True, half)
        pl.when(half == 0)(lambda: quad.take(1))
        pl.when(half == 1)(lambda: quad.take(3))
        work(2 * other + 1 - p.c, False, half)
        return 0

    lax.fori_loop(0, 2, both, 0)
    back.relay()
    down.relay()

    def weight_grads(i, _):
        at = pl.ds(pl.multiple_of(i * 256, 256), 256)
        tokens = normed[:, :, at].reshape(4 * rows, 256)
        grads_ref[at, :units] = tn(tokens, grad_gate[...]).astype(BF16)
        grads_ref[at, units : 2 * units] = tn(tokens, grad_up[...]).astype(BF16)
        cotangent = ct_ref[:, :, at].reshape(4 * rows, 256)
        grads_ref[at, 2 * units :] = tn(cotangent, active[...]).astype(BF16)
        return 0

    lax.fori_loop(0, width // 256, weight_grads, 0)
    grad_normed = back.result()
    unit = unit_ref[...]
    gain_ref[...] = jnp.sum(grad_normed * unit, axis=0, keepdims=True)
    scaled = grad_normed * gain
    mean = jnp.mean(scaled * unit, axis=-1, keepdims=True)
    grad = ct_ref[2 * p.b + p.c].astype(F32) + scale * (scaled - unit * mean)
    grad_ref[...] = grad
    branch_ref[...] = grad.astype(BF16)
    output_ref[...] = (hidden_ref[...] + down.result()).astype(BF16)
    quad.finish()
    back.finish()
    down.finish()


def third(dp, tensor, hidden, gains, wm, ct):
    rows, width = hidden.shape
    units = wm.shape[1] // 3
    shapes = [
        ((rows, width), BF16),
        ((rows, width), F32),
        ((rows, width), BF16),
        ((1, width), F32),
        ((width, wm.shape[1]), BF16),
    ]
    return pl.pallas_call(
        functools.partial(third_kernel, dp, tensor),
        out_shape=[jax.ShapeDtypeStruct(*s) for s in shapes],
        in_specs=vmem(4),
        out_specs=vmem(len(shapes)),
        scratch_shapes=[
            pltpu.VMEM((rows, width), BF16),
            pltpu.VMEM((4, rows, width), BF16),
            pltpu.VMEM((rows, width), F32),
            *[pltpu.VMEM((4 * rows, units), BF16)] * 3,
            *QUAD_SEMAPHORES,
            *pair_scratch(rows, width),
            *pair_scratch(rows, width),
        ],
        compiler_params=params(3),
    )(hidden, gains, wm, ct)


class Collect:
    def __init__(self, place, source, slots, summed, landed, send, receive, across):
        self.p, self.source, self.slots, self.summed, self.landed = place, source, slots, summed, landed
        self.send, self.receive, self.across = send, receive, across
        self.rows = slots.shape[1]
        self.step = 16

    def part(self, index):
        return self.source.at[pl.ds(pl.multiple_of(index * self.rows, self.rows), self.rows)]

    def own(self):
        p = self.p
        return pltpu.make_async_copy(self.part(p.d), self.slots.at[p.d], self.send.at[0])

    def other(self, k):
        p = self.p
        target = lax.rem(p.d + k, p.dp)
        return remote(
            self.part(target), self.slots.at[p.d], self.send.at[k], self.receive.at[p.d], (target, p.t)
        )

    def start(self):
        for k in range(1, self.p.dp):
            self.other(k).start()
        self.own().start()

    def cross(self):
        p = self.p
        return remote(self.summed, self.landed, self.across.at[0], self.across.at[1], (p.d, p.far))

    def total(self, core, at):
        return lax.fori_loop(
            1,
            self.p.columns,
            lambda i, s: s + self.slots[2 * i + core, at].astype(F32),
            self.slots[core, at].astype(F32),
        )

    def each_rows(self, act):
        def body(i, _):
            act(pl.ds(pl.multiple_of(i * self.step, self.step), self.step))
            return 0

        lax.fori_loop(0, self.rows // self.step, body, 0)

    def relay(self):
        p = self.p
        self.own().wait()
        for k in range(1, p.dp):
            source = lax.rem(p.d + k, p.dp)
            remote(
                self.part(source),
                self.slots.at[source],
                self.send.at[k],
                self.receive.at[source],
                (p.d, p.t),
            ).wait_recv()

        def act(at):
            self.summed[at] = self.total(1 - p.a, at).astype(BF16)

        self.each_rows(act)
        self.cross().start()

    def result(self, store):
        self.cross().wait_recv()

        def act(at):
            store(at, self.total(self.p.a, at) + self.landed[at].astype(F32))

        self.each_rows(act)

    def finish(self):
        for k in range(1, self.p.dp):
            self.other(k).wait_send()
        self.cross().wait_send()


def collect_scratch(dp, rows, columns):
    return [
        pltpu.VMEM((dp, rows, columns), BF16),
        pltpu.VMEM((rows, columns), BF16),
        pltpu.VMEM((rows, columns), BF16),
        pltpu.SemaphoreType.DMA((dp,)),
        pltpu.SemaphoreType.DMA((dp,)),
        pltpu.SemaphoreType.DMA((2,)),
    ]


def fourth_kernel(
    dp,
    tensor,
    branch_ref,
    wo_ref,
    mixed_ref,
    q_ref,
    k_ref,
    v_ref,
    lse_ref,
    gains_ref,
    grads_ref,
    dq_ref,
    dk_ref,
    dv_ref,
    wm_grad_ref,
    wo_grad_ref,
    branches,
    grad_mixed,
    delta,
    mask,
    grad_wo,
    *scratch,
):
    p = Place(dp, tensor)
    fan = Fan(p, branch_ref, branches, *scratch[:3])
    collect_m = Collect(p, grads_ref, *scratch[3:9])
    collect_o = Collect(p, grad_wo, *scratch[9:15])
    rows, width = branch_ref.shape
    heads, kv_heads = q_ref.shape[0], k_ref.shape[0]
    repeat, blocks = heads // kv_heads, 4
    p.barrier()
    fan.start()
    collect_m.start()
    slots = [p.plane(k // 2, k % 2) for k in range(4)]
    fan.take(0, slots[0], True)
    for number in range(blocks):
        base = jnp.int32(number * rows)
        mask[number] = allowed_mask(p, gains_ref[...], base, rows, 2 * rows, True)
    dk_ref[...] = jnp.zeros_like(dk_ref)
    dv_ref[...] = jnp.zeros_like(dv_ref)

    def spread_back(k, _):
        slot = p.plane(lax.div(k, 2), lax.rem(k, 2))
        pl.when(k >= 1)(lambda: fan.take(k, slot, False))
        at = pl.ds(pl.multiple_of(slot * rows, rows), rows)
        for i in range(heads * HEAD // 256):
            grad = nn(branches[slot], wo_ref[:, i * 256 : (i + 1) * 256]).astype(BF16)
            for j in range(256 // HEAD):
                head = i * (256 // HEAD) + j
                one = grad[:, j * HEAD : (j + 1) * HEAD]
                grad_mixed[head, at] = one
                both = one.astype(F32) * mixed_ref[at, head * HEAD : (head + 1) * HEAD].astype(F32)
                ones = jnp.ones((8, HEAD), F32)
                row = lax.dot_general(
                    ones,
                    both,
                    (((1,), (1,)), ((), ())),
                    precision=lax.Precision.HIGHEST,
                    preferred_element_type=F32,
                )
                delta[head, :, at] = row[0:1]
        return 0

    lax.fori_loop(0, 4, spread_back, 0)

    def out_grads(i, _):
        at = pl.ds(pl.multiple_of(i * 256, 256), 256)
        grad_wo[at] = tn(branches[:, :, at].reshape(4 * rows, 256), mixed_ref[...]).astype(BF16)
        return 0

    lax.fori_loop(0, width // 256, out_grads, 0)
    collect_o.start()

    def head_back(head, _):
        g = lax.div(head, repeat)
        for number in range(blocks):
            at = slice(number * rows, (number + 1) * rows)
            queries, grads = q_ref[head, at], grad_mixed[head, at]
            logs, sums = lse_ref[head, :, at], delta[head, :, at]
            grad_queries = jnp.zeros((rows, HEAD), F32)
            for kb in range(min(number + 2, blocks)):
                here = slice(kb * rows, (kb + 1) * rows)
                keys = k_ref[g, here]
                probs = jnp.exp2(nt(keys, queries) * (SCALE * LOG2E) - logs)
                if kb >= number:
                    probs = probs * mask[number, (kb - number) * rows : (kb - number + 1) * rows]
                scores = (probs * (nt(v_ref[g, here], grads) - sums)).astype(BF16)
                dv_ref[g, here] += nn(probs.astype(BF16), grads)
                dk_ref[g, here] += nn(scores, queries) * SCALE
                grad_queries = grad_queries + tn(scores, keys)
            dq_ref[head, at] = grad_queries * SCALE
        return 0

    lax.fori_loop(0, heads // 2, head_back, 0)
    collect_m.relay()
    collect_o.relay()
    lax.fori_loop(heads // 2, heads, head_back, 0)

    def store_m(at, value):
        wm_grad_ref[at] = value

    def store_o(at, value):
        wo_grad_ref[at] = value

    collect_m.result(store_m)
    collect_o.result(store_o)
    fan.finish(slots)
    collect_m.finish()
    collect_o.finish()


def fourth(dp, tensor, branch, wo, mixed, q, k, v, lse, gains, grads):
    rows, width = branch.shape
    heads, tokens, _ = q.shape
    shard = width // dp
    shapes = [
        (q.shape, F32),
        (k.shape, F32),
        (v.shape, F32),
        ((shard, grads.shape[1]), F32),
        ((shard, wo.shape[1]), F32),
    ]
    return pl.pallas_call(
        functools.partial(fourth_kernel, dp, tensor),
        out_shape=[jax.ShapeDtypeStruct(*s) for s in shapes],
        in_specs=vmem(9),
        out_specs=vmem(len(shapes)),
        scratch_shapes=[
            pltpu.VMEM((4, rows, width), BF16),
            pltpu.VMEM((heads, tokens, HEAD), BF16),
            pltpu.VMEM((heads, 1, tokens), F32),
            pltpu.VMEM((4, 2 * rows, rows), F32),
            pltpu.VMEM(wo.shape, BF16),
            *FAN_SEMAPHORES,
            *collect_scratch(dp, shard, grads.shape[1]),
            *collect_scratch(dp, shard, wo.shape[1]),
        ],
        compiler_params=params(4),
    )(branch, wo, mixed, q, k, v, lse, gains, grads)


def fifth_kernel(
    dp,
    tensor,
    dq_ref,
    dk_ref,
    dv_ref,
    q_pre_ref,
    k_pre_ref,
    normed_ref,
    wa_ref,
    gains_ref,
    cos_ref,
    sin_ref,
    x_ref,
    grad_ref,
    mlp_gain_ref,
    input_grad_ref,
    wa_grad_ref,
    gain_grad_ref,
    grads,
    grad_wa,
    gain_pack,
    plane_slots,
    plane_sum,
    tensor_slots,
    plane_send,
    plane_receive,
    tensor_send,
    tensor_receive,
    *scratch,
):
    p = Place(dp, tensor)
    home = Home(p, *scratch[:5], scratch[5:9])
    collect = Collect(p, grad_wa, *scratch[9:15])
    rows, width = x_ref.shape
    heads, kv_heads = dq_ref.shape[0], dk_ref.shape[0]
    gain_one, _, q_gain, k_gain = gains_rows(gains_ref[...])
    gain_pack[...] = jnp.zeros_like(gain_pack)
    p.barrier()

    def project(k):
        block = home.block(k)
        at = pl.ds(pl.multiple_of(block * rows, rows), rows)
        cosine, sine = cos_ref[block], sin_ref[block]

        def back(grad, before, gain):
            unit, scale = unit_of(before)
            turned = grad * cosine - pltpu.roll(grad, 64, 1) * sine
            total = jnp.sum(turned * unit, axis=0, keepdims=True)
            scaled = turned * gain
            mean = jnp.mean(scaled * unit, axis=-1, keepdims=True)
            return (scale * (scaled - unit * mean)).astype(BF16), total

        for kind, (source, before, gain, count, offset) in enumerate(
            [
                (dq_ref, q_pre_ref, q_gain, heads, 0),
                (dk_ref, k_pre_ref, k_gain, kv_heads, heads),
            ]
        ):
            for head in range(count):
                column = (offset + head) * HEAD
                result, total = back(source[head, at], before[head, at], gain)
                grads[at, column : column + HEAD] = result
                gain_pack[16 + kind : 17 + kind] += total
        for head in range(kv_heads):
            column = (heads + kv_heads + head) * HEAD
            grads[at, column : column + HEAD] = dv_ref[head, at].astype(BF16)

        def part(i):
            return lambda: nt(grads[at], wa_ref[i * 256 : (i + 1) * 256])

        home.add(k, [part(i) for i in range(width // 256)])

    project(0)
    project(1)
    home.settle(0)
    project(2)
    home.settle(1)
    project(3)
    home.settle(2)
    home.settle(3)

    def weight_grads(i, _):
        at = pl.ds(pl.multiple_of(i * 256, 256), 256)
        tokens = normed_ref[:, :, at].reshape(4 * rows, 256)
        grad_wa[at] = tn(tokens, grads[...]).astype(BF16)
        return 0

    lax.fori_loop(0, width // 256, weight_grads, 0)
    collect.start()
    grad_normed = home.result()
    unit, scale = unit_of(x_ref[...].astype(F32))
    total = jnp.sum(grad_normed * unit, axis=0, keepdims=True)
    scaled = grad_normed * gain_one
    mean = jnp.mean(scaled * unit, axis=-1, keepdims=True)
    input_grad_ref[...] = grad_ref[...] + scale * (scaled - unit * mean)
    for i in range(8):
        gain_pack[i : i + 1] = total[:, i * 128 : (i + 1) * 128]
        gain_pack[8 + i : 9 + i] = mlp_gain_ref[:, i * 128 : (i + 1) * 128]

    def in_plane(k, slot):
        return remote(
            gain_pack,
            plane_slots.at[slot],
            plane_send.at[k],
            plane_receive.at[slot],
            (lax.rem(p.d + k, dp), p.t),
        )

    def in_tensor(k, slot):
        return remote(
            plane_sum,
            tensor_slots.at[slot],
            tensor_send.at[k],
            tensor_receive.at[slot],
            (p.d, lax.rem(p.t + k, tensor)),
        )

    def added(slots, count):
        return lax.fori_loop(1, count, lambda i, s: s + slots[i], slots[0])

    for k in range(1, dp):
        in_plane(k, p.d).start()
    plane_slots[p.d] = gain_pack[...]
    collect.relay()
    for k in range(1, dp):
        in_plane(k, lax.rem(p.d + k, dp)).wait_recv()
    plane_sum[...] = added(plane_slots, dp)
    for k in range(1, tensor):
        in_tensor(k, p.t).start()
    tensor_slots[p.t] = plane_sum[...]
    for k in range(1, tensor):
        in_tensor(k, lax.rem(p.t + k, tensor)).wait_recv()
    gain_grad_ref[...] = added(tensor_slots, tensor)

    def store(at, value):
        wa_grad_ref[at] = value

    collect.result(store)
    home.finish()
    collect.finish()
    for k in range(1, dp):
        in_plane(k, p.d).wait_send()
    for k in range(1, tensor):
        in_tensor(k, p.t).wait_send()


def fifth(dp, tensor, dq, dk, dv, q_pre, k_pre, normed, wa, gains, cosine, sine, x, grad, mlp_gain):
    rows, width = x.shape
    shard = width // dp
    columns = wa.shape[1]
    shapes = [((rows, width), F32), ((shard, columns), F32), ((32, 128), F32)]
    return pl.pallas_call(
        functools.partial(fifth_kernel, dp, tensor),
        out_shape=[jax.ShapeDtypeStruct(*s) for s in shapes],
        in_specs=vmem(13),
        out_specs=vmem(len(shapes)),
        scratch_shapes=[
            pltpu.VMEM((4 * rows, columns), BF16),
            pltpu.VMEM((width, columns), BF16),
            pltpu.VMEM((32, 128), F32),
            pltpu.VMEM((dp, 32, 128), F32),
            pltpu.VMEM((32, 128), F32),
            pltpu.VMEM((tensor, 32, 128), F32),
            pltpu.SemaphoreType.DMA((dp,)),
            pltpu.SemaphoreType.DMA((dp,)),
            pltpu.SemaphoreType.DMA((tensor,)),
            pltpu.SemaphoreType.DMA((tensor,)),
            *home_scratch(rows, width),
            *collect_scratch(dp, shard, columns),
        ],
        compiler_params=params(5),
    )(dq, dk, dv, q_pre, k_pre, normed, wa, gains, cosine, sine, x, grad, mlp_gain)


def shards(dp, tensor, debug, x, starts, attn_gain, q_gain, k_gain, wq, wk, wv, wo, mlp_gain, wg, wu, wd, ct):
    rows = x.shape[1]
    cosine, sine = (jnp.asarray(v).reshape(tensor, rows, HEAD) for v in rotary(rows * tensor))
    pack = small_pack(dp, attn_gain, mlp_gain, q_gain, k_gain, starts)
    normed, q, k, v, q_pre, k_pre, wa, gains = first(
        dp, tensor, x[0], wq, wk, wv, pack, cosine, sine
    )
    wm = jnp.concatenate([wg, wu, wd.T], axis=1)
    mixed, lse, hidden, wo_whole, wm_whole, ct_whole = second(
        dp, tensor, q, k, v, gains, x[0], wo.T, wm, ct[0]
    )
    output, grad_hidden, branch, grad_mlp_gain, grads = third(
        dp, tensor, hidden, gains, wm_whole, ct_whole
    )
    dq, dk, dv, wm_grad, wo_grad = fourth(
        dp, tensor, branch, wo_whole, mixed, q, k, v, lse, gains, grads
    )
    input_grad, wa_grad, gain_grad = fifth(
        dp, tensor, dq, dk, dv, q_pre, k_pre, normed, wa, gains, cosine, sine, x[0], grad_hidden,
        grad_mlp_gain,
    )
    if debug:
        return output, grad_hidden, branch, grads, dq, dk, dv, wm_grad, wo_grad, input_grad, wa_grad, gain_grad, hidden, gains
    d = lax.axis_index("dp")
    flat = gain_grad.reshape(-1)

    def mine(offset, size):
        return lax.dynamic_slice(flat, (offset + d * size,), (size,))

    nq, nk, units = wq.shape[1], wk.shape[1], wg.shape[1]
    return (
        output[None],
        input_grad[None],
        mine(0, attn_gain.shape[0]),
        mine(2048, q_gain.shape[0]),
        mine(2048 + 128, k_gain.shape[0]),
        wa_grad[:, :nq],
        wa_grad[:, nq : nq + nk],
        wa_grad[:, nq + nk :],
        wo_grad.T,
        mine(1024, mlp_gain.shape[0]),
        wm_grad[:, :units],
        wm_grad[:, units : 2 * units],
        wm_grad[:, 2 * units :].T,
    )


def solution(mesh):
    sequence, square, turned = P("dp", "tensor", None), P("dp", "tensor"), P("tensor", "dp")
    gain = P("dp")
    in_specs = (
        sequence, P("dp", None), gain, gain, gain, square, square, square, turned, gain, square, square,
        turned, sequence,
    )
    out_specs = (
        sequence, sequence, gain, gain, gain, square, square, square, turned, gain, square, square,
        turned,
    )
    return jax.shard_map(
        functools.partial(shards, mesh.shape["dp"], mesh.shape["tensor"], False),
        mesh=mesh,
        in_specs=in_specs,
        out_specs=out_specs,
        check_vma=False,
    )
```

```python
import functools
import math
import types

import jax
import jax.numpy as jnp
import numpy as np
from jax import lax
from jax.experimental import pallas as pl
from jax.experimental.pallas import tpu as pltpu
from jax.sharding import PartitionSpec as P

HEAD = 128
PIECE = 256
EPS = 1e-06
THETA = 1000000.0
SCALE = HEAD**-0.5
LOG2E = math.log2(math.e)
MESH = pl.DeviceIdType.MESH
F32 = jnp.float32
BF16 = jnp.bfloat16
VMEM_LIMIT = 62 * 2**20


def nt(x, y):
    return lax.dot_general(x, y, (((1,), (1,)), ((), ())), preferred_element_type=F32)


def nn(x, y):
    return lax.dot_general(x, y, (((1,), (0,)), ((), ())), preferred_element_type=F32)


def tn(x, y):
    return lax.dot_general(x, y, (((0,), (0,)), ((), ())), preferred_element_type=F32)


def start(copy):
    copy.start()


def wait(copy):
    copy.wait()


def wait_send(copy):
    copy.wait_send()


def by_rows(rows, act, step=64):
    def body(i, _):
        act(pl.ds(pl.multiple_of(i * step, step), step))
        return 0

    lax.fori_loop(0, rows // step, body, 0)


class Place:
    def __init__(self, dp, tensor):
        self.dp, self.tensor, self.columns = dp, tensor, dp // 2
        self.d = lax.axis_index("dp")
        self.t = lax.axis_index("tensor")
        self.col, self.c = lax.div(self.d, 2), lax.rem(self.d, 2)
        self.a, self.b = lax.div(self.t, 2), lax.rem(self.t, 2)
        self.sibling = self.d + 1 - 2 * self.c
        self.near = self.t + 1 - 2 * self.b
        self.far = self.t + 2 - 4 * self.a

    def barrier(self):
        semaphore = pltpu.get_barrier_semaphore()
        for k in range(1, self.dp):
            pl.semaphore_signal(
                semaphore, 1, device_id=(lax.rem(self.d + k, self.dp), self.t), device_id_type=MESH
            )
        for k in range(1, self.tensor):
            pl.semaphore_signal(
                semaphore,
                1,
                device_id=(self.d, lax.rem(self.t + k, self.tensor)),
                device_id_type=MESH,
            )
        pl.semaphore_wait(semaphore, self.dp + self.tensor - 2)

    def plane(self, bits_a, bits_b):
        first = self.a + bits_a - 2 * self.a * bits_a
        second = self.b + bits_b - 2 * self.b * bits_b
        return 2 * first + second


def remote(source, target, send, receive, device):
    return pltpu.make_async_remote_copy(
        src_ref=source,
        dst_ref=target,
        send_sem=send,
        recv_sem=receive,
        device_id=device,
        device_id_type=MESH,
    )


class Spread:
    def __init__(self, place, shard, stage, whole, send, receive, cross):
        self.p, self.shard, self.stage, self.whole = place, shard, stage, whole
        self.send, self.receive, self.cross = send, receive, cross
        self.rows = shard.shape[0]
        self.square = place.columns == 4
        y, x = lax.div(place.col, 2), lax.rem(place.col, 2)
        if self.square:
            self.side = [2 * y + 1 - x, 2 * (1 - y) + x]
            self.corner = 2 * (1 - y) + 1 - x

    def slot(self, index, half=None):
        size = self.rows if half is None else self.rows // 2
        begin = index * self.rows + (0 if half is None else half * size)
        return self.whole.at[pl.ds(pl.multiple_of(begin, size), size)]

    def crossing(self):
        p = self.p
        return remote(self.shard, self.stage, self.cross.at[0], self.cross.at[1], (p.d, p.far))

    def each(self, phase, act_remote, act_local):
        p = self.p
        source = self.shard if phase == 0 else self.stage
        core = p.a if phase == 0 else 1 - p.a
        columns = (
            [p.col] + self.side
            if self.square
            else [lax.rem(p.col + j, p.columns) for j in range(p.columns)]
        )
        for j, column in enumerate(columns):
            send = self.send.at[phase, j]

            def to_other():
                act_remote(
                    remote(
                        source,
                        self.slot(p.d),
                        send,
                        self.receive.at[p.d, 0],
                        (2 * column + core, p.t),
                    )
                )

            def to_self():
                act_local(pltpu.make_async_copy(source, self.slot(p.d), send))

            if j == 0 and act_local:
                pl.when(core == p.c)(to_self)
            if act_remote:
                if j:
                    to_other()
                else:
                    pl.when(core != p.c)(to_other)

    def start(self, phase):
        self.each(phase, start, start)

    def cross_start(self):
        self.crossing().start()

    def cross_wait(self):
        self.crossing().wait_recv()

    def landed(self, index, half):
        p = self.p
        part = self.slot(index, half)
        remote(
            part, part, self.send.at[0, 0], self.receive.at[index, half or 0], (p.d, p.t)
        ).wait_recv()

    def forwards(self, act):
        p = self.p
        for direction in range(2):
            for core in range(2):
                index = 2 * self.side[direction] + core
                part = self.slot(index, direction)
                act(
                    remote(
                        part,
                        part,
                        self.send.at[2 + direction, core],
                        self.receive.at[index, direction],
                        (2 * self.side[1 - direction] + p.c, p.t),
                    )
                )

    def forward(self):
        if self.square:
            for direction in range(2):
                for core in range(2):
                    self.landed(2 * self.side[direction] + core, None)
            self.forwards(start)

    def wait_whole(self):
        p = self.p
        self.each(0, None, wait)
        self.each(1, None, wait)
        if self.square:
            self.landed(p.sibling, None)
            for core in range(2):
                for half in range(2):
                    self.landed(2 * self.corner + core, half)
        else:
            for k in range(1, p.dp):
                self.landed(lax.rem(p.d + k, p.dp), None)

    def wait_sends(self):
        self.crossing().wait_send()
        self.each(0, wait_send, None)
        self.each(1, wait_send, None)
        if self.square:
            self.forwards(wait_send)


def spread_semaphores(dp):
    return [
        pltpu.SemaphoreType.DMA((4, max(dp // 2, 4))),
        pltpu.SemaphoreType.DMA((dp, 2)),
        pltpu.SemaphoreType.DMA((2,)),
    ]


class Fan:
    PIECES = 4

    def __init__(self, place, block, whole, send, receive, onward):
        self.p, self.block, self.whole = place, block, whole
        self.send, self.receive, self.onward = send, receive, onward
        self.slots = [place.plane(k // 2, k % 2) for k in range(4)]
        self.rows = block.shape[0] // self.PIECES

    def first_hop(self, act):
        p = self.p
        plane = lax.select(p.a == p.c, p.near, p.c + 1)
        for piece in range(self.PIECES):
            at = pl.ds(piece * self.rows, self.rows)
            act(
                remote(
                    self.block.at[at],
                    self.whole.at[p.t, at],
                    self.send.at[piece],
                    self.receive.at[p.t, piece],
                    (p.d, plane),
                )
            )

    def start(self):
        p = self.p
        self.first_hop(start)

        @pl.when(p.a == p.c)
        def _():
            self.whole[p.t] = self.block[...]

    def hop(self, index, piece, device, row):
        part = self.whole.at[self.slots[index], pl.ds(piece * self.rows, self.rows)]
        return remote(
            part,
            part,
            self.onward.at[row, index, piece],
            self.receive.at[self.slots[index], piece],
            device,
        )

    def to_sibling(self, index, piece):
        return self.hop(index, piece, (self.p.sibling, self.p.t), 0)

    def to_near(self, index, piece):
        return self.hop(index, piece, (self.p.d, self.p.near), 1)

    def take(self, *indices):
        p = self.p
        for piece in range(self.PIECES):
            for index in indices:

                def arrived():
                    self.to_sibling(index, piece).wait_recv()

                if index == 0:
                    pl.when(p.a != p.c)(arrived)
                else:
                    arrived()

                @pl.when(p.a == p.c)
                def _():
                    if index >= 2:
                        pl.when(p.t == p.c + 1)(lambda: self.to_near(index, piece).start())
                    self.to_sibling(index, piece).start()

    def finish(self):
        p = self.p
        self.first_hop(wait_send)

        @pl.when(p.a == p.c)
        def _():
            for index in range(4):
                for piece in range(self.PIECES):
                    self.to_sibling(index, piece).wait_send()
                    if index >= 2:
                        pl.when(p.t == p.c + 1)(lambda: self.to_near(index, piece).wait_send())


FAN_SEMAPHORES = [
    pltpu.SemaphoreType.DMA((Fan.PIECES,)),
    pltpu.SemaphoreType.DMA((4, Fan.PIECES)),
    pltpu.SemaphoreType.DMA((2, 4, Fan.PIECES)),
]


def gains_rows(total):
    one = jnp.concatenate([total[i : i + 1] for i in range(8)], axis=1)
    two = jnp.concatenate([total[i : i + 1] for i in range(8, 16)], axis=1)
    return one, two, total[16:17], total[17:18]


def unit_of(values):
    scale = lax.rsqrt(jnp.mean(values * values, axis=-1, keepdims=True) + EPS)
    return values * scale, scale


class Home:
    def __init__(self, place, kept, given, taken, summed, landed, semaphores):
        self.p = place
        self.kept, self.given, self.taken, self.summed, self.landed = kept, given, taken, summed, landed
        self.given_send, self.taken_receive, self.summed_send, self.landed_receive = semaphores

    def block(self, k):
        k = 3 - k
        return self.p.plane(k // 2, k % 2)

    def mine(self, k):
        return self.p.c == (self.p.b if k % 2 else 1 - self.p.b)

    def give(self, slot):
        return remote(
            self.given.at[slot],
            self.taken.at[slot],
            self.given_send.at[slot],
            self.taken_receive.at[slot],
            (self.p.sibling, self.p.t),
        )

    def send(self, k):
        p = self.p
        return remote(
            self.summed.at[k // 2],
            self.landed.at[p.b],
            self.summed_send.at[k // 2],
            self.landed_receive.at[p.b],
            (2 * p.col + p.a, self.block(k)),
        )

    def add(self, k, parts):
        @pl.when(self.mine(k))
        def _():
            for i, part in enumerate(parts):
                self.kept[:, i * 256 : (i + 1) * 256] = part()

        @pl.when(jnp.logical_not(self.mine(k)))
        def _():
            for i, part in enumerate(parts):
                self.given[k // 2, :, i * 256 : (i + 1) * 256] = part().astype(BF16)
            self.give(k // 2).start()

    def stays(self, k):
        return jnp.logical_and(self.p.a == self.p.c, k == 3)

    def settle(self, k):
        p = self.p

        @pl.when(self.mine(k))
        def _():
            self.give(k // 2).wait_recv()

            def total(target, slot):
                def act(at):
                    target[slot, at] = (
                        self.kept[at] + self.taken[k // 2, at].astype(F32)
                    ).astype(BF16)

                by_rows(self.kept.shape[0], act)

            if k == 3:
                pl.when(p.a == p.c)(lambda: total(self.landed, p.b))

                @pl.when(p.a != p.c)
                def _():
                    total(self.summed, k // 2)
                    self.send(k).start()
            else:
                total(self.summed, k // 2)
                self.send(k).start()

    def arrive(self):
        p = self.p

        def arrived(slot):
            remote(
                self.summed.at[0],
                self.landed.at[slot],
                self.summed_send.at[0],
                self.landed_receive.at[slot],
                (p.d, p.t),
            ).wait_recv()

        arrived(1 - p.b)
        here = jnp.logical_and(p.c == p.b, p.a == p.c)
        pl.when(jnp.logical_not(here))(lambda: arrived(p.b))

    def value(self, at):
        return self.landed[0, at].astype(F32) + self.landed[1, at].astype(F32)

    def finish(self):
        for k in range(4):

            @pl.when(jnp.logical_not(self.mine(k)))
            def _():
                self.give(k // 2).wait_send()

            sent = self.mine(k)
            if k == 3:
                sent = jnp.logical_and(sent, self.p.a != self.p.c)

            @pl.when(sent)
            def _():
                self.send(k).wait_send()


HOME_SEMAPHORES = [pltpu.SemaphoreType.DMA((2,))] * 4


class Quad:
    def __init__(self, place, block, whole, send, receive):
        self.p, self.whole_block, self.whole, self.sent, self.receive = place, block, whole, send, receive
        b, c = place.b, place.c
        self.slots = [2 * b + c, 2 * b + 1 - c, 2 * (1 - b) + c, 2 * (1 - b) + 1 - c]

    def copy(self, index, source, slot, device):
        return remote(
            source, self.whole.at[slot], self.sent.at[index], self.receive.at[slot], device
        )

    def near(self):
        p = self.p
        return self.copy(0, self.whole_block, self.slots[0], (p.d, p.near))

    def beside(self):
        p = self.p
        return self.copy(1, self.whole_block, self.slots[0], (p.sibling, p.t))

    def onward(self):
        p = self.p
        return self.copy(2, self.whole.at[self.slots[2]], self.slots[2], (p.sibling, p.t))

    def start(self):
        self.near().start()
        self.beside().start()
        self.whole[self.slots[0]] = self.whole_block[...]

    def take(self, index):
        slot = self.slots[index]
        self.copy(0, self.whole_block, slot, (self.p.d, self.p.near)).wait_recv()
        if index == 2:
            self.onward().start()

    def finish(self):
        self.near().wait_send()
        self.beside().wait_send()
        self.onward().wait_send()


QUAD_SEMAPHORES = [pltpu.SemaphoreType.DMA((3,)), pltpu.SemaphoreType.DMA((4,))]


class PairSum:
    def __init__(self, place, kept, given, taken, summed, landed, given_send, taken_receive, across):
        self.p = place
        self.kept, self.given, self.taken, self.summed, self.landed = kept, given, taken, summed, landed
        self.given_send, self.taken_receive, self.across = given_send, taken_receive, across

    def give(self, half):
        return remote(
            self.given.at[half],
            self.taken.at[half],
            self.given_send.at[half],
            self.taken_receive.at[half],
            (self.p.sibling, self.p.t),
        )

    def send(self):
        p = self.p
        return remote(self.summed, self.landed, self.across.at[0], self.across.at[1], (p.d, p.near))

    def relay(self):
        self.give(1).wait_recv()

        def far(at):
            self.summed[at] = (self.kept[1, at] + self.taken[1, at].astype(F32)).astype(BF16)

        def own(at):
            self.kept[0, at] += self.taken[0, at].astype(F32)

        by_rows(self.summed.shape[0], far)
        self.send().start()
        self.give(0).wait_recv()
        by_rows(self.summed.shape[0], own)

    def arrive(self):
        self.send().wait_recv()

    def value(self, at):
        return self.kept[0, at] + self.landed[at].astype(F32)

    def finish(self):
        self.give(0).wait_send()
        self.give(1).wait_send()
        self.send().wait_send()


PAIR_SEMAPHORES = [pltpu.SemaphoreType.DMA((2,))] * 3


class Collect:
    def __init__(self, place, source, slots, summed, landed, send, receive, across):
        self.p, self.source, self.slots, self.summed, self.landed = place, source, slots, summed, landed
        self.send, self.receive, self.across = send, receive, across
        self.rows = slots.shape[1]

    def part(self, index):
        return self.source.at[pl.ds(pl.multiple_of(index * self.rows, self.rows), self.rows)]

    def own(self):
        p = self.p
        return pltpu.make_async_copy(self.part(p.d), self.slots.at[p.d], self.send.at[p.d])

    def other(self, target):
        p = self.p
        return remote(
            self.part(target),
            self.slots.at[p.d],
            self.send.at[target],
            self.receive.at[p.d],
            (target, p.t),
        )

    def start(self, chunk, size):
        count = size // self.rows

        def body(i, _):
            target = chunk * count + i
            pl.when(target == self.p.d)(lambda: self.own().start())
            pl.when(target != self.p.d)(lambda: self.other(target).start())
            return 0

        lax.fori_loop(0, count, body, 0)

    def cross(self):
        p = self.p
        return remote(self.summed, self.landed, self.across.at[0], self.across.at[1], (p.d, p.far))

    def total(self, core, here):
        return lax.fori_loop(
            1,
            self.p.columns,
            lambda i, s: s + self.slots[2 * i + core, :, here].astype(F32),
            self.slots[core, :, here].astype(F32),
        )

    def relay(self):
        p = self.p
        self.own().wait()
        for k in range(1, p.dp):
            source = lax.rem(p.d + k, p.dp)
            remote(
                self.part(source),
                self.slots.at[source],
                self.send.at[source],
                self.receive.at[source],
                (p.d, p.t),
            ).wait_recv()
        for begin in range(0, self.summed.shape[1], 256):
            here = slice(begin, begin + 256)
            self.summed[:, here] = self.total(1 - p.a, here).astype(BF16)
        self.cross().start()

    def result(self, targets):
        self.cross().wait_recv()
        begin = 0
        for target, turned in targets:
            for offset in range(0, target.shape[0 if turned else 1], 256):
                here = slice(begin, begin + 256)
                value = self.total(self.p.a, here) + self.landed[:, here].astype(F32)
                if turned:
                    target[offset : offset + 256] = value.T
                else:
                    target[:, offset : offset + 256] = value
                begin += 256

    def finish(self):
        p = self.p
        for k in range(1, p.dp):
            self.other(lax.rem(p.d + k, p.dp)).wait_send()
        self.cross().wait_send()


def collect_semaphores(dp):
    return [
        pltpu.SemaphoreType.DMA((dp,)),
        pltpu.SemaphoreType.DMA((dp,)),
        pltpu.SemaphoreType.DMA((2,)),
    ]


def vmem(count):
    return [pl.BlockSpec(memory_space=pltpu.VMEM)] * count


def params(identity):
    return pltpu.CompilerParams(
        collective_id=identity, has_side_effects=True, vmem_limit_bytes=VMEM_LIMIT
    )


def rotary(tokens):
    frequency = np.float32(THETA) ** (
        -(np.arange(HEAD // 2, dtype=np.float32) * np.float32(2.0)) / np.float32(HEAD)
    )
    angles = np.arange(tokens, dtype=np.float32)[:, None] * frequency.astype(np.float32)[None, :]
    return np.concatenate([np.cos(angles), np.sin(angles)], axis=1).astype(np.float32)


def rotary_rows(table):
    other = pltpu.roll(table, HEAD // 2, 1)
    low = lax.broadcasted_iota(jnp.int32, (1, HEAD), 1) < HEAD // 2
    return jnp.where(low, table, other), jnp.where(low, -other, table)


def allowed_mask(place, gains, base, rows, keys, transposed):
    lane = lax.broadcasted_iota(jnp.int32, (1, 128), 1)
    chosen = (lane == 2 * place.col + place.a).astype(F32)
    shape = (keys, rows) if transposed else (rows, keys)
    query_dim, key_dim = (1, 0) if transposed else (0, 1)
    line = lambda dim: tuple(n if i == dim else 1 for i, n in enumerate(shape))
    query = lax.broadcasted_iota(jnp.int32, shape, query_dim)
    key = lax.broadcasted_iota(jnp.int32, shape, key_dim)
    mask = (key <= query).astype(F32)
    for piece in range(2):
        numbers = gains[18 + piece : 19 + piece]
        first_position = jnp.sum(numbers * chosen, axis=1, keepdims=True) - base.astype(F32)

        def inside(position):
            position = position.astype(F32)
            return jnp.logical_and(
                position >= first_position, position < first_position + PIECE
            ).astype(F32)

        in_query = inside(lax.broadcasted_iota(jnp.int32, line(query_dim), query_dim))
        in_key = inside(lax.broadcasted_iota(jnp.int32, line(key_dim), key_dim))
        mask = jnp.maximum(mask, in_query * in_key)
    return mask


def placed(place, values, base):
    size = values.shape[1]
    begin = place.d * size
    if size < 128:
        values = jnp.concatenate([values, jnp.zeros((1, 128 - size), F32)], axis=1)
        values = pltpu.roll(values, lax.rem(begin, 128), 1)
    row = lax.broadcasted_iota(jnp.int32, (24, 128), 0)
    return jnp.where(row == base + lax.div(begin, 128), values, 0.0)


def share(place, tile, base, size):
    begin = place.d * size
    row = lax.broadcasted_iota(jnp.int32, (24, 128), 0)
    chosen = jnp.where(row == base + lax.div(begin, 128), tile, 0.0)
    values = jnp.sum(chosen, axis=0, keepdims=True)
    if size < 128:
        values = pltpu.roll(values, lax.rem(128 - lax.rem(begin, 128), 128), 1)
    return values[:, :size]


class Exchange:
    def __init__(self, place, tile, slots, send, receive, in_plane):
        self.p, self.tile, self.slots, self.in_plane = place, tile, slots, in_plane
        self.sent, self.receive = send, receive
        self.count = place.dp if in_plane else place.tensor
        self.me = place.d if in_plane else place.t

    def copy(self, k, slot):
        p = self.p
        other = lax.rem(self.me + k, self.count)
        device = (other, p.t) if self.in_plane else (p.d, other)
        return remote(
            self.tile, self.slots.at[slot], self.sent.at[k], self.receive.at[slot], device
        )

    def start(self):
        for k in range(1, self.count):
            self.copy(k, self.me).start()
        self.slots[self.me] = self.tile[...]

    def total(self):
        for k in range(1, self.count):
            self.copy(k, lax.rem(self.me + k, self.count)).wait_recv()
        return lax.fori_loop(1, self.count, lambda i, s: s + self.slots[i], self.slots[0])

    def finish(self):
        for k in range(1, self.count):
            self.copy(k, self.me).wait_send()


def exchange_semaphores(count):
    return [pltpu.SemaphoreType.DMA((count,)), pltpu.SemaphoreType.DMA((count,))]


def layer(dp, tensor, turned, names, *refs):
    r = types.SimpleNamespace(**dict(zip(names, refs)))
    rest = list(refs[len(names) :])

    def take(count):
        head, rest[:] = rest[:count], rest[count:]
        return head

    p = Place(dp, tensor)
    gains_out = Exchange(p, r.pack, r.gain_slots, *take(2), True)
    gains_plane = Exchange(p, r.gain_pack, r.plane_slots, *take(2), True)
    gains_tensor = Exchange(p, r.plane_sum, r.tensor_slots, *take(2), False)
    fan = Fan(p, r.x, r.tokens, *take(3))
    fan_back = Fan(p, r.block, r.tokens, *take(3))
    spread_a = Spread(p, r.wa, r.wa_stage, r.wa_whole, *take(3))
    spread_o = Spread(p, r.wo_shard, r.wo_stage, r.wo_whole, *take(3))
    spread_m = Spread(p, r.wm, r.wm_stage, r.wm_whole, *take(3))
    quad_ct = Quad(p, r.ct, r.ct_whole, *take(2))
    quad = Quad(p, r.block, r.normed_two, *take(2))
    home_buffers = (r.kept, r.given, r.taken, r.summed, r.landed)
    home = Home(p, *home_buffers, take(4))
    home_back = Home(p, *home_buffers, take(4))
    down_semaphores, back_semaphores = take(3), take(3)
    collect_m = Collect(p, r.wm_whole, r.cm_slots, r.wm, r.cm_landed, *take(3))
    collect_o = Collect(p, r.wo_whole, r.co_slots, r.wo_shard, r.co_landed, *take(3))
    collect_a = Collect(p, r.wa_whole, r.ca_slots, r.wa, r.ca_landed, *take(3))

    rows, width = r.x.shape
    nq, nk, units = r.wq.shape[1], r.wk.shape[1], r.wg.shape[1]
    heads, kv_heads, blocks = nq // HEAD, nk // HEAD, 4
    repeat = heads // kv_heads

    tile = jnp.zeros((24, 128), F32)
    for base, ref in ((0, r.gain_one), (8, r.gain_two), (16, r.q_gain), (17, r.k_gain)):
        tile = tile + placed(p, ref[...].astype(F32), base)
    row = lax.broadcasted_iota(jnp.int32, (24, 128), 0)
    lane = lax.broadcasted_iota(jnp.int32, (24, 128), 1)
    for piece in range(2):
        here = jnp.logical_and(row == 18 + piece, lane == p.d)
        tile = tile + jnp.where(here, r.starts[0, piece], 0).astype(F32)
    r.pack[...] = tile
    r.wa[:, :nq] = r.wq[...]
    r.wa[:, nq : nq + nk] = r.wk[...]
    r.wa[:, nq + nk :] = r.wv[...]
    p.barrier()
    gains_out.start()
    spread_a.cross_start()
    fan.start()
    spread_a.start(0)

    def turn(target, source, begin):
        if source.shape[0] == target.shape[0]:
            target[:, begin : begin + source.shape[1]] = source[...]
        else:
            for i in range(0, source.shape[0], 128):
                target[:, begin + i : begin + i + 128] = source[i : i + 128].T

    turn(r.wo_shard, r.wo, 0)
    r.wm[:, :units] = r.wg[...]
    r.wm[:, units : 2 * units] = r.wu[...]
    turn(r.wm, r.wd, 2 * units)
    fan.take(0)
    total = gains_out.total()
    r.gains[...] = total
    gain_one, gain_two, q_gain, k_gain = gains_rows(total)
    fan.take(1)
    spread_a.cross_wait()
    spread_a.start(1)
    spread_o.cross_start()
    spread_o.start(0)

    def normalize(slot):
        def act(at):
            unit, _ = unit_of(r.tokens[slot, at].astype(F32))
            r.normed[slot, at] = (unit * gain_one).astype(BF16)

        by_rows(rows, act)

    normalize(fan.slots[0])
    normalize(fan.slots[1])
    fan.take(2, 3)
    spread_m.cross_start()
    spread_a.forward()
    spread_m.start(0)
    quad_ct.start()
    normalize(fan.slots[2])
    normalize(fan.slots[3])
    spread_a.wait_whole()
    fan.finish()
    spread_a.wait_sends()

    def attention(v_wide, mask):
        v_wide[:, :, HEAD:] = jnp.ones((kv_heads, rows * 4, HEAD), BF16)

        def qkv(slot, _):
            at = pl.ds(pl.multiple_of(slot * rows, rows), rows)
            cosine, sine = rotary_rows(r.rotary[slot])

            def rotated(values, gain):
                unit_values, _ = unit_of(values)
                scaled = unit_values * gain
                return (scaled * cosine + pltpu.roll(scaled, 64, 1) * sine).astype(BF16)

            for part in range((nq + 2 * nk) // 256):
                product = nn(r.normed[slot], r.wa_whole[:, part * 256 : (part + 1) * 256])
                for half in range(2):
                    column = part * 256 + half * HEAD
                    values = product[:, half * HEAD : (half + 1) * HEAD]
                    if column < nq:
                        head = column // HEAD
                        r.q_pre[head, at] = values
                        r.q[head, at] = rotated(values, q_gain)
                    elif column < nq + nk:
                        head = (column - nq) // HEAD
                        r.k_pre[head, at] = values
                        r.k[head, at] = rotated(values, k_gain)
                    else:
                        v_wide[(column - nq - nk) // HEAD, at, :HEAD] = values.astype(BF16)
            return 0

        lax.fori_loop(0, 4, qkv, 0)

        def attend(k):
            block = home.block(k)
            mask[...] = allowed_mask(p, r.gains[...], block * rows, rows, 2 * rows, False)
            for number in range(blocks):

                @pl.when(block == number)
                def _():
                    at = slice(number * rows, (number + 1) * rows)

                    def group(g, _):
                        queries = r.q[pl.ds(g * repeat, repeat), at].reshape(repeat * rows, HEAD)
                        total = jnp.zeros((repeat * rows, 2 * HEAD), F32)
                        for kb in range(min(number + 2, blocks)):
                            keys = slice(kb * rows, (kb + 1) * rows)
                            weight = jnp.exp2(nt(queries, r.k[g, keys]) * (SCALE * LOG2E))
                            if kb >= number:
                                part = mask[:, (kb - number) * rows : (kb - number + 1) * rows]
                                weight = weight * jnp.concatenate([part] * repeat, axis=0)
                            total = total + nn(weight.astype(BF16), v_wide[g, keys])
                        summed = total[:, HEAD:]
                        result = (total[:, :HEAD] / summed).astype(BF16)
                        result = jnp.concatenate(
                            [result[i * rows : (i + 1) * rows] for i in range(repeat)], axis=1
                        )
                        wide = repeat * HEAD
                        r.mixed[at, pl.ds(pl.multiple_of(g * wide, wide), wide)] = result
                        logs = jnp.log2(summed)
                        for i in range(repeat):
                            across = logs[i * rows : (i + 1) * rows].T
                            r.lse[g * repeat + i, :, at] = across[0:1]
                        return 0

                    lax.fori_loop(0, kv_heads, group, 0)

        def project(k):
            at = pl.ds(pl.multiple_of(home.block(k) * rows, rows), rows)

            def part(i):
                return lambda: nt(r.mixed[at], r.wo_whole[i * 256 : (i + 1) * 256])

            home.add(k, [part(i) for i in range(width // 256)])

        spread_o.cross_wait()
        spread_o.start(1)
        attend(0)
        attend(1)
        spread_o.forward()
        quad_ct.take(1)
        attend(2)
        spread_o.wait_whole()
        project(0)
        project(1)
        home.settle(0)
        project(2)
        home.settle(1)
        attend(3)
        home.settle(2)
        project(3)
        home.settle(3)
        r.v[...] = v_wide[:, :, :HEAD]

    pl.run_scoped(
        attention,
        pltpu.VMEM((kv_heads, 4 * rows, 2 * HEAD), BF16),
        pltpu.VMEM((rows, 2 * rows), F32),
    )
    spread_m.cross_wait()
    spread_m.start(1)
    quad_ct.take(2)
    quad_ct.take(3)
    spread_o.wait_sends()
    home.arrive()

    def norm_two(at):
        hidden = r.x[at].astype(F32) + home.value(at)
        r.kept[at] = hidden
        unit, _ = unit_of(hidden)
        r.block[at] = (unit * gain_two).astype(BF16)

    by_rows(rows, norm_two)
    quad.start()
    quad.take(1)
    spread_m.forward()
    quad.take(2)
    quad.take(3)
    quad.finish()
    home.finish()
    spread_m.wait_whole()
    spread_m.wait_sends()

    def feed_forward(active, grad_gate, grad_up, down_kept, back_kept):
        down = PairSum(
            p, down_kept, r.given, r.taken, r.summed.at[0], r.down_landed, *down_semaphores
        )
        back = PairSum(
            p, back_kept, r.back_given, r.back_taken, r.back_summed, r.back_landed, *back_semaphores
        )
        wm = r.wm_whole

        def work(slot, keep, half):
            tokens, cotangent = r.normed_two[slot], r.ct_whole[slot]
            at = pl.ds(pl.multiple_of(slot * rows, rows), rows)
            for i in range(units // 256):
                here = slice(i * 256, (i + 1) * 256)
                gate = nn(tokens, wm[:, i * 256 : (i + 1) * 256])
                upward = nn(tokens, wm[:, units + i * 256 : units + (i + 1) * 256])
                grad = nn(cotangent, wm[:, 2 * units + i * 256 : 2 * units + (i + 1) * 256])
                sigmoid = 1.0 / (1.0 + jnp.exp2(gate * -LOG2E))
                silu = gate * sigmoid
                active[at, here] = (silu * upward).astype(BF16)
                grad_gate[at, here] = (
                    grad * upward * sigmoid * (1.0 + gate * (1.0 - sigmoid))
                ).astype(BF16)
                grad_up[at, here] = (grad * silu).astype(BF16)
            for i in range(width // 256):
                here = slice(i * 256, (i + 1) * 256)
                out = nt(grad_gate[at], wm[here, :units]) + nt(
                    grad_up[at], wm[here, units : 2 * units]
                )
                if keep:
                    back.kept[half, :, here] = out
                else:
                    back.given[half, :, here] = out.astype(BF16)
            if not keep:
                back.give(half).start()
            for i in range(width // 256):
                here = slice(i * 256, (i + 1) * 256)
                out = nt(active[at], wm[here, 2 * units :])
                if keep:
                    down.kept[half, :, here] = out
                else:
                    down.given[half, :, here] = out.astype(BF16)
            if not keep:
                down.give(half).start()

        def both(step, _):
            half = 1 - step
            other = lax.select(half == 1, 1 - p.b, p.b)
            work(2 * other + p.c, True, half)
            work(2 * other + 1 - p.c, False, half)
            return 0

        lax.fori_loop(0, 2, both, 0)
        back.relay()
        down.relay()

        def weight_grads(i, _):
            chunk = lax.rem(i + 1 + p.col, width // 256)
            at = pl.ds(pl.multiple_of(chunk * 256, 256), 256)
            tokens = r.normed_two[:, :, at].reshape(4 * rows, 256)
            wm[at, :units] = tn(tokens, grad_gate[...]).astype(BF16)
            wm[at, units : 2 * units] = tn(tokens, grad_up[...]).astype(BF16)
            cotangent = r.ct_whole[:, :, at].reshape(4 * rows, 256)
            wm[at, 2 * units :] = tn(cotangent, active[...]).astype(BF16)
            collect_m.start(chunk, 256)
            return 0

        lax.fori_loop(0, width // 256, weight_grads, 0)
        back.arrive()
        gain = gains_rows(r.gains[...])[1]
        r.gain_rows[...] = jnp.zeros_like(r.gain_rows)

        def norm_two_back(at):
            grad_normed = back.value(at)
            unit, scale = unit_of(r.kept[at])
            r.gain_rows[...] += jnp.sum(grad_normed * unit, axis=0, keepdims=True)
            scaled = grad_normed * gain
            mean = jnp.mean(scaled * unit, axis=-1, keepdims=True)
            grad = r.ct[at].astype(F32) + scale * (scaled - unit * mean)
            r.input_grad[at] = grad
            r.block[at] = grad.astype(BF16)

        by_rows(rows, norm_two_back)
        fan_back.start()
        fan_back.take(0)
        fan_back.take(1)
        for i in range(8):
            r.gain_pack[8 + i : 9 + i] = r.gain_rows[:, i * 128 : (i + 1) * 128]
        down.arrive()

        def output(at):
            r.output[at] = (r.kept[at] + down.value(at)).astype(BF16)

        by_rows(rows, output)
        back.finish()
        down.finish()

    r.gain_pack[16:24] = jnp.zeros((8, 128), F32)
    pl.run_scoped(
        feed_forward,
        *[pltpu.VMEM((4 * rows, units), BF16)] * 3,
        *[pltpu.VMEM((2, rows, width), F32)] * 2,
    )

    def attention_back(grads, grad_mixed, delta, mask, grad_keys, grad_values):
        for number in range(blocks):
            base = jnp.int32(number * rows)
            mask[number] = allowed_mask(p, r.gains[...], base, rows, 2 * rows, True)
        fan_back.take(2, 3)

        def mixed_back(slot, _):
            at = pl.ds(pl.multiple_of(slot * rows, rows), rows)
            for i in range(heads * HEAD // 256):
                grad = nn(r.tokens[slot], r.wo_whole[:, i * 256 : (i + 1) * 256]).astype(BF16)
                for j in range(256 // HEAD):
                    head = i * (256 // HEAD) + j
                    one = grad[:, j * HEAD : (j + 1) * HEAD]
                    grad_mixed[head, at] = one
                    mixed = r.mixed[at, head * HEAD : (head + 1) * HEAD]
                    row = lax.dot_general(
                        jnp.ones((8, HEAD), F32),
                        one.astype(F32) * mixed.astype(F32),
                        (((1,), (1,)), ((), ())),
                        precision=lax.Precision.HIGHEST,
                        preferred_element_type=F32,
                    )
                    delta[head, :, at] = row[0:1]
            return 0

        lax.fori_loop(0, 4, mixed_back, 0)

        def out_grads(i, _):
            chunk = lax.rem(i + 1 + p.col, width // 256)
            at = pl.ds(pl.multiple_of(chunk * 256, 256), 256)
            tokens = r.tokens[:, :, at].reshape(4 * rows, 256)
            r.wo_whole[at] = tn(tokens, r.mixed[...]).astype(BF16)
            collect_o.start(chunk, 256)
            return 0

        lax.fori_loop(0, width // 256, out_grads, 0)
        _, _, q_gain, k_gain = gains_rows(r.gains[...])

        def head_norm_back(grad, before, gain, number, row):
            unit, scale = unit_of(before)
            cosine, sine = rotary_rows(r.rotary[number])
            back = grad * cosine - pltpu.roll(grad, 64, 1) * sine
            r.gain_pack[row : row + 1] += jnp.sum(back * unit, axis=0, keepdims=True)
            scaled = back * gain
            mean = jnp.mean(scaled * unit, axis=-1, keepdims=True)
            return (scale * (scaled - unit * mean)).astype(BF16)

        def lanes(head, offset):
            return pl.ds(pl.multiple_of(offset + head * HEAD, HEAD), HEAD)

        def group(g, _):
            grad_keys[...] = jnp.zeros_like(grad_keys)
            grad_values[...] = jnp.zeros_like(grad_values)

            def head_back(i, _):
                head = g * repeat + i
                for number in range(blocks):
                    at = slice(number * rows, (number + 1) * rows)
                    queries, grad = r.q[head, at], grad_mixed[head, at]
                    logs, sums = r.lse[head, :, at], delta[head, :, at]
                    grad_queries = jnp.zeros((rows, HEAD), F32)
                    for kb in range(min(number + 2, blocks)):
                        here = slice(kb * rows, (kb + 1) * rows)
                        keys = r.k[g, here]
                        probs = jnp.exp2(nt(keys, queries) * (SCALE * LOG2E) - logs)
                        if kb >= number:
                            begin = (kb - number) * rows
                            probs = probs * mask[number, begin : begin + rows]
                        scores = (probs * (nt(r.v[g, here], grad) - sums)).astype(BF16)
                        grad_values[here] += nn(probs.astype(BF16), grad)
                        grad_keys[here] += nn(scores, queries)
                        grad_queries = grad_queries + tn(scores, keys)
                    grads[at, lanes(head, 0)] = head_norm_back(
                        grad_queries * SCALE, r.q_pre[head, at], q_gain, number, 16
                    )
                return 0

            lax.fori_loop(0, repeat, head_back, 0)
            for number in range(blocks):
                at = slice(number * rows, (number + 1) * rows)
                grads[at, lanes(g, nq)] = head_norm_back(
                    grad_keys[at] * SCALE, r.k_pre[g, at], k_gain, number, 17
                )
                grads[at, lanes(g, nq + nk)] = grad_values[at].astype(BF16)
            return 0

        lax.fori_loop(0, kv_heads, group, 0)
        collect_m.relay()
        collect_o.relay()

        def project(k):
            at = pl.ds(pl.multiple_of(home_back.block(k) * rows, rows), rows)

            def part(i):
                return lambda: nt(grads[at], r.wa_whole[i * 256 : (i + 1) * 256])

            home_back.add(k, [part(i) for i in range(width // 256)])

        project(0)
        project(1)
        home_back.settle(0)
        project(2)
        home_back.settle(1)
        project(3)
        home_back.settle(2)
        home_back.settle(3)

        def weight_grads(i, _):
            chunk = lax.rem(i + 1 + p.col, width // 256)
            at = pl.ds(pl.multiple_of(chunk * 256, 256), 256)
            tokens = r.normed[:, :, at].reshape(4 * rows, 256)
            r.wa_whole[at] = tn(tokens, grads[...]).astype(BF16)
            collect_a.start(chunk, 256)
            return 0

        lax.fori_loop(0, width // 256, weight_grads, 0)

    pl.run_scoped(
        attention_back,
        pltpu.VMEM((4 * rows, nq + 2 * nk), BF16),
        pltpu.VMEM((heads, 4 * rows, HEAD), BF16),
        pltpu.VMEM((heads, 1, 4 * rows), F32),
        pltpu.VMEM((4, 2 * rows, rows), F32),
        pltpu.VMEM((4 * rows, HEAD), F32),
        pltpu.VMEM((4 * rows, HEAD), F32),
    )
    collect_m.result([(r.grad_gate, False), (r.grad_up, False), (r.grad_down, turned)])
    collect_o.result([(r.grad_out, turned)])
    home_back.arrive()
    gain = gains_rows(r.gains[...])[0]
    r.gain_rows[...] = jnp.zeros_like(r.gain_rows)

    def norm_one_back(at):
        grad_normed = home_back.value(at)
        unit, scale = unit_of(r.x[at].astype(F32))
        r.gain_rows[...] += jnp.sum(grad_normed * unit, axis=0, keepdims=True)
        scaled = grad_normed * gain
        mean = jnp.mean(scaled * unit, axis=-1, keepdims=True)
        r.input_grad[at] += scale * (scaled - unit * mean)

    by_rows(rows, norm_one_back)
    for i in range(8):
        r.gain_pack[i : i + 1] = r.gain_rows[:, i * 128 : (i + 1) * 128]
    gains_plane.start()
    r.plane_sum[...] = gains_plane.total()
    gains_tensor.start()
    collect_a.relay()
    total = gains_tensor.total()
    for base, ref in (
        (0, r.grad_gain_one), (8, r.grad_gain_two), (16, r.grad_q_gain), (17, r.grad_k_gain),
    ):
        ref[...] = share(p, total, base, ref.shape[1])
    collect_a.result([(r.grad_query, False), (r.grad_key, False), (r.grad_value, False)])
    for part in (
        gains_out, gains_plane, gains_tensor, fan_back, quad_ct, home_back, collect_m, collect_o,
        collect_a,
    ):
        part.finish()


def call(dp, tensor, x, starts, gain_one, q_gain, k_gain, gain_two, wq, wk, wv, wo, wg, wu, wd, ct):
    rows, width = x.shape
    tokens = rows * tensor
    shard, nq = wq.shape
    nk, units = wk.shape[1], wg.shape[1]
    heads, kv_heads = nq // HEAD, nk // HEAD
    na, nm = nq + 2 * nk, 3 * units
    turned = shard % 128 == 0
    if not turned:
        wo, wd = wo.T, wd.T
    inputs = dict(
        x=x, starts=starts, gain_one=gain_one, q_gain=q_gain, k_gain=k_gain, gain_two=gain_two,
        wq=wq, wk=wk, wv=wv, wo=wo, wg=wg, wu=wu, wd=wd, ct=ct,
        rotary=jnp.asarray(rotary(tokens)).reshape(tensor, rows, HEAD),
    )
    outputs = dict(
        output=((rows, width), BF16),
        input_grad=((rows, width), F32),
        grad_gain_one=(gain_one.shape, F32),
        grad_q_gain=(q_gain.shape, F32),
        grad_k_gain=(k_gain.shape, F32),
        grad_query=((shard, nq), F32),
        grad_key=((shard, nk), F32),
        grad_value=((shard, nk), F32),
        grad_out=((nq, shard) if turned else (shard, nq), F32),
        grad_gain_two=(gain_two.shape, F32),
        grad_gate=((shard, units), F32),
        grad_up=((shard, units), F32),
        grad_down=((units, shard) if turned else (shard, units), F32),
    )
    scratch = dict(
        pack=((24, 128), F32),
        gain_slots=((dp, 24, 128), F32),
        gains=((24, 128), F32),
        gain_pack=((24, 128), F32),
        gain_rows=((1, width), F32),
        plane_slots=((dp, 24, 128), F32),
        plane_sum=((24, 128), F32),
        tensor_slots=((tensor, 24, 128), F32),
        tokens=((4, rows, width), BF16),
        normed=((4, rows, width), BF16),
        block=((rows, width), BF16),
        q=((heads, tokens, HEAD), BF16),
        k=((kv_heads, tokens, HEAD), BF16),
        v=((kv_heads, tokens, HEAD), BF16),
        q_pre=((heads, tokens, HEAD), F32),
        k_pre=((kv_heads, tokens, HEAD), F32),
        mixed=((tokens, nq), BF16),
        lse=((heads, 1, tokens), F32),
        normed_two=((4, rows, width), BF16),
        ct_whole=((4, rows, width), BF16),
        wa=((shard, na), BF16),
        wa_stage=((shard, na), BF16),
        wa_whole=((width, na), BF16),
        wo_shard=((shard, nq), BF16),
        wo_stage=((shard, nq), BF16),
        wo_whole=((width, nq), BF16),
        wm=((shard, nm), BF16),
        wm_stage=((shard, nm), BF16),
        wm_whole=((width, nm), BF16),
        kept=((rows, width), F32),
        given=((2, rows, width), BF16),
        taken=((2, rows, width), BF16),
        summed=((2, rows, width), BF16),
        landed=((2, rows, width), BF16),
        down_landed=((rows, width), BF16),
        back_given=((2, rows, width), BF16),
        back_taken=((2, rows, width), BF16),
        back_summed=((rows, width), BF16),
        back_landed=((rows, width), BF16),
        cm_slots=((dp, shard, nm), BF16),
        cm_landed=((shard, nm), BF16),
        co_slots=((dp, shard, nq), BF16),
        co_landed=((shard, nq), BF16),
        ca_slots=((dp, shard, na), BF16),
        ca_landed=((shard, na), BF16),
    )
    semaphores = [
        *exchange_semaphores(dp),
        *exchange_semaphores(dp),
        *exchange_semaphores(tensor),
        *FAN_SEMAPHORES,
        *FAN_SEMAPHORES,
        *spread_semaphores(dp),
        *spread_semaphores(dp),
        *spread_semaphores(dp),
        *QUAD_SEMAPHORES,
        *QUAD_SEMAPHORES,
        *HOME_SEMAPHORES,
        *HOME_SEMAPHORES,
        *PAIR_SEMAPHORES,
        *PAIR_SEMAPHORES,
        *collect_semaphores(dp),
        *collect_semaphores(dp),
        *collect_semaphores(dp),
    ]
    names = [*inputs, *outputs, *scratch]

    def body(*refs):
        layer_refs = list(refs)
        layer(dp, tensor, turned, names, *layer_refs)

    in_specs = vmem(len(inputs))
    in_specs[1] = pl.BlockSpec(memory_space=pltpu.SMEM)
    return pl.pallas_call(
        body,
        out_shape=[jax.ShapeDtypeStruct(*s) for s in outputs.values()],
        in_specs=in_specs,
        out_specs=vmem(len(outputs)),
        scratch_shapes=[pltpu.VMEM(*s) for s in scratch.values()] + semaphores,
        compiler_params=params(1),
    )(*inputs.values()), turned


def shards(dp, tensor, *args):
    x, starts, attn_gain, q_gain, k_gain, wq, wk, wv, wo, mlp_gain, wg, wu, wd, ct = args
    outs, turned = call(
        dp, tensor, x[0], starts, attn_gain[None], q_gain[None], k_gain[None], mlp_gain[None],
        wq, wk, wv, wo, wg, wu, wd, ct[0],
    )
    outs = list(outs)
    for i in (0, 1):
        outs[i] = outs[i][None]
    for i in (2, 3, 4, 9):
        outs[i] = outs[i][0]
    if not turned:
        for i in (8, 12):
            outs[i] = outs[i].T
    return tuple(outs)


def solution(mesh):
    sequence, square, turned = P("dp", "tensor", None), P("dp", "tensor"), P("tensor", "dp")
    gain = P("dp")
    in_specs = (
        sequence, P("dp", None), gain, gain, gain, square, square, square, turned, gain, square, square,
        turned, sequence,
    )
    out_specs = (
        sequence, sequence, gain, gain, gain, square, square, square, turned, gain, square, square,
        turned,
    )
    return jax.shard_map(
        functools.partial(shards, mesh.shape["dp"], mesh.shape["tensor"]),
        mesh=mesh,
        in_specs=in_specs,
        out_specs=out_specs,
        check_vma=False,
    )
```

```python
import functools
import math
import types

import jax
import jax.numpy as jnp
import numpy as np
from jax import lax
from jax.experimental import pallas as pl
from jax.experimental.pallas import tpu as pltpu
from jax.sharding import PartitionSpec as P

HEAD = 128
PIECE = 256
EPS = 1e-06
THETA = 1000000.0
SCALE = HEAD**-0.5
LOG2E = math.log2(math.e)
MESH = pl.DeviceIdType.MESH
F32 = jnp.float32
BF16 = jnp.bfloat16
VMEM_LIMIT = 62 * 2**20


def nt(x, y):
    return lax.dot_general(x, y, (((1,), (1,)), ((), ())), preferred_element_type=F32)


def nn(x, y):
    return lax.dot_general(x, y, (((1,), (0,)), ((), ())), preferred_element_type=F32)


def tn(x, y):
    return lax.dot_general(x, y, (((0,), (0,)), ((), ())), preferred_element_type=F32)


def start(copy):
    copy.start()


def wait(copy):
    copy.wait()


def wait_send(copy):
    copy.wait_send()


def by_rows(rows, act, step=64):
    def body(i, _):
        act(pl.ds(pl.multiple_of(i * step, step), step))
        return 0

    lax.fori_loop(0, rows // step, body, 0)


class Place:
    def __init__(self, dp, tensor):
        self.dp, self.tensor, self.columns = dp, tensor, dp // 2
        self.d = lax.axis_index("dp")
        self.t = lax.axis_index("tensor")
        self.col, self.c = lax.div(self.d, 2), lax.rem(self.d, 2)
        self.a, self.b = lax.div(self.t, 2), lax.rem(self.t, 2)
        self.sibling = self.d + 1 - 2 * self.c
        self.near = self.t + 1 - 2 * self.b
        self.far = self.t + 2 - 4 * self.a

    def barrier(self):
        semaphore = pltpu.get_barrier_semaphore()
        for k in range(1, self.dp):
            pl.semaphore_signal(
                semaphore, 1, device_id=(lax.rem(self.d + k, self.dp), self.t), device_id_type=MESH
            )
        for k in range(1, self.tensor):
            pl.semaphore_signal(
                semaphore,
                1,
                device_id=(self.d, lax.rem(self.t + k, self.tensor)),
                device_id_type=MESH,
            )
        pl.semaphore_wait(semaphore, self.dp + self.tensor - 2)

    def plane(self, bits_a, bits_b):
        first = self.a + bits_a - 2 * self.a * bits_a
        second = self.b + bits_b - 2 * self.b * bits_b
        return 2 * first + second


def remote(source, target, send, receive, device):
    return pltpu.make_async_remote_copy(
        src_ref=source,
        dst_ref=target,
        send_sem=send,
        recv_sem=receive,
        device_id=device,
        device_id_type=MESH,
    )


class Spread:
    def __init__(self, place, shard, stage, whole, send, receive, cross):
        self.p, self.shard, self.stage, self.whole = place, shard, stage, whole
        self.send, self.receive, self.cross = send, receive, cross
        self.rows = shard.shape[0]
        self.square = place.columns == 4
        y, x = lax.div(place.col, 2), lax.rem(place.col, 2)
        if self.square:
            self.side = [2 * y + 1 - x, 2 * (1 - y) + x]
            self.corner = 2 * (1 - y) + 1 - x

    def slot(self, index, half=None):
        size = self.rows if half is None else self.rows // 2
        begin = index * self.rows + (0 if half is None else half * size)
        return self.whole.at[pl.ds(pl.multiple_of(begin, size), size)]

    def crossing(self):
        p = self.p
        return remote(self.shard, self.stage, self.cross.at[0], self.cross.at[1], (p.d, p.far))

    def each(self, phase, act_remote, act_local):
        p = self.p
        source = self.shard if phase == 0 else self.stage
        core = p.a if phase == 0 else 1 - p.a
        columns = (
            [p.col] + self.side
            if self.square
            else [lax.rem(p.col + j, p.columns) for j in range(p.columns)]
        )
        for j, column in enumerate(columns):
            send = self.send.at[phase, j]

            def to_other():
                act_remote(
                    remote(
                        source,
                        self.slot(p.d),
                        send,
                        self.receive.at[p.d, 0],
                        (2 * column + core, p.t),
                    )
                )

            def to_self():
                act_local(pltpu.make_async_copy(source, self.slot(p.d), send))

            if j == 0 and act_local:
                pl.when(core == p.c)(to_self)
            if act_remote:
                if j:
                    to_other()
                else:
                    pl.when(core != p.c)(to_other)

    def start(self, phase):
        self.each(phase, start, start)

    def cross_start(self):
        self.crossing().start()

    def cross_wait(self):
        self.crossing().wait_recv()

    def landed(self, index, half):
        p = self.p
        part = self.slot(index, half)
        remote(
            part, part, self.send.at[0, 0], self.receive.at[index, half or 0], (p.d, p.t)
        ).wait_recv()

    def forwards(self, act):
        p = self.p
        for direction in range(2):
            for core in range(2):
                index = 2 * self.side[direction] + core
                part = self.slot(index, direction)
                act(
                    remote(
                        part,
                        part,
                        self.send.at[2 + direction, core],
                        self.receive.at[index, direction],
                        (2 * self.side[1 - direction] + p.c, p.t),
                    )
                )

    def forward(self):
        if self.square:
            for direction in range(2):
                for core in range(2):
                    self.landed(2 * self.side[direction] + core, None)
            self.forwards(start)

    def wait_whole(self):
        p = self.p
        self.each(0, None, wait)
        self.each(1, None, wait)
        if self.square:
            self.landed(p.sibling, None)
            for core in range(2):
                for half in range(2):
                    self.landed(2 * self.corner + core, half)
        else:
            for k in range(1, p.dp):
                self.landed(lax.rem(p.d + k, p.dp), None)

    def cross_sent(self):
        self.crossing().wait_send()

    def wait_sends(self):
        self.each(0, wait_send, None)
        self.each(1, wait_send, None)
        if self.square:
            self.forwards(wait_send)


def spread_semaphores(dp):
    return [
        pltpu.SemaphoreType.DMA((4, max(dp // 2, 4))),
        pltpu.SemaphoreType.DMA((dp, 2)),
        pltpu.SemaphoreType.DMA((2,)),
    ]


class Fan:
    PIECES = 4

    def __init__(self, place, block, whole, send, receive, onward):
        self.p, self.block, self.whole = place, block, whole
        self.send, self.receive, self.onward = send, receive, onward
        self.slots = [place.plane(k // 2, k % 2) for k in range(4)]
        self.rows = block.shape[0] // self.PIECES

    def first_hop(self, act):
        p = self.p
        plane = lax.select(p.a == p.c, p.near, p.c + 1)
        for piece in range(self.PIECES):
            at = pl.ds(piece * self.rows, self.rows)
            act(
                remote(
                    self.block.at[at],
                    self.whole.at[p.t, at],
                    self.send.at[piece],
                    self.receive.at[p.t, piece],
                    (p.d, plane),
                )
            )

    def start(self):
        p = self.p
        self.first_hop(start)

        @pl.when(p.a == p.c)
        def _():
            self.whole[p.t] = self.block[...]

    def hop(self, index, piece, device, row):
        part = self.whole.at[self.slots[index], pl.ds(piece * self.rows, self.rows)]
        return remote(
            part,
            part,
            self.onward.at[row, index, piece],
            self.receive.at[self.slots[index], piece],
            device,
        )

    def to_sibling(self, index, piece):
        return self.hop(index, piece, (self.p.sibling, self.p.t), 0)

    def to_near(self, index, piece):
        return self.hop(index, piece, (self.p.d, self.p.near), 1)

    def take(self, *indices):
        p = self.p
        for piece in range(self.PIECES):
            for index in indices:

                def arrived():
                    self.to_sibling(index, piece).wait_recv()

                if index == 0:
                    pl.when(p.a != p.c)(arrived)
                else:
                    arrived()

                @pl.when(p.a == p.c)
                def _():
                    if index >= 2:
                        pl.when(p.t == p.c + 1)(lambda: self.to_near(index, piece).start())
                    self.to_sibling(index, piece).start()

    def finish(self):
        p = self.p
        self.first_hop(wait_send)

        @pl.when(p.a == p.c)
        def _():
            for index in range(4):
                for piece in range(self.PIECES):
                    self.to_sibling(index, piece).wait_send()
                    if index >= 2:
                        pl.when(p.t == p.c + 1)(lambda: self.to_near(index, piece).wait_send())


FAN_SEMAPHORES = [
    pltpu.SemaphoreType.DMA((Fan.PIECES,)),
    pltpu.SemaphoreType.DMA((4, Fan.PIECES)),
    pltpu.SemaphoreType.DMA((2, 4, Fan.PIECES)),
]


def gains_rows(total):
    one = jnp.concatenate([total[i : i + 1] for i in range(8)], axis=1)
    two = jnp.concatenate([total[i : i + 1] for i in range(8, 16)], axis=1)
    return one, two, total[16:17], total[17:18]


def unit_of(values):
    scale = lax.rsqrt(jnp.mean(values * values, axis=-1, keepdims=True) + EPS)
    return values * scale, scale


class Home:
    def __init__(self, place, kept, given, taken, summed, landed, semaphores):
        self.p = place
        self.kept, self.given, self.taken, self.summed, self.landed = kept, given, taken, summed, landed
        self.given_send, self.taken_receive, self.summed_send, self.landed_receive = semaphores

    def block(self, k):
        k = 3 - k
        return self.p.plane(k // 2, k % 2)

    def mine(self, k):
        return self.p.c == (self.p.b if k % 2 else 1 - self.p.b)

    def give(self, slot):
        return remote(
            self.given.at[slot],
            self.taken.at[slot],
            self.given_send.at[slot],
            self.taken_receive.at[slot],
            (self.p.sibling, self.p.t),
        )

    def send(self, k):
        p = self.p
        return remote(
            self.summed.at[k // 2],
            self.landed.at[p.b],
            self.summed_send.at[k // 2],
            self.landed_receive.at[p.b],
            (2 * p.col + p.a, self.block(k)),
        )

    def add(self, k, parts):
        @pl.when(self.mine(k))
        def _():
            for i, part in enumerate(parts):
                self.kept[:, i * 256 : (i + 1) * 256] = part()

        @pl.when(jnp.logical_not(self.mine(k)))
        def _():
            for i, part in enumerate(parts):
                self.given[k // 2, :, i * 256 : (i + 1) * 256] = part().astype(BF16)
            self.give(k // 2).start()

    def stays(self, k):
        return jnp.logical_and(self.p.a == self.p.c, k == 3)

    def settle(self, k):
        p = self.p

        @pl.when(self.mine(k))
        def _():
            self.give(k // 2).wait_recv()

            def total(target, slot):
                def act(at):
                    target[slot, at] = (
                        self.kept[at] + self.taken[k // 2, at].astype(F32)
                    ).astype(BF16)

                by_rows(self.kept.shape[0], act)

            if k == 3:
                pl.when(p.a == p.c)(lambda: total(self.landed, p.b))

                @pl.when(p.a != p.c)
                def _():
                    total(self.summed, k // 2)
                    self.send(k).start()
            else:
                total(self.summed, k // 2)
                self.send(k).start()

    def arrive(self):
        p = self.p

        def arrived(slot):
            remote(
                self.summed.at[0],
                self.landed.at[slot],
                self.summed_send.at[0],
                self.landed_receive.at[slot],
                (p.d, p.t),
            ).wait_recv()

        arrived(1 - p.b)
        here = jnp.logical_and(p.c == p.b, p.a == p.c)
        pl.when(jnp.logical_not(here))(lambda: arrived(p.b))

    def value(self, at):
        return self.landed[0, at].astype(F32) + self.landed[1, at].astype(F32)

    def finish(self):
        for k in range(4):

            @pl.when(jnp.logical_not(self.mine(k)))
            def _():
                self.give(k // 2).wait_send()

            sent = self.mine(k)
            if k == 3:
                sent = jnp.logical_and(sent, self.p.a != self.p.c)

            @pl.when(sent)
            def _():
                self.send(k).wait_send()


HOME_SEMAPHORES = [pltpu.SemaphoreType.DMA((2,))] * 4


class Quad:
    def __init__(self, place, block, whole, send, receive):
        self.p, self.whole_block, self.whole, self.sent, self.receive = place, block, whole, send, receive
        b, c = place.b, place.c
        self.slots = [2 * b + c, 2 * b + 1 - c, 2 * (1 - b) + c, 2 * (1 - b) + 1 - c]

    def copy(self, index, source, slot, device):
        return remote(
            source, self.whole.at[slot], self.sent.at[index], self.receive.at[slot], device
        )

    def near(self):
        p = self.p
        return self.copy(0, self.whole_block, self.slots[0], (p.d, p.near))

    def beside(self):
        p = self.p
        return self.copy(1, self.whole_block, self.slots[0], (p.sibling, p.t))

    def onward(self):
        p = self.p
        return self.copy(2, self.whole.at[self.slots[2]], self.slots[2], (p.sibling, p.t))

    def start(self):
        self.near().start()
        self.beside().start()
        self.whole[self.slots[0]] = self.whole_block[...]

    def take(self, index):
        slot = self.slots[index]
        self.copy(0, self.whole_block, slot, (self.p.d, self.p.near)).wait_recv()
        if index == 2:
            self.onward().start()

    def finish(self):
        self.near().wait_send()
        self.beside().wait_send()
        self.onward().wait_send()


QUAD_SEMAPHORES = [pltpu.SemaphoreType.DMA((3,)), pltpu.SemaphoreType.DMA((4,))]


class PairSum:
    def __init__(self, place, kept, given, taken, summed, landed, given_send, taken_receive, across):
        self.p = place
        self.kept, self.given, self.taken, self.summed, self.landed = kept, given, taken, summed, landed
        self.given_send, self.taken_receive, self.across = given_send, taken_receive, across

    def give(self, half):
        return remote(
            self.given.at[half],
            self.taken.at[half],
            self.given_send.at[half],
            self.taken_receive.at[half],
            (self.p.sibling, self.p.t),
        )

    def send(self):
        p = self.p
        return remote(self.summed, self.landed, self.across.at[0], self.across.at[1], (p.d, p.near))

    def add_far(self):
        self.give(1).wait_recv()

        def act(at):
            self.summed[at] = (self.kept[1, at] + self.taken[1, at].astype(F32)).astype(BF16)

        by_rows(self.summed.shape[0], act)

    def take_own(self):
        self.give(0).wait_recv()

    def own(self, at):
        return self.kept[0, at] + self.taken[0, at].astype(F32)

    def arrive(self):
        self.send().wait_recv()

    def finish(self):
        self.give(0).wait_send()
        self.give(1).wait_send()


PAIR_SEMAPHORES = [pltpu.SemaphoreType.DMA((2,))] * 3


class Collect:
    def __init__(self, place, source, slots, summed, landed, send, receive, across):
        self.p, self.source, self.slots, self.summed, self.landed = place, source, slots, summed, landed
        self.send, self.receive, self.across = send, receive, across
        self.rows = slots.shape[1]

    def part(self, index):
        return self.source.at[pl.ds(pl.multiple_of(index * self.rows, self.rows), self.rows)]

    def own(self):
        p = self.p
        return pltpu.make_async_copy(self.part(p.d), self.slots.at[p.d], self.send.at[p.d])

    def other(self, target):
        p = self.p
        return remote(
            self.part(target),
            self.slots.at[p.d],
            self.send.at[target],
            self.receive.at[p.d],
            (target, p.t),
        )

    def start(self, chunk, size):
        count = size // self.rows

        def body(i, _):
            target = chunk * count + i
            pl.when(target == self.p.d)(lambda: self.own().start())
            pl.when(target != self.p.d)(lambda: self.other(target).start())
            return 0

        lax.fori_loop(0, count, body, 0)

    def cross(self):
        p = self.p
        return remote(self.summed, self.landed, self.across.at[0], self.across.at[1], (p.d, p.far))

    def total(self, core, here):
        return lax.fori_loop(
            1,
            self.p.columns,
            lambda i, s: s + self.slots[2 * i + core, :, here].astype(F32),
            self.slots[core, :, here].astype(F32),
        )

    def relay(self):
        p = self.p
        self.own().wait()
        for k in range(1, p.dp):
            source = lax.rem(p.d + k, p.dp)
            remote(
                self.part(source),
                self.slots.at[source],
                self.send.at[source],
                self.receive.at[source],
                (p.d, p.t),
            ).wait_recv()
        for begin in range(0, self.summed.shape[1], 256):
            here = slice(begin, begin + 256)
            self.summed[:, here] = self.total(1 - p.a, here).astype(BF16)
        self.cross().start()

    def result(self, targets):
        self.cross().wait_recv()
        begin = 0
        for target, first, count, turned in targets:
            for offset in range(0, count, min(count, 256)):
                size = min(count, 256)
                here = slice(begin, begin + size)
                there = slice(first + offset, first + offset + size)
                value = self.total(self.p.a, here) + self.landed[:, here].astype(F32)
                if turned:
                    target[there] = value.T
                else:
                    target[:, there] = value
                begin += size

    def finish(self):
        p = self.p
        for k in range(1, p.dp):
            self.other(lax.rem(p.d + k, p.dp)).wait_send()
        self.cross().wait_send()


def collect_semaphores(dp):
    return [
        pltpu.SemaphoreType.DMA((dp,)),
        pltpu.SemaphoreType.DMA((dp,)),
        pltpu.SemaphoreType.DMA((2,)),
    ]


def vmem(count):
    return [pl.BlockSpec(memory_space=pltpu.VMEM)] * count


def params(identity):
    return pltpu.CompilerParams(
        collective_id=identity, has_side_effects=True, vmem_limit_bytes=VMEM_LIMIT
    )


def rotary(tokens):
    frequency = np.float32(THETA) ** (
        -(np.arange(HEAD // 2, dtype=np.float32) * np.float32(2.0)) / np.float32(HEAD)
    )
    angles = np.arange(tokens, dtype=np.float32)[:, None] * frequency.astype(np.float32)[None, :]
    return np.concatenate([np.cos(angles), np.sin(angles)], axis=1).astype(np.float32)


def rotary_rows(table):
    other = pltpu.roll(table, HEAD // 2, 1)
    low = lax.broadcasted_iota(jnp.int32, (1, HEAD), 1) < HEAD // 2
    return jnp.where(low, table, other), jnp.where(low, -other, table)


def allowed_mask(place, gains, base, rows, keys, transposed):
    lane = lax.broadcasted_iota(jnp.int32, (1, 128), 1)
    chosen = (lane == 2 * place.col + place.a).astype(F32)
    shape = (keys, rows) if transposed else (rows, keys)
    query_dim, key_dim = (1, 0) if transposed else (0, 1)
    line = lambda dim: tuple(n if i == dim else 1 for i, n in enumerate(shape))
    query = lax.broadcasted_iota(jnp.int32, shape, query_dim)
    key = lax.broadcasted_iota(jnp.int32, shape, key_dim)
    mask = (key <= query).astype(F32)
    for piece in range(2):
        numbers = gains[18 + piece : 19 + piece]
        first_position = jnp.sum(numbers * chosen, axis=1, keepdims=True) - base.astype(F32)

        def inside(position):
            position = position.astype(F32)
            return jnp.logical_and(
                position >= first_position, position < first_position + PIECE
            ).astype(F32)

        in_query = inside(lax.broadcasted_iota(jnp.int32, line(query_dim), query_dim))
        in_key = inside(lax.broadcasted_iota(jnp.int32, line(key_dim), key_dim))
        mask = jnp.maximum(mask, in_query * in_key)
    return mask


def placed(place, values, base):
    size = values.shape[1]
    begin = place.d * size
    if size < 128:
        values = jnp.concatenate([values, jnp.zeros((1, 128 - size), F32)], axis=1)
        values = pltpu.roll(values, lax.rem(begin, 128), 1)
    row = lax.broadcasted_iota(jnp.int32, (24, 128), 0)
    return jnp.where(row == base + lax.div(begin, 128), values, 0.0)


def share(place, tile, base, size):
    begin = place.d * size
    row = lax.broadcasted_iota(jnp.int32, (24, 128), 0)
    chosen = jnp.where(row == base + lax.div(begin, 128), tile, 0.0)
    values = jnp.sum(chosen, axis=0, keepdims=True)
    if size < 128:
        values = pltpu.roll(values, lax.rem(128 - lax.rem(begin, 128), 128), 1)
    return values[:, :size]


class Exchange:
    def __init__(self, place, tile, slots, send, receive, in_plane):
        self.p, self.tile, self.slots, self.in_plane = place, tile, slots, in_plane
        self.sent, self.receive = send, receive
        self.count = place.dp if in_plane else place.tensor
        self.me = place.d if in_plane else place.t

    def copy(self, k, slot):
        p = self.p
        other = lax.rem(self.me + k, self.count)
        device = (other, p.t) if self.in_plane else (p.d, other)
        return remote(
            self.tile, self.slots.at[slot], self.sent.at[k], self.receive.at[slot], device
        )

    def start(self):
        for k in range(1, self.count):
            self.copy(k, self.me).start()
        self.slots[self.me] = self.tile[...]

    def total(self):
        for k in range(1, self.count):
            self.copy(k, lax.rem(self.me + k, self.count)).wait_recv()
        return lax.fori_loop(1, self.count, lambda i, s: s + self.slots[i], self.slots[0])

    def finish(self):
        for k in range(1, self.count):
            self.copy(k, self.me).wait_send()


def exchange_semaphores(count):
    return [pltpu.SemaphoreType.DMA((count,)), pltpu.SemaphoreType.DMA((count,))]


def layer(dp, tensor, turned, names, *refs):
    r = types.SimpleNamespace(**dict(zip(names, refs)))
    rest = list(refs[len(names) :])

    def take(count):
        head, rest[:] = rest[:count], rest[count:]
        return head

    p = Place(dp, tensor)
    gains_out = Exchange(p, r.pack, r.gain_slots, *take(2), True)
    gains_plane = Exchange(p, r.gain_pack, r.plane_slots, *take(2), True)
    gains_tensor = Exchange(p, r.plane_sum, r.tensor_slots, *take(2), False)
    fan = Fan(p, r.x, r.tokens, *take(3))
    fan_back = Fan(p, r.block, r.tokens, *take(3))
    spread_a = Spread(p, r.wa, r.wa_stage, r.wa_whole, *take(3))
    spread_o = Spread(p, r.wo_shard, r.wo_stage, r.wo_whole, *take(3))
    units = r.wg.shape[1]
    thirds = [slice(i * units, (i + 1) * units) for i in range(3)]
    spread_m = [
        Spread(p, r.wm.at[:, c], r.wm_stage.at[:, c], r.wm_whole.at[:, c], *take(3)) for c in thirds
    ]
    quad_ct = Quad(p, r.ct, r.ct_whole, *take(2))
    quad = Quad(p, r.block, r.normed_two, *take(2))
    home_buffers = (r.kept, r.given, r.taken, r.summed, r.landed)
    home = Home(p, *home_buffers, take(4))
    home_back = Home(p, *home_buffers, take(4))
    down_semaphores, back_semaphores = take(3), take(3)
    collect_m = [
        Collect(
            p, r.wm_whole.at[:, c], r.cm_slots.at[:, :, c], r.wm.at[:, c], r.cm_landed.at[:, c], *take(3)
        )
        for c in thirds
    ]
    collect_o = Collect(p, r.wo_whole, r.co_slots, r.wo_shard, r.co_landed, *take(3))
    rows, width = r.x.shape
    nq, nk = r.wq.shape[1], r.wk.shape[1]
    heads, kv_heads, blocks = nq // HEAD, nk // HEAD, 4
    repeat = heads // kv_heads
    wide = (repeat + 2) * HEAD
    of_group = [slice(g * wide, (g + 1) * wide) for g in range(kv_heads)]
    collect_a_semaphores = [take(3) for _ in of_group]

    tile = jnp.zeros((24, 128), F32)
    for base, ref in ((0, r.gain_one), (8, r.gain_two), (16, r.q_gain), (17, r.k_gain)):
        tile = tile + placed(p, ref[...].astype(F32), base)
    row = lax.broadcasted_iota(jnp.int32, (24, 128), 0)
    lane = lax.broadcasted_iota(jnp.int32, (24, 128), 1)
    for piece in range(2):
        here = jnp.logical_and(row == 18 + piece, lane == p.d)
        tile = tile + jnp.where(here, r.starts[0, piece], 0).astype(F32)
    r.pack[...] = tile
    for g in range(kv_heads):
        begin = g * wide
        for ref, size in ((r.wq, repeat * HEAD), (r.wk, HEAD), (r.wv, HEAD)):
            r.wa[:, begin : begin + size] = ref[:, g * size : (g + 1) * size]
            begin += size
    p.barrier()
    gains_out.start()
    spread_a.cross_start()
    pl.when(p.a == p.c)(fan.start)
    spread_a.start(0)

    def turn(target, source, begin):
        if source.shape[0] == target.shape[0]:
            target[:, begin : begin + source.shape[1]] = source[...]
        else:
            for i in range(0, source.shape[0], 128):
                target[:, begin + i : begin + i + 128] = source[i : i + 128].T

    turn(r.wo_shard, r.wo, 0)
    r.wm[:, :units] = r.wg[...]
    r.wm[:, units : 2 * units] = r.wu[...]
    turn(r.wm, r.wd, 2 * units)
    total = gains_out.total()
    r.gains[...] = total
    gain_one, gain_two, q_gain, k_gain = gains_rows(total)
    fan.take(0)
    spread_a.cross_sent()
    pl.when(p.a != p.c)(fan.start)
    spread_a.cross_wait()
    spread_a.start(1)
    spread_o.start(0)
    fan.take(1)
    spread_a.forward()
    fan.take(2, 3)
    spread_o.cross_start()
    spread_m[0].cross_start()
    for part in spread_m:
        part.start(0)

    def normalize(slot):
        def act(at):
            unit, _ = unit_of(r.tokens[slot, at].astype(F32))
            r.normed[slot, at] = (unit * gain_one).astype(BF16)

        by_rows(rows, act)

    for slot in fan.slots:
        normalize(slot)
    spread_a.wait_whole()
    fan.finish()
    spread_a.wait_sends()

    def attention(v_wide, mask):
        v_wide[:, :, HEAD:] = jnp.ones((kv_heads, rows * 4, HEAD), BF16)

        def qkv(slot, _):
            at = pl.ds(pl.multiple_of(slot * rows, rows), rows)
            cosine, sine = rotary_rows(r.rotary[slot])

            def rotated(values, gain):
                unit_values, _ = unit_of(values)
                scaled = unit_values * gain
                return (scaled * cosine + pltpu.roll(scaled, 64, 1) * sine).astype(BF16)

            for g in range(kv_heads):
                for i in range(0, repeat + 2, 2):
                    begin = g * wide + i * HEAD
                    product = nn(r.normed[slot], r.wa_whole[:, begin : begin + 2 * HEAD])
                    for j in range(2):
                        values = product[:, j * HEAD : (j + 1) * HEAD]
                        if i + j < repeat:
                            r.q_pre[g * repeat + i + j, at] = values
                            r.q[g * repeat + i + j, at] = rotated(values, q_gain)
                        elif i + j == repeat:
                            r.k_pre[g, at] = values
                            r.k[g, at] = rotated(values, k_gain)
                        else:
                            v_wide[g, at, :HEAD] = values.astype(BF16)
            return 0

        lax.fori_loop(0, 4, qkv, 0)

        def attend(k):
            block = home.block(k)
            mask[...] = allowed_mask(p, r.gains[...], block * rows, rows, 2 * rows, False)
            for number in range(blocks):

                @pl.when(block == number)
                def _():
                    at = slice(number * rows, (number + 1) * rows)

                    def group(g, _):
                        queries = r.q[pl.ds(g * repeat, repeat), at].reshape(repeat * rows, HEAD)
                        total = jnp.zeros((repeat * rows, 2 * HEAD), F32)
                        for kb in range(min(number + 2, blocks)):
                            keys = slice(kb * rows, (kb + 1) * rows)
                            weight = jnp.exp2(nt(queries, r.k[g, keys]) * (SCALE * LOG2E))
                            if kb >= number:
                                part = mask[:, (kb - number) * rows : (kb - number + 1) * rows]
                                weight = weight * jnp.concatenate([part] * repeat, axis=0)
                            total = total + nn(weight.astype(BF16), v_wide[g, keys])
                        summed = total[:, HEAD:]
                        result = (total[:, :HEAD] / summed).astype(BF16)
                        result = jnp.concatenate(
                            [result[i * rows : (i + 1) * rows] for i in range(repeat)], axis=1
                        )
                        size = repeat * HEAD
                        r.mixed[at, pl.ds(pl.multiple_of(g * size, size), size)] = result
                        logs = jnp.log2(summed)
                        for i in range(repeat):
                            across = logs[i * rows : (i + 1) * rows].T
                            r.lse[g * repeat + i, :, at] = across[0:1]
                        return 0

                    lax.fori_loop(0, kv_heads, group, 0)

        def project(k):
            at = pl.ds(pl.multiple_of(home.block(k) * rows, rows), rows)

            def part(i):
                return lambda: nt(r.mixed[at], r.wo_whole[i * 256 : (i + 1) * 256])

            home.add(k, [part(i) for i in range(width // 256)])

        spread_o.cross_wait()
        spread_o.start(1)
        attend(0)
        spread_m[1].cross_start()
        attend(1)
        spread_o.forward()
        spread_o.wait_whole()
        project(0)
        project(1)
        home.settle(0)
        attend(2)
        home.settle(1)
        project(2)
        attend(3)
        home.settle(2)
        project(3)
        spread_m[2].cross_start()
        home.settle(3)
        quad_ct.start()
        r.v[...] = v_wide[:, :, :HEAD]

    pl.run_scoped(
        attention,
        pltpu.VMEM((kv_heads, 4 * rows, 2 * HEAD), BF16),
        pltpu.VMEM((rows, 2 * rows), F32),
    )
    spread_m[0].cross_wait()
    spread_m[0].start(1)
    spread_m[1].cross_wait()
    spread_m[1].start(1)
    quad_ct.take(1)
    quad_ct.take(2)
    home.arrive()

    def norm_two(at):
        hidden = r.x[at].astype(F32) + home.value(at)
        r.kept[at] = hidden
        unit, _ = unit_of(hidden)
        r.block[at] = (unit * gain_two).astype(BF16)

    by_rows(rows, norm_two)
    quad.start()
    spread_m[2].cross_wait()
    spread_m[2].start(1)
    spread_m[0].forward()
    quad_ct.take(3)
    spread_m[1].forward()
    quad.take(1)
    quad.take(2)
    quad.take(3)
    spread_m[2].forward()
    quad.finish()
    home.finish()
    spread_o.cross_sent()
    spread_o.wait_sends()
    for part in spread_m:
        part.wait_whole()
    for part in spread_m:
        part.cross_sent()
        part.wait_sends()

    def feed_forward(active, grad_gate, grad_up, down_kept, back_kept):
        down = PairSum(
            p, down_kept, r.given, r.taken, r.summed.at[0], r.down_landed, *down_semaphores
        )
        back = PairSum(
            p, back_kept, r.back_given, r.back_taken, r.back_summed, r.back_landed, *back_semaphores
        )
        wm = r.wm_whole

        def work(slot, keep, half):
            tokens, cotangent = r.normed_two[slot], r.ct_whole[slot]
            at = pl.ds(pl.multiple_of(slot * rows, rows), rows)
            for i in range(units // 256):
                here = slice(i * 256, (i + 1) * 256)
                gate = nn(tokens, wm[:, i * 256 : (i + 1) * 256])
                upward = nn(tokens, wm[:, units + i * 256 : units + (i + 1) * 256])
                grad = nn(cotangent, wm[:, 2 * units + i * 256 : 2 * units + (i + 1) * 256])
                sigmoid = 1.0 / (1.0 + jnp.exp2(gate * -LOG2E))
                silu = gate * sigmoid
                active[at, here] = (silu * upward).astype(BF16)
                grad_gate[at, here] = (
                    grad * upward * sigmoid * (1.0 + gate * (1.0 - sigmoid))
                ).astype(BF16)
                grad_up[at, here] = (grad * silu).astype(BF16)
            for i in range(width // 256):
                here = slice(i * 256, (i + 1) * 256)
                out = nt(grad_gate[at], wm[here, :units]) + nt(
                    grad_up[at], wm[here, units : 2 * units]
                )
                if keep:
                    back.kept[half, :, here] = out
                else:
                    back.given[half, :, here] = out.astype(BF16)
            if not keep:
                back.give(half).start()
            for i in range(width // 256):
                here = slice(i * 256, (i + 1) * 256)
                out = nt(active[at], wm[here, 2 * units :])
                if keep:
                    down.kept[half, :, here] = out
                else:
                    down.given[half, :, here] = out.astype(BF16)
            if not keep:
                down.give(half).start()

        def both(step, _):
            half = 1 - step
            other = lax.select(half == 1, 1 - p.b, p.b)
            work(2 * other + p.c, True, half)
            work(2 * other + 1 - p.c, False, half)

            @pl.when(half == 1)
            def _():
                back.add_far()
                back.send().start()

            return 0

        lax.fori_loop(0, 2, both, 0)

        def weight_grads(third, tokens_ref, grad):
            def body(i, _):
                chunk = lax.rem(i + 1 + p.col, width // 256)
                at = pl.ds(pl.multiple_of(chunk * 256, 256), 256)
                tokens = tokens_ref[:, :, at].reshape(4 * rows, 256)
                wm[at, thirds[third]] = tn(tokens, grad[...]).astype(BF16)
                collect_m[third].start(chunk, 256)
                return 0

            lax.fori_loop(0, width // 256, body, 0)

        weight_grads(0, r.normed_two, grad_gate)
        weight_grads(1, r.normed_two, grad_up)
        weight_grads(2, r.ct_whole, active)
        down.add_far()
        down.take_own()
        back.take_own()
        back.arrive()
        gain = gains_rows(r.gains[...])[1]
        r.gain_rows[...] = jnp.zeros_like(r.gain_rows)

        def norm_two_back(at):
            grad_normed = back.own(at) + back.landed[at].astype(F32)
            unit, scale = unit_of(r.kept[at])
            r.gain_rows[...] += jnp.sum(grad_normed * unit, axis=0, keepdims=True)
            scaled = grad_normed * gain
            mean = jnp.mean(scaled * unit, axis=-1, keepdims=True)
            grad = r.ct[at].astype(F32) + scale * (scaled - unit * mean)
            r.input_grad[at] = grad
            r.block[at] = grad.astype(BF16)

        by_rows(rows, norm_two_back)
        fan_back.start()
        fan_back.take(0)

        def hidden_sum(at):
            r.kept[at] += down.own(at)

        by_rows(rows, hidden_sum)
        for i in range(8):
            r.gain_pack[8 + i : 9 + i] = r.gain_rows[:, i * 128 : (i + 1) * 128]
        fan_back.take(1)
        back.send().wait_send()
        back.finish()
        down.finish()

    r.gain_pack[16:24] = jnp.zeros((8, 128), F32)
    pl.run_scoped(
        feed_forward,
        *[pltpu.VMEM((4 * rows, units), BF16)] * 3,
        *[pltpu.VMEM((2, rows, width), F32)] * 2,
    )

    def attention_back(grads, grad_mixed, delta, mask, grad_keys, grad_values, grad_wa):
        collect_a = [
            Collect(
                p, grad_wa.at[:, c], r.ca_slots.at[:, :, c], r.wa.at[:, c], r.ca_landed.at[:, c],
                *semaphores,
            )
            for c, semaphores in zip(of_group, collect_a_semaphores)
        ]
        down_send = remote(
            r.summed.at[0], r.down_landed, down_semaphores[2].at[0], down_semaphores[2].at[1], (p.d, p.near)
        )
        for number in range(blocks):
            base = jnp.int32(number * rows)
            mask[number] = allowed_mask(p, r.gains[...], base, rows, 2 * rows, True)
        fan_back.take(2, 3)
        down_send.start()
        collect_m[0].relay()

        def mixed_back(slot, _):
            at = pl.ds(pl.multiple_of(slot * rows, rows), rows)
            for i in range(heads * HEAD // 256):
                grad = nn(r.tokens[slot], r.wo_whole[:, i * 256 : (i + 1) * 256]).astype(BF16)
                for j in range(256 // HEAD):
                    head = i * (256 // HEAD) + j
                    one = grad[:, j * HEAD : (j + 1) * HEAD]
                    grad_mixed[head, at] = one
                    mixed = r.mixed[at, head * HEAD : (head + 1) * HEAD]
                    row = lax.dot_general(
                        jnp.ones((8, HEAD), F32),
                        one.astype(F32) * mixed.astype(F32),
                        (((1,), (1,)), ((), ())),
                        precision=lax.Precision.HIGHEST,
                        preferred_element_type=F32,
                    )
                    delta[head, :, at] = row[0:1]
            return 0

        lax.fori_loop(0, 4, mixed_back, 0)

        def out_grads(i, _):
            chunk = lax.rem(i + 1 + p.col, width // 256)
            at = pl.ds(pl.multiple_of(chunk * 256, 256), 256)
            tokens = r.tokens[:, :, at].reshape(4 * rows, 256)
            r.wo_whole[at] = tn(tokens, r.mixed[...]).astype(BF16)
            collect_o.start(chunk, 256)
            return 0

        lax.fori_loop(0, width // 256, out_grads, 0)
        _, _, q_gain, k_gain = gains_rows(r.gains[...])

        def head_norm_back(grad, before, gain, number, row):
            unit, scale = unit_of(before)
            cosine, sine = rotary_rows(r.rotary[number])
            back = grad * cosine - pltpu.roll(grad, 64, 1) * sine
            r.gain_pack[row : row + 1] += jnp.sum(back * unit, axis=0, keepdims=True)
            scaled = back * gain
            mean = jnp.mean(scaled * unit, axis=-1, keepdims=True)
            return (scale * (scaled - unit * mean)).astype(BF16)

        def group(g):
            grad_keys[...] = jnp.zeros_like(grad_keys)
            grad_values[...] = jnp.zeros_like(grad_values)

            def head_back(i, _):
                head = g * repeat + i
                for number in range(blocks):
                    at = slice(number * rows, (number + 1) * rows)
                    queries, grad = r.q[head, at], grad_mixed[head, at]
                    logs, sums = r.lse[head, :, at], delta[head, :, at]
                    grad_queries = jnp.zeros((rows, HEAD), F32)
                    for kb in range(min(number + 2, blocks)):
                        here = slice(kb * rows, (kb + 1) * rows)
                        keys = r.k[g, here]
                        probs = jnp.exp2(nt(keys, queries) * (SCALE * LOG2E) - logs)
                        if kb >= number:
                            begin = (kb - number) * rows
                            probs = probs * mask[number, begin : begin + rows]
                        scores = (probs * (nt(r.v[g, here], grad) - sums)).astype(BF16)
                        grad_values[here] += nn(probs.astype(BF16), grad)
                        grad_keys[here] += nn(scores, queries)
                        grad_queries = grad_queries + tn(scores, keys)
                    grads[at, pl.ds(pl.multiple_of(g * wide + i * HEAD, HEAD), HEAD)] = head_norm_back(
                        grad_queries * SCALE, r.q_pre[head, at], q_gain, number, 16
                    )
                return 0

            lax.fori_loop(0, repeat, head_back, 0)
            key_columns = slice(g * wide + repeat * HEAD, g * wide + (repeat + 1) * HEAD)
            value_columns = slice(g * wide + (repeat + 1) * HEAD, (g + 1) * wide)
            for number in range(blocks):
                at = slice(number * rows, (number + 1) * rows)
                grads[at, key_columns] = head_norm_back(
                    grad_keys[at] * SCALE, r.k_pre[g, at], k_gain, number, 17
                )
                grads[at, value_columns] = grad_values[at].astype(BF16)

        def weight_grads(g):
            def body(i, _):
                chunk = lax.rem(i + 1 + p.col, width // 256)
                at = pl.ds(pl.multiple_of(chunk * 256, 256), 256)
                tokens = r.normed[:, :, at].reshape(4 * rows, 256)
                grad_wa[at, of_group[g]] = tn(tokens, grads[:, of_group[g]]).astype(BF16)
                collect_a[g].start(chunk, 256)
                return 0

            lax.fori_loop(0, width // 256, body, 0)

        def project(k):
            at = pl.ds(pl.multiple_of(home_back.block(k) * rows, rows), rows)

            def part(i):
                return lambda: nt(grads[at], r.wa_whole[i * 256 : (i + 1) * 256])

            home_back.add(k, [part(i) for i in range(width // 256)])

        for g in range(kv_heads - 1):
            group(g)
            weight_grads(g)
        collect_m[1].relay()
        group(kv_heads - 1)
        down_send.wait_recv()
        down_send.wait_send()

        def output(at):
            r.output[at] = (r.kept[at] + r.down_landed[at].astype(F32)).astype(BF16)

        by_rows(rows, output)
        collect_o.relay()
        project(0)
        project(1)
        home_back.settle(0)
        project(2)
        home_back.settle(1)
        project(3)
        home_back.settle(2)
        weight_grads(kv_heads - 1)
        home_back.settle(3)
        collect_m[2].relay()
        for part in collect_a[:-1]:
            part.relay()
        collect_m[0].result([(r.grad_gate, 0, units, False)])
        collect_m[1].result([(r.grad_up, 0, units, False)])
        home_back.arrive()
        gain = gains_rows(r.gains[...])[0]
        r.gain_rows[...] = jnp.zeros_like(r.gain_rows)

        def norm_one_back(at):
            grad_normed = home_back.value(at)
            unit, scale = unit_of(r.x[at].astype(F32))
            r.gain_rows[...] += jnp.sum(grad_normed * unit, axis=0, keepdims=True)
            scaled = grad_normed * gain
            mean = jnp.mean(scaled * unit, axis=-1, keepdims=True)
            r.input_grad[at] += scale * (scaled - unit * mean)

        by_rows(rows, norm_one_back)
        for i in range(8):
            r.gain_pack[i : i + 1] = r.gain_rows[:, i * 128 : (i + 1) * 128]
        gains_plane.start()
        collect_a[-1].relay()
        r.plane_sum[...] = gains_plane.total()
        gains_tensor.start()
        collect_m[2].result([(r.grad_down, 0, units, turned)])
        collect_o.result([(r.grad_out, 0, nq, turned)])
        total = gains_tensor.total()
        for base, ref in (
            (0, r.grad_gain_one), (8, r.grad_gain_two), (16, r.grad_q_gain), (17, r.grad_k_gain),
        ):
            ref[...] = share(p, total, base, ref.shape[1])
        for g, part in enumerate(collect_a):
            size = repeat * HEAD
            part.result(
                [
                    (r.grad_query, g * size, size, False),
                    (r.grad_key, g * HEAD, HEAD, False),
                    (r.grad_value, g * HEAD, HEAD, False),
                ]
            )
        for part in collect_a:
            part.finish()

    pl.run_scoped(
        attention_back,
        pltpu.VMEM((4 * rows, nq + 2 * nk), BF16),
        pltpu.VMEM((heads, 4 * rows, HEAD), BF16),
        pltpu.VMEM((heads, 1, 4 * rows), F32),
        pltpu.VMEM((4, 2 * rows, rows), F32),
        pltpu.VMEM((4 * rows, HEAD), F32),
        pltpu.VMEM((4 * rows, HEAD), F32),
        pltpu.VMEM((width, nq + 2 * nk), BF16),
    )
    for part in (
        gains_out, gains_plane, gains_tensor, fan_back, quad_ct, home_back, *collect_m, collect_o,
    ):
        part.finish()


def call(dp, tensor, x, starts, gain_one, q_gain, k_gain, gain_two, wq, wk, wv, wo, wg, wu, wd, ct):
    rows, width = x.shape
    tokens = rows * tensor
    shard, nq = wq.shape
    nk, units = wk.shape[1], wg.shape[1]
    heads, kv_heads = nq // HEAD, nk // HEAD
    na, nm = nq + 2 * nk, 3 * units
    turned = shard % 128 == 0
    if not turned:
        wo, wd = wo.T, wd.T
    inputs = dict(
        x=x, starts=starts, gain_one=gain_one, q_gain=q_gain, k_gain=k_gain, gain_two=gain_two,
        wq=wq, wk=wk, wv=wv, wo=wo, wg=wg, wu=wu, wd=wd, ct=ct,
        rotary=jnp.asarray(rotary(tokens)).reshape(tensor, rows, HEAD),
    )
    outputs = dict(
        output=((rows, width), BF16),
        input_grad=((rows, width), F32),
        grad_gain_one=(gain_one.shape, F32),
        grad_q_gain=(q_gain.shape, F32),
        grad_k_gain=(k_gain.shape, F32),
        grad_query=((shard, nq), F32),
        grad_key=((shard, nk), F32),
        grad_value=((shard, nk), F32),
        grad_out=((nq, shard) if turned else (shard, nq), F32),
        grad_gain_two=(gain_two.shape, F32),
        grad_gate=((shard, units), F32),
        grad_up=((shard, units), F32),
        grad_down=((units, shard) if turned else (shard, units), F32),
    )
    scratch = dict(
        pack=((24, 128), F32),
        gain_slots=((dp, 24, 128), F32),
        gains=((24, 128), F32),
        gain_pack=((24, 128), F32),
        gain_rows=((1, width), F32),
        plane_slots=((dp, 24, 128), F32),
        plane_sum=((24, 128), F32),
        tensor_slots=((tensor, 24, 128), F32),
        tokens=((4, rows, width), BF16),
        normed=((4, rows, width), BF16),
        block=((rows, width), BF16),
        q=((heads, tokens, HEAD), BF16),
        k=((kv_heads, tokens, HEAD), BF16),
        v=((kv_heads, tokens, HEAD), BF16),
        q_pre=((heads, tokens, HEAD), F32),
        k_pre=((kv_heads, tokens, HEAD), F32),
        mixed=((tokens, nq), BF16),
        lse=((heads, 1, tokens), F32),
        normed_two=((4, rows, width), BF16),
        ct_whole=((4, rows, width), BF16),
        wa=((shard, na), BF16),
        wa_stage=((shard, na), BF16),
        wa_whole=((width, na), BF16),
        wo_shard=((shard, nq), BF16),
        wo_stage=((shard, nq), BF16),
        wo_whole=((width, nq), BF16),
        wm=((shard, nm), BF16),
        wm_stage=((shard, nm), BF16),
        wm_whole=((width, nm), BF16),
        kept=((rows, width), F32),
        given=((2, rows, width), BF16),
        taken=((2, rows, width), BF16),
        summed=((2, rows, width), BF16),
        landed=((2, rows, width), BF16),
        down_landed=((rows, width), BF16),
        back_given=((2, rows, width), BF16),
        back_taken=((2, rows, width), BF16),
        back_summed=((rows, width), BF16),
        back_landed=((rows, width), BF16),
        cm_slots=((dp, shard, nm), BF16),
        cm_landed=((shard, nm), BF16),
        co_slots=((dp, shard, nq), BF16),
        co_landed=((shard, nq), BF16),
        ca_slots=((dp, shard, na), BF16),
        ca_landed=((shard, na), BF16),
    )
    semaphores = [
        *exchange_semaphores(dp),
        *exchange_semaphores(dp),
        *exchange_semaphores(tensor),
        *FAN_SEMAPHORES,
        *FAN_SEMAPHORES,
        *(spread_semaphores(dp) * 5),
        *QUAD_SEMAPHORES,
        *QUAD_SEMAPHORES,
        *HOME_SEMAPHORES,
        *HOME_SEMAPHORES,
        *PAIR_SEMAPHORES,
        *PAIR_SEMAPHORES,
        *(collect_semaphores(dp) * (4 + kv_heads)),
    ]
    names = [*inputs, *outputs, *scratch]

    def body(*refs):
        layer_refs = list(refs)
        layer(dp, tensor, turned, names, *layer_refs)

    in_specs = vmem(len(inputs))
    in_specs[1] = pl.BlockSpec(memory_space=pltpu.SMEM)
    return pl.pallas_call(
        body,
        out_shape=[jax.ShapeDtypeStruct(*s) for s in outputs.values()],
        in_specs=in_specs,
        out_specs=vmem(len(outputs)),
        scratch_shapes=[pltpu.VMEM(*s) for s in scratch.values()] + semaphores,
        compiler_params=params(1),
    )(*inputs.values()), turned


def copies_kernel(count, *refs):
    for source, target in zip(refs[:count], refs[count:]):
        target[...] = source[...]


def copied(arrays):
    return pl.pallas_call(
        functools.partial(copies_kernel, len(arrays)),
        out_shape=[jax.ShapeDtypeStruct(a.shape, a.dtype) for a in arrays],
        in_specs=vmem(len(arrays)),
        out_specs=vmem(len(arrays)),
    )(*arrays)


def shards(dp, tensor, *args):
    x, starts, attn_gain, q_gain, k_gain, wq, wk, wv, wo, mlp_gain, wg, wu, wd, ct = args
    outs, turned = call(
        dp, tensor, x[0], starts, attn_gain[None], q_gain[None], k_gain[None], mlp_gain[None],
        wq, wk, wv, wo, wg, wu, wd, ct[0],
    )
    outs = list(copied(outs))
    for i in (0, 1):
        outs[i] = outs[i][None]
    for i in (2, 3, 4, 9):
        outs[i] = outs[i][0]
    if not turned:
        for i in (8, 12):
            outs[i] = outs[i].T
    return tuple(outs)


def solution(mesh):
    sequence, square, turned = P("dp", "tensor", None), P("dp", "tensor"), P("tensor", "dp")
    gain = P("dp")
    in_specs = (
        sequence, P("dp", None), gain, gain, gain, square, square, square, turned, gain, square, square,
        turned, sequence,
    )
    out_specs = (
        sequence, sequence, gain, gain, gain, square, square, square, turned, gain, square, square,
        turned,
    )
    return jax.shard_map(
        functools.partial(shards, mesh.shape["dp"], mesh.shape["tensor"]),
        mesh=mesh,
        in_specs=in_specs,
        out_specs=out_specs,
        check_vma=False,
    )
```

```python
import functools
import math
import types

import jax
import jax.numpy as jnp
import numpy as np
from jax import lax
from jax.experimental import pallas as pl
from jax.experimental.pallas import tpu as pltpu
from jax.sharding import PartitionSpec as P

HEAD = 128
PIECE = 256
EPS = 1e-06
THETA = 1000000.0
SCALE = HEAD**-0.5
LOG2E = math.log2(math.e)
MESH = pl.DeviceIdType.MESH
F32 = jnp.float32
BF16 = jnp.bfloat16
VMEM_LIMIT = 62 * 2**20


def nt(x, y):
    return lax.dot_general(x, y, (((1,), (1,)), ((), ())), preferred_element_type=F32)


def nn(x, y):
    return lax.dot_general(x, y, (((1,), (0,)), ((), ())), preferred_element_type=F32)


def tn(x, y):
    return lax.dot_general(x, y, (((0,), (0,)), ((), ())), preferred_element_type=F32)


def start(copy):
    copy.start()


def wait(copy):
    copy.wait()


def wait_send(copy):
    copy.wait_send()


def by_rows(rows, act, step=64):
    def body(i, _):
        act(pl.ds(pl.multiple_of(i * step, step), step))
        return 0

    lax.fori_loop(0, rows // step, body, 0)


class Place:
    def __init__(self, dp, tensor):
        self.dp, self.tensor, self.columns = dp, tensor, dp // 2
        self.d = lax.axis_index("dp")
        self.t = lax.axis_index("tensor")
        self.col, self.c = lax.div(self.d, 2), lax.rem(self.d, 2)
        self.a, self.b = lax.div(self.t, 2), lax.rem(self.t, 2)
        self.sibling = self.d + 1 - 2 * self.c
        self.near = self.t + 1 - 2 * self.b
        self.far = self.t + 2 - 4 * self.a

    def barrier(self):
        semaphore = pltpu.get_barrier_semaphore()
        for k in range(1, self.dp):
            pl.semaphore_signal(
                semaphore, 1, device_id=(lax.rem(self.d + k, self.dp), self.t), device_id_type=MESH
            )
        for k in range(1, self.tensor):
            pl.semaphore_signal(
                semaphore,
                1,
                device_id=(self.d, lax.rem(self.t + k, self.tensor)),
                device_id_type=MESH,
            )
        pl.semaphore_wait(semaphore, self.dp + self.tensor - 2)

    def plane(self, bits_a, bits_b):
        first = self.a + bits_a - 2 * self.a * bits_a
        second = self.b + bits_b - 2 * self.b * bits_b
        return 2 * first + second


def remote(source, target, send, receive, device):
    return pltpu.make_async_remote_copy(
        src_ref=source,
        dst_ref=target,
        send_sem=send,
        recv_sem=receive,
        device_id=device,
        device_id_type=MESH,
    )


class Spread:
    def __init__(self, place, shard, stage, whole, send, receive, cross):
        self.p, self.shard, self.stage, self.whole = place, shard, stage, whole
        self.send, self.receive, self.cross = send, receive, cross
        self.rows = shard.shape[0]
        self.square = place.columns == 4
        y, x = lax.div(place.col, 2), lax.rem(place.col, 2)
        if self.square:
            self.side = [2 * y + 1 - x, 2 * (1 - y) + x]
            self.corner = 2 * (1 - y) + 1 - x

    def slot(self, index, half=None):
        size = self.rows if half is None else self.rows // 2
        begin = index * self.rows + (0 if half is None else half * size)
        return self.whole.at[pl.ds(pl.multiple_of(begin, size), size)]

    def crossing(self):
        p = self.p
        return remote(self.shard, self.stage, self.cross.at[0], self.cross.at[1], (p.d, p.far))

    def each(self, phase, act_remote, act_local):
        p = self.p
        source = self.shard if phase == 0 else self.stage
        core = p.a if phase == 0 else 1 - p.a
        columns = (
            [p.col] + self.side
            if self.square
            else [lax.rem(p.col + j, p.columns) for j in range(p.columns)]
        )
        for j, column in enumerate(columns):
            send = self.send.at[phase, j]

            def to_other():
                act_remote(
                    remote(
                        source,
                        self.slot(p.d),
                        send,
                        self.receive.at[p.d, 0],
                        (2 * column + core, p.t),
                    )
                )

            def to_self():
                act_local(pltpu.make_async_copy(source, self.slot(p.d), send))

            if j == 0 and act_local:
                pl.when(core == p.c)(to_self)
            if act_remote:
                if j:
                    to_other()
                else:
                    pl.when(core != p.c)(to_other)

    def start(self, phase):
        self.each(phase, start, start)

    def cross_start(self):
        self.crossing().start()

    def cross_wait(self):
        self.crossing().wait_recv()

    def landed(self, index, half):
        p = self.p
        part = self.slot(index, half)
        remote(
            part, part, self.send.at[0, 0], self.receive.at[index, half or 0], (p.d, p.t)
        ).wait_recv()

    def forwards(self, act):
        p = self.p
        for direction in range(2):
            for core in range(2):
                index = 2 * self.side[direction] + core
                part = self.slot(index, direction)
                act(
                    remote(
                        part,
                        part,
                        self.send.at[2 + direction, core],
                        self.receive.at[index, direction],
                        (2 * self.side[1 - direction] + p.c, p.t),
                    )
                )

    def forward(self):
        if self.square:
            for direction in range(2):
                for core in range(2):
                    self.landed(2 * self.side[direction] + core, None)
            self.forwards(start)

    def wait_whole(self):
        p = self.p
        self.each(0, None, wait)
        self.each(1, None, wait)
        if self.square:
            self.landed(p.sibling, None)
            for core in range(2):
                for half in range(2):
                    self.landed(2 * self.corner + core, half)
        else:
            for k in range(1, p.dp):
                self.landed(lax.rem(p.d + k, p.dp), None)

    def cross_sent(self):
        self.crossing().wait_send()

    def wait_sends(self):
        self.each(0, wait_send, None)
        self.each(1, wait_send, None)
        if self.square:
            self.forwards(wait_send)


def spread_semaphores(dp):
    return [
        pltpu.SemaphoreType.DMA((4, max(dp // 2, 4))),
        pltpu.SemaphoreType.DMA((dp, 2)),
        pltpu.SemaphoreType.DMA((2,)),
    ]


class Fan:
    PIECES = 4

    def __init__(self, place, block, whole, send, receive, onward):
        self.p, self.block, self.whole = place, block, whole
        self.send, self.receive, self.onward = send, receive, onward
        self.slots = [place.plane(k // 2, k % 2) for k in range(4)]
        self.rows = block.shape[0] // self.PIECES

    def first_hop(self, act, pieces):
        p = self.p
        plane = lax.select(p.a == p.c, p.near, p.c + 1)
        for piece in pieces:
            at = pl.ds(piece * self.rows, self.rows)
            act(
                remote(
                    self.block.at[at],
                    self.whole.at[p.t, at],
                    self.send.at[piece],
                    self.receive.at[p.t, piece],
                    (p.d, plane),
                )
            )

    def start(self, piece=None):
        p = self.p
        pieces = range(self.PIECES) if piece is None else [piece]
        self.first_hop(start, pieces)

        @pl.when(p.a == p.c)
        def _():
            for piece in pieces:
                at = pl.ds(piece * self.rows, self.rows)
                self.whole[p.t, at] = self.block[at]

    def hop(self, index, piece, device, row):
        part = self.whole.at[self.slots[index], pl.ds(piece * self.rows, self.rows)]
        return remote(
            part,
            part,
            self.onward.at[row, index, piece],
            self.receive.at[self.slots[index], piece],
            device,
        )

    def to_sibling(self, index, piece):
        return self.hop(index, piece, (self.p.sibling, self.p.t), 0)

    def to_near(self, index, piece):
        return self.hop(index, piece, (self.p.d, self.p.near), 1)

    def take(self, *indices):
        p = self.p
        for piece in range(self.PIECES):
            for index in indices:

                def arrived():
                    self.to_sibling(index, piece).wait_recv()

                if index == 0:
                    pl.when(p.a != p.c)(arrived)
                else:
                    arrived()

                @pl.when(p.a == p.c)
                def _():
                    if index >= 2:
                        pl.when(p.t == p.c + 1)(lambda: self.to_near(index, piece).start())
                    self.to_sibling(index, piece).start()

    def finish(self):
        p = self.p
        self.first_hop(wait_send, range(self.PIECES))

        @pl.when(p.a == p.c)
        def _():
            for index in range(4):
                for piece in range(self.PIECES):
                    self.to_sibling(index, piece).wait_send()
                    if index >= 2:
                        pl.when(p.t == p.c + 1)(lambda: self.to_near(index, piece).wait_send())


FAN_SEMAPHORES = [
    pltpu.SemaphoreType.DMA((Fan.PIECES,)),
    pltpu.SemaphoreType.DMA((4, Fan.PIECES)),
    pltpu.SemaphoreType.DMA((2, 4, Fan.PIECES)),
]


def gains_rows(total):
    one = jnp.concatenate([total[i : i + 1] for i in range(8)], axis=1)
    two = jnp.concatenate([total[i : i + 1] for i in range(8, 16)], axis=1)
    return one, two, total[16:17], total[17:18]


def unit_of(values):
    scale = lax.rsqrt(jnp.mean(values * values, axis=-1, keepdims=True) + EPS)
    return values * scale, scale


class Home:
    PIECES = 4

    def __init__(self, place, kept, given, taken, summed, landed, passed, semaphores):
        self.p = place
        self.kept, self.given, self.taken, self.summed, self.landed = kept, given, taken, summed, landed
        self.passed = passed
        self.given_send, self.taken_receive, self.summed_send, self.landed_receive, self.passing = (
            semaphores
        )
        self.rows = landed.shape[1] // self.PIECES
        self.gate = place.t == place.a + 1

    def block(self, k):
        k = 3 - k
        return self.p.plane(k // 2, k % 2)

    def mine(self, k):
        return self.p.c == (self.p.b if k % 2 else 1 - self.p.b)

    def give(self, slot):
        return remote(
            self.given.at[slot],
            self.taken.at[slot],
            self.given_send.at[slot],
            self.taken_receive.at[slot],
            (self.p.sibling, self.p.t),
        )

    def at(self, piece):
        return pl.ds(piece * self.rows, self.rows)

    def send(self, k, piece):
        p = self.p
        return remote(
            self.summed.at[k // 2, self.at(piece)],
            self.landed.at[p.b, self.at(piece)],
            self.summed_send.at[k // 2, piece],
            self.landed_receive.at[p.b, piece],
            (2 * p.col + p.a, self.block(k)),
        )

    def to_gate(self, piece):
        p = self.p
        return remote(
            self.summed.at[0, self.at(piece)],
            self.passed.at[self.at(piece)],
            self.passing.at[0, piece],
            self.passing.at[1, piece],
            (p.d, p.near),
        )

    def add(self, k, parts):
        @pl.when(self.mine(k))
        def _():
            for i, part in enumerate(parts):
                self.kept[k // 2, :, i * 256 : (i + 1) * 256] = part()

        @pl.when(jnp.logical_not(self.mine(k)))
        def _():
            for i, part in enumerate(parts):
                self.given[k // 2, :, i * 256 : (i + 1) * 256] = part().astype(BF16)
            self.give(k // 2).start()

    def total(self, k, piece):
        at = self.at(piece)
        return self.kept[k // 2, at] + self.taken[k // 2, at].astype(F32)

    def settle_outer(self, k):
        @pl.when(jnp.logical_and(self.mine(k), jnp.logical_not(self.gate)))
        def _():
            self.give(0).wait_recv()
            for piece in range(self.PIECES):
                self.summed[0, self.at(piece)] = self.total(k, piece).astype(BF16)
                self.to_gate(piece).start()

    def settle_gate(self, k):
        @pl.when(jnp.logical_and(self.mine(k), self.gate))
        def _():
            self.give(0).wait_recv()
            for piece in range(self.PIECES):
                at = self.at(piece)
                self.to_gate(piece).wait_recv()
                self.summed[0, at] = (
                    self.total(k, piece) + self.passed[at].astype(F32)
                ).astype(BF16)
                self.send(k, piece).start()

    def settle(self, k):
        p = self.p

        @pl.when(self.mine(k))
        def _():
            self.give(1).wait_recv()
            stays = jnp.logical_and(p.a == p.c, jnp.asarray(k == 3))

            @pl.when(stays)
            def _():
                for piece in range(self.PIECES):
                    self.landed[p.b, self.at(piece)] = self.total(k, piece).astype(BF16)

            @pl.when(jnp.logical_not(stays))
            def _():
                for piece in range(self.PIECES):
                    self.summed[1, self.at(piece)] = self.total(k, piece).astype(BF16)
                    self.send(k, piece).start()

    def arrive(self):
        p = self.p

        def arrived(slot):
            for piece in range(self.PIECES):
                part = self.landed.at[slot, self.at(piece)]
                remote(
                    part,
                    part,
                    self.summed_send.at[0, piece],
                    self.landed_receive.at[slot, piece],
                    (p.d, p.t),
                ).wait_recv()

        @pl.when(p.a == p.c)
        def _():
            arrived(1 - p.b)
            pl.when(p.c != p.b)(lambda: arrived(p.b))

        @pl.when(p.a != p.c)
        def _():
            self.landed[p.c] = jnp.zeros(self.landed.shape[1:], BF16)
            arrived(1 - p.c)

    def value(self, at):
        return self.landed[0, at].astype(F32) + self.landed[1, at].astype(F32)

    def finish(self):
        for k in range(4):

            @pl.when(jnp.logical_not(self.mine(k)))
            def _():
                self.give(k // 2).wait_send()

            sent = self.mine(k)
            if k == 3:
                sent = jnp.logical_and(sent, self.p.a != self.p.c)
            if k < 2:
                sent = jnp.logical_and(sent, self.gate)

                @pl.when(jnp.logical_and(self.mine(k), jnp.logical_not(self.gate)))
                def _():
                    for piece in range(self.PIECES):
                        self.to_gate(piece).wait_send()

            @pl.when(sent)
            def _():
                for piece in range(self.PIECES):
                    self.send(k, piece).wait_send()


HOME_SEMAPHORES = [
    pltpu.SemaphoreType.DMA((2,)),
    pltpu.SemaphoreType.DMA((2,)),
    *[pltpu.SemaphoreType.DMA((2, Home.PIECES))] * 3,
]


class Quad:
    def __init__(self, place, block, whole, send, receive):
        self.p, self.whole_block, self.whole, self.sent, self.receive = place, block, whole, send, receive
        b, c = place.b, place.c
        self.slots = [2 * b + c, 2 * b + 1 - c, 2 * (1 - b) + c, 2 * (1 - b) + 1 - c]

    def copy(self, index, source, slot, device):
        return remote(
            source, self.whole.at[slot], self.sent.at[index], self.receive.at[slot], device
        )

    def near(self):
        p = self.p
        return self.copy(0, self.whole_block, self.slots[0], (p.d, p.near))

    def beside(self):
        p = self.p
        return self.copy(1, self.whole_block, self.slots[0], (p.sibling, p.t))

    def onward(self):
        p = self.p
        return self.copy(2, self.whole.at[self.slots[2]], self.slots[2], (p.sibling, p.t))

    def start(self):
        self.near().start()
        self.beside().start()
        self.whole[self.slots[0]] = self.whole_block[...]

    def take(self, index):
        slot = self.slots[index]
        self.copy(0, self.whole_block, slot, (self.p.d, self.p.near)).wait_recv()
        if index == 2:
            self.onward().start()

    def finish(self):
        self.near().wait_send()
        self.beside().wait_send()
        self.onward().wait_send()


QUAD_SEMAPHORES = [pltpu.SemaphoreType.DMA((3,)), pltpu.SemaphoreType.DMA((4,))]


class PairSum:
    def __init__(self, place, kept, given, taken, summed, landed, given_send, taken_receive, across):
        self.p = place
        self.kept, self.given, self.taken, self.summed, self.landed = kept, given, taken, summed, landed
        self.given_send, self.taken_receive, self.across = given_send, taken_receive, across

    def give(self, half):
        return remote(
            self.given.at[half],
            self.taken.at[half],
            self.given_send.at[half],
            self.taken_receive.at[half],
            (self.p.sibling, self.p.t),
        )

    PIECES = 4

    def at(self, piece):
        size = self.summed.shape[0] // self.PIECES
        return pl.ds(piece * size, size)

    def send(self, piece):
        p = self.p
        return remote(
            self.summed.at[self.at(piece)],
            self.landed.at[self.at(piece)],
            self.across.at[0, piece],
            self.across.at[1, piece],
            (p.d, p.near),
        )

    def add_far(self, send):
        self.give(1).wait_recv()
        for piece in range(self.PIECES):
            at = self.at(piece)
            self.summed[at] = (self.kept[1, at] + self.taken[1, at].astype(F32)).astype(BF16)
            if send:
                self.send(piece).start()

    def take_own(self):
        self.give(0).wait_recv()

    def own(self, at):
        return self.kept[0, at] + self.taken[0, at].astype(F32)

    def finish(self):
        self.give(0).wait_send()
        self.give(1).wait_send()


PAIR_SEMAPHORES = [
    pltpu.SemaphoreType.DMA((2,)),
    pltpu.SemaphoreType.DMA((2,)),
    pltpu.SemaphoreType.DMA((2, PairSum.PIECES)),
]


class Collect:
    def __init__(self, place, source, slots, summed, landed, send, receive, across):
        self.p, self.source, self.slots, self.summed, self.landed = place, source, slots, summed, landed
        self.send, self.receive, self.across = send, receive, across
        self.rows = slots.shape[1]

    def part(self, index):
        return self.source.at[pl.ds(pl.multiple_of(index * self.rows, self.rows), self.rows)]

    def own(self):
        p = self.p
        return pltpu.make_async_copy(self.part(p.d), self.slots.at[p.d], self.send.at[p.d])

    def other(self, target):
        p = self.p
        return remote(
            self.part(target),
            self.slots.at[p.d],
            self.send.at[target],
            self.receive.at[p.d],
            (target, p.t),
        )

    def start(self, chunk, size):
        count = size // self.rows

        def body(i, _):
            target = chunk * count + i
            pl.when(target == self.p.d)(lambda: self.own().start())
            pl.when(target != self.p.d)(lambda: self.other(target).start())
            return 0

        lax.fori_loop(0, count, body, 0)

    def cross(self):
        p = self.p
        return remote(self.summed, self.landed, self.across.at[0], self.across.at[1], (p.d, p.far))

    def total(self, core, here):
        return lax.fori_loop(
            1,
            self.p.columns,
            lambda i, s: s + self.slots[2 * i + core, :, here].astype(F32),
            self.slots[core, :, here].astype(F32),
        )

    def relay(self):
        p = self.p
        self.own().wait()
        for k in range(1, p.dp):
            source = lax.rem(p.d + k, p.dp)
            remote(
                self.part(source),
                self.slots.at[source],
                self.send.at[source],
                self.receive.at[source],
                (p.d, p.t),
            ).wait_recv()
        for begin in range(0, self.summed.shape[1], 256):
            here = slice(begin, begin + 256)
            self.summed[:, here] = self.total(1 - p.a, here).astype(BF16)
        self.cross().start()

    def result(self, targets):
        self.cross().wait_recv()
        begin = 0
        for target, first, count, turned in targets:
            for offset in range(0, count, min(count, 256)):
                size = min(count, 256)
                here = slice(begin, begin + size)
                there = slice(first + offset, first + offset + size)
                value = self.total(self.p.a, here) + self.landed[:, here].astype(F32)
                if turned:
                    target[there] = value.T
                else:
                    target[:, there] = value
                begin += size

    def finish(self):
        p = self.p
        for k in range(1, p.dp):
            self.other(lax.rem(p.d + k, p.dp)).wait_send()
        self.cross().wait_send()


def collect_semaphores(dp):
    return [
        pltpu.SemaphoreType.DMA((dp,)),
        pltpu.SemaphoreType.DMA((dp,)),
        pltpu.SemaphoreType.DMA((2,)),
    ]


def vmem(count):
    return [pl.BlockSpec(memory_space=pltpu.VMEM)] * count


def params(identity):
    return pltpu.CompilerParams(
        collective_id=identity, has_side_effects=True, vmem_limit_bytes=VMEM_LIMIT
    )


def rotary(tokens):
    frequency = np.float32(THETA) ** (
        -(np.arange(HEAD // 2, dtype=np.float32) * np.float32(2.0)) / np.float32(HEAD)
    )
    angles = np.arange(tokens, dtype=np.float32)[:, None] * frequency.astype(np.float32)[None, :]
    return np.concatenate([np.cos(angles), np.sin(angles)], axis=1).astype(np.float32)


def rotary_rows(table):
    other = pltpu.roll(table, HEAD // 2, 1)
    low = lax.broadcasted_iota(jnp.int32, (1, HEAD), 1) < HEAD // 2
    return jnp.where(low, table, other), jnp.where(low, -other, table)


def allowed_mask(place, gains, base, rows, keys, transposed):
    lane = lax.broadcasted_iota(jnp.int32, (1, 128), 1)
    chosen = (lane == 2 * place.col + place.a).astype(F32)
    shape = (keys, rows) if transposed else (rows, keys)
    query_dim, key_dim = (1, 0) if transposed else (0, 1)
    line = lambda dim: tuple(n if i == dim else 1 for i, n in enumerate(shape))
    query = lax.broadcasted_iota(jnp.int32, shape, query_dim)
    key = lax.broadcasted_iota(jnp.int32, shape, key_dim)
    mask = (key <= query).astype(F32)
    for piece in range(2):
        numbers = gains[18 + piece : 19 + piece]
        first_position = jnp.sum(numbers * chosen, axis=1, keepdims=True) - base.astype(F32)

        def inside(position):
            position = position.astype(F32)
            return jnp.logical_and(
                position >= first_position, position < first_position + PIECE
            ).astype(F32)

        in_query = inside(lax.broadcasted_iota(jnp.int32, line(query_dim), query_dim))
        in_key = inside(lax.broadcasted_iota(jnp.int32, line(key_dim), key_dim))
        mask = jnp.maximum(mask, in_query * in_key)
    return mask


def placed(place, values, base):
    size = values.shape[1]
    begin = place.d * size
    if size < 128:
        values = jnp.concatenate([values, jnp.zeros((1, 128 - size), F32)], axis=1)
        values = pltpu.roll(values, lax.rem(begin, 128), 1)
    row = lax.broadcasted_iota(jnp.int32, (24, 128), 0)
    return jnp.where(row == base + lax.div(begin, 128), values, 0.0)


def share(place, tile, base, size):
    begin = place.d * size
    row = lax.broadcasted_iota(jnp.int32, (24, 128), 0)
    chosen = jnp.where(row == base + lax.div(begin, 128), tile, 0.0)
    values = jnp.sum(chosen, axis=0, keepdims=True)
    if size < 128:
        values = pltpu.roll(values, lax.rem(128 - lax.rem(begin, 128), 128), 1)
    return values[:, :size]


class Exchange:
    def __init__(self, place, tile, slots, send, receive, in_plane):
        self.p, self.tile, self.slots, self.in_plane = place, tile, slots, in_plane
        self.sent, self.receive = send, receive
        self.count = place.dp if in_plane else place.tensor
        self.me = place.d if in_plane else place.t

    def copy(self, k, slot):
        p = self.p
        other = lax.rem(self.me + k, self.count)
        device = (other, p.t) if self.in_plane else (p.d, other)
        return remote(
            self.tile, self.slots.at[slot], self.sent.at[k], self.receive.at[slot], device
        )

    def start(self):
        for k in range(1, self.count):
            self.copy(k, self.me).start()
        self.slots[self.me] = self.tile[...]

    def total(self):
        for k in range(1, self.count):
            self.copy(k, lax.rem(self.me + k, self.count)).wait_recv()
        return lax.fori_loop(1, self.count, lambda i, s: s + self.slots[i], self.slots[0])

    def finish(self):
        for k in range(1, self.count):
            self.copy(k, self.me).wait_send()


def exchange_semaphores(count):
    return [pltpu.SemaphoreType.DMA((count,)), pltpu.SemaphoreType.DMA((count,))]


def layer(dp, tensor, turned, names, *refs):
    r = types.SimpleNamespace(**dict(zip(names, refs)))
    rest = list(refs[len(names) :])

    def take(count):
        head, rest[:] = rest[:count], rest[count:]
        return head

    p = Place(dp, tensor)
    gains_out = Exchange(p, r.pack, r.gain_slots, *take(2), True)
    gains_plane = Exchange(p, r.gain_pack, r.plane_slots, *take(2), True)
    gains_tensor = Exchange(p, r.plane_sum, r.tensor_slots, *take(2), False)
    fan = Fan(p, r.x, r.tokens, *take(3))
    fan_back = Fan(p, r.block, r.tokens, *take(3))
    spread_a = Spread(p, r.wa, r.wa_stage, r.wa_whole, *take(3))
    spread_o = Spread(p, r.wo_shard, r.wo_stage, r.wo_whole, *take(3))
    units = r.wg.shape[1]
    thirds = [slice(i * units, (i + 1) * units) for i in range(3)]
    spread_m = [
        Spread(p, r.wm.at[:, c], r.wm_stage.at[:, c], r.wm_whole.at[:, c], *take(3)) for c in thirds
    ]
    quad_ct = Quad(p, r.ct, r.ct_whole, *take(2))
    quad = Quad(p, r.block, r.normed_two, *take(2))
    home_buffers = (r.kept, r.given, r.taken, r.summed, r.landed, r.passed)
    home = Home(p, *home_buffers, take(5))
    home_back = Home(p, *home_buffers, take(5))
    down_semaphores, back_semaphores = take(3), take(3)
    collect_m = [
        Collect(
            p, r.wm_whole.at[:, c], r.cm_slots.at[:, :, c], r.wm.at[:, c], r.cm_landed.at[:, c], *take(3)
        )
        for c in thirds
    ]
    collect_o = Collect(p, r.wo_whole, r.co_slots, r.wo_shard, r.co_landed, *take(3))
    rows, width = r.x.shape
    nq, nk = r.wq.shape[1], r.wk.shape[1]
    heads, kv_heads, blocks = nq // HEAD, nk // HEAD, 4
    repeat = heads // kv_heads
    wide = (repeat + 2) * HEAD
    of_group = [slice(g * wide, (g + 1) * wide) for g in range(kv_heads)]
    collect_a_semaphores = [take(3) for _ in of_group]

    tile = jnp.zeros((24, 128), F32)
    for base, ref in ((0, r.gain_one), (8, r.gain_two), (16, r.q_gain), (17, r.k_gain)):
        tile = tile + placed(p, ref[...].astype(F32), base)
    row = lax.broadcasted_iota(jnp.int32, (24, 128), 0)
    lane = lax.broadcasted_iota(jnp.int32, (24, 128), 1)
    for piece in range(2):
        here = jnp.logical_and(row == 18 + piece, lane == p.d)
        tile = tile + jnp.where(here, r.starts[0, piece], 0).astype(F32)
    r.pack[...] = tile
    for g in range(kv_heads):
        begin = g * wide
        for ref, size in ((r.wq, repeat * HEAD), (r.wk, HEAD), (r.wv, HEAD)):
            r.wa[:, begin : begin + size] = ref[:, g * size : (g + 1) * size]
            begin += size
    p.barrier()
    gains_out.start()
    spread_a.cross_start()
    pl.when(p.a == p.c)(fan.start)
    spread_a.start(0)

    def turn(target, source, begin):
        if source.shape[0] == target.shape[0]:
            target[:, begin : begin + source.shape[1]] = source[...]
        else:
            for i in range(0, source.shape[0], 128):
                target[:, begin + i : begin + i + 128] = source[i : i + 128].T

    turn(r.wo_shard, r.wo, 0)
    r.wm[:, :units] = r.wg[...]
    r.wm[:, units : 2 * units] = r.wu[...]
    turn(r.wm, r.wd, 2 * units)
    total = gains_out.total()
    r.gains[...] = total
    gain_one, gain_two, q_gain, k_gain = gains_rows(total)
    def normalize(slot):
        def act(at):
            unit, _ = unit_of(r.tokens[slot, at].astype(F32))
            r.normed[slot, at] = (unit * gain_one).astype(BF16)

        by_rows(rows, act)

    fan.take(0)
    spread_a.cross_sent()
    pl.when(p.a != p.c)(fan.start)
    spread_a.cross_wait()
    spread_a.start(1)
    spread_o.start(0)
    fan.take(1)
    spread_a.forward()
    normalize(fan.slots[0])
    normalize(fan.slots[1])
    fan.take(2, 3)
    spread_o.cross_start()
    quad_ct.start()
    for part in spread_m:
        part.start(0)
    normalize(fan.slots[2])
    normalize(fan.slots[3])
    spread_a.wait_whole()
    fan.finish()
    spread_a.wait_sends()

    def attention(v_wide, mask):
        v_wide[:, :, HEAD:] = jnp.ones((kv_heads, rows * 4, HEAD), BF16)

        def qkv(slot, _):
            at = pl.ds(pl.multiple_of(slot * rows, rows), rows)
            cosine, sine = rotary_rows(r.rotary[slot])

            def rotated(values, gain):
                unit_values, _ = unit_of(values)
                scaled = unit_values * gain
                return (scaled * cosine + pltpu.roll(scaled, 64, 1) * sine).astype(BF16)

            for g in range(kv_heads):
                for i in range(0, repeat + 2, 2):
                    begin = g * wide + i * HEAD
                    product = nn(r.normed[slot], r.wa_whole[:, begin : begin + 2 * HEAD])
                    for j in range(2):
                        values = product[:, j * HEAD : (j + 1) * HEAD]
                        if i + j < repeat:
                            r.q_pre[g * repeat + i + j, at] = values
                            r.q[g * repeat + i + j, at] = rotated(values, q_gain)
                        elif i + j == repeat:
                            r.k_pre[g, at] = values
                            r.k[g, at] = rotated(values, k_gain)
                        else:
                            v_wide[g, at, :HEAD] = values.astype(BF16)
            return 0

        lax.fori_loop(0, 4, qkv, 0)

        def attend(k):
            block = home.block(k)
            mask[...] = allowed_mask(p, r.gains[...], block * rows, rows, 2 * rows, False)
            for number in range(blocks):

                @pl.when(block == number)
                def _():
                    at = slice(number * rows, (number + 1) * rows)

                    def group(g, _):
                        queries = r.q[pl.ds(g * repeat, repeat), at].reshape(repeat * rows, HEAD)
                        total = jnp.zeros((repeat * rows, 2 * HEAD), F32)
                        for kb in range(min(number + 2, blocks)):
                            keys = slice(kb * rows, (kb + 1) * rows)
                            weight = jnp.exp2(nt(queries, r.k[g, keys]) * (SCALE * LOG2E))
                            if kb >= number:
                                part = mask[:, (kb - number) * rows : (kb - number + 1) * rows]
                                weight = weight * jnp.concatenate([part] * repeat, axis=0)
                            total = total + nn(weight.astype(BF16), v_wide[g, keys])
                        summed = total[:, HEAD:]
                        result = (total[:, :HEAD] / summed).astype(BF16)
                        result = jnp.concatenate(
                            [result[i * rows : (i + 1) * rows] for i in range(repeat)], axis=1
                        )
                        size = repeat * HEAD
                        r.mixed[at, pl.ds(pl.multiple_of(g * size, size), size)] = result
                        logs = jnp.log2(summed)
                        for i in range(repeat):
                            across = logs[i * rows : (i + 1) * rows].T
                            r.lse[g * repeat + i, :, at] = across[0:1]
                        return 0

                    lax.fori_loop(0, kv_heads, group, 0)

        def project(k):
            at = pl.ds(pl.multiple_of(home.block(k) * rows, rows), rows)

            def part(i):
                return lambda: nt(r.mixed[at], r.wo_whole[i * 256 : (i + 1) * 256])

            home.add(k, [part(i) for i in range(width // 256)])

        spread_o.cross_wait()
        spread_o.start(1)
        spread_m[0].cross_start()
        attend(0)
        attend(1)
        spread_m[1].cross_start()
        spread_o.forward()
        spread_o.wait_whole()
        project(0)
        project(1)
        home.settle_outer(0)
        home.settle_outer(1)
        attend(2)
        project(2)
        spread_m[0].cross_wait()
        spread_m[0].start(1)
        spread_m[2].cross_start()
        attend(3)
        project(3)
        home.settle_gate(0)
        home.settle_gate(1)
        home.settle(2)
        home.settle(3)
        r.v[...] = v_wide[:, :, :HEAD]

    pl.run_scoped(
        attention,
        pltpu.VMEM((kv_heads, 4 * rows, 2 * HEAD), BF16),
        pltpu.VMEM((rows, 2 * rows), F32),
    )
    spread_m[0].forward()
    spread_m[1].cross_wait()
    spread_m[1].start(1)
    quad_ct.take(1)
    quad_ct.take(2)
    home.arrive()

    def norm_two(at):
        hidden = r.x[at].astype(F32) + home.value(at)
        r.kept[0, at] = hidden
        unit, _ = unit_of(hidden)
        r.block[at] = (unit * gain_two).astype(BF16)

    by_rows(rows, norm_two)
    quad.start()
    spread_m[2].cross_wait()
    spread_m[2].start(1)
    spread_m[1].forward()
    quad_ct.take(3)
    quad.take(1)
    quad.take(2)
    quad.take(3)
    spread_m[2].forward()
    quad.finish()
    home.finish()
    spread_o.cross_sent()
    spread_o.wait_sends()
    for part in spread_m:
        part.wait_whole()
    for part in spread_m:
        part.cross_sent()
        part.wait_sends()

    def feed_forward(active, grad_gate, grad_up, down_kept, back_kept):
        down = PairSum(
            p, down_kept, r.given, r.taken, r.summed.at[0], r.down_landed, *down_semaphores
        )
        back = PairSum(
            p, back_kept, r.back_given, r.back_taken, r.back_summed, r.back_landed, *back_semaphores
        )
        wm = r.wm_whole

        def work(slot, keep, half):
            tokens, cotangent = r.normed_two[slot], r.ct_whole[slot]
            at = pl.ds(pl.multiple_of(slot * rows, rows), rows)
            for i in range(units // 256):
                here = slice(i * 256, (i + 1) * 256)
                gate = nn(tokens, wm[:, i * 256 : (i + 1) * 256])
                upward = nn(tokens, wm[:, units + i * 256 : units + (i + 1) * 256])
                grad = nn(cotangent, wm[:, 2 * units + i * 256 : 2 * units + (i + 1) * 256])
                sigmoid = 1.0 / (1.0 + jnp.exp2(gate * -LOG2E))
                silu = gate * sigmoid
                active[at, here] = (silu * upward).astype(BF16)
                grad_gate[at, here] = (
                    grad * upward * sigmoid * (1.0 + gate * (1.0 - sigmoid))
                ).astype(BF16)
                grad_up[at, here] = (grad * silu).astype(BF16)
            for i in range(width // 256):
                here = slice(i * 256, (i + 1) * 256)
                out = nt(grad_gate[at], wm[here, :units]) + nt(
                    grad_up[at], wm[here, units : 2 * units]
                )
                if keep:
                    back.kept[half, :, here] = out
                else:
                    back.given[half, :, here] = out.astype(BF16)
            if not keep:
                back.give(half).start()
            for i in range(width // 256):
                here = slice(i * 256, (i + 1) * 256)
                out = nt(active[at], wm[here, 2 * units :])
                if keep:
                    down.kept[half, :, here] = out
                else:
                    down.given[half, :, here] = out.astype(BF16)
            if not keep:
                down.give(half).start()

        def both(step, _):
            half = 1 - step
            other = lax.select(half == 1, 1 - p.b, p.b)
            work(2 * other + p.c, True, half)
            work(2 * other + 1 - p.c, False, half)

            @pl.when(half == 1)
            def _():
                back.add_far(True)

            return 0

        lax.fori_loop(0, 2, both, 0)

        def weight_grads(third, tokens_ref, grad):
            def body(i, _):
                chunk = lax.rem(i + 1 + p.col, width // 256)
                at = pl.ds(pl.multiple_of(chunk * 256, 256), 256)
                tokens = tokens_ref[:, :, at].reshape(4 * rows, 256)
                wm[at, thirds[third]] = tn(tokens, grad[...]).astype(BF16)
                collect_m[third].start(chunk, 256)
                return 0

            lax.fori_loop(0, width // 256, body, 0)

        weight_grads(0, r.normed_two, grad_gate)
        down.add_far(False)
        down.take_own()
        back.take_own()
        gain = gains_rows(r.gains[...])[1]
        r.gain_rows[...] = jnp.zeros_like(r.gain_rows)

        def norm_two_back(at):
            grad_normed = back.own(at) + back.landed[at].astype(F32)
            unit, scale = unit_of(r.kept[0, at])
            r.gain_rows[...] += jnp.sum(grad_normed * unit, axis=0, keepdims=True)
            scaled = grad_normed * gain
            mean = jnp.mean(scaled * unit, axis=-1, keepdims=True)
            grad = r.ct[at].astype(F32) + scale * (scaled - unit * mean)
            r.input_grad[at] = grad
            r.block[at] = grad.astype(BF16)

        for piece in range(back.PIECES):
            back.send(piece).wait_recv()
            norm_two_back(back.at(piece))
            fan_back.start(piece)
        fan_back.take(0)

        def hidden_sum(at):
            r.kept[0, at] += down.own(at)

        by_rows(rows, hidden_sum)
        weight_grads(1, r.normed_two, grad_up)
        fan_back.take(1)

        for i in range(8):
            r.gain_pack[8 + i : 9 + i] = r.gain_rows[:, i * 128 : (i + 1) * 128]
        fan_back.take(2, 3)
        weight_grads(2, r.ct_whole, active)
        collect_m[0].relay()
        for piece in range(back.PIECES):
            back.send(piece).wait_send()
        back.finish()
        down.finish()

    r.gain_pack[16:24] = jnp.zeros((8, 128), F32)
    pl.run_scoped(
        feed_forward,
        *[pltpu.VMEM((4 * rows, units), BF16)] * 3,
        *[pltpu.VMEM((2, rows, width), F32)] * 2,
    )

    def attention_back(grads, grad_mixed, delta, mask, grad_keys, grad_values, grad_wa):
        collect_a = [
            Collect(
                p, grad_wa.at[:, c], r.ca_slots.at[:, :, c], r.wa.at[:, c], r.ca_landed.at[:, c],
                *semaphores,
            )
            for c, semaphores in zip(of_group, collect_a_semaphores)
        ]
        down_sends = [
            remote(
                r.summed.at[0, at],
                r.down_landed.at[at],
                down_semaphores[2].at[0, i],
                down_semaphores[2].at[1, i],
                (p.d, p.near),
            )
            for i, at in enumerate(pl.ds(j * (rows // 4), rows // 4) for j in range(4))
        ]
        for number in range(blocks):
            base = jnp.int32(number * rows)
            mask[number] = allowed_mask(p, r.gains[...], base, rows, 2 * rows, True)
        for copy in down_sends:
            copy.start()

        def mixed_back(slot, _):
            at = pl.ds(pl.multiple_of(slot * rows, rows), rows)
            for i in range(heads * HEAD // 256):
                grad = nn(r.tokens[slot], r.wo_whole[:, i * 256 : (i + 1) * 256]).astype(BF16)
                for j in range(256 // HEAD):
                    head = i * (256 // HEAD) + j
                    one = grad[:, j * HEAD : (j + 1) * HEAD]
                    grad_mixed[head, at] = one
                    mixed = r.mixed[at, head * HEAD : (head + 1) * HEAD]
                    row = lax.dot_general(
                        jnp.ones((8, HEAD), F32),
                        one.astype(F32) * mixed.astype(F32),
                        (((1,), (1,)), ((), ())),
                        precision=lax.Precision.HIGHEST,
                        preferred_element_type=F32,
                    )
                    delta[head, :, at] = row[0:1]
            return 0

        lax.fori_loop(0, 4, mixed_back, 0)

        def out_grads(i, _):
            chunk = lax.rem(i + 1 + p.col, width // 256)
            at = pl.ds(pl.multiple_of(chunk * 256, 256), 256)
            tokens = r.tokens[:, :, at].reshape(4 * rows, 256)
            r.wo_whole[at] = tn(tokens, r.mixed[...]).astype(BF16)
            collect_o.start(chunk, 256)
            return 0

        lax.fori_loop(0, width // 256, out_grads, 0)
        collect_m[1].relay()
        _, _, q_gain, k_gain = gains_rows(r.gains[...])

        def head_norm_back(grad, before, gain, number, row):
            unit, scale = unit_of(before)
            cosine, sine = rotary_rows(r.rotary[number])
            back = grad * cosine - pltpu.roll(grad, 64, 1) * sine
            r.gain_pack[row : row + 1] += jnp.sum(back * unit, axis=0, keepdims=True)
            scaled = back * gain
            mean = jnp.mean(scaled * unit, axis=-1, keepdims=True)
            return (scale * (scaled - unit * mean)).astype(BF16)

        def group(g):
            grad_keys[...] = jnp.zeros_like(grad_keys)
            grad_values[...] = jnp.zeros_like(grad_values)

            for number in range(blocks):
                at = slice(number * rows, (number + 1) * rows)
                heads_here = range(g * repeat, (g + 1) * repeat)
                queries = r.q[g * repeat : (g + 1) * repeat, at].reshape(repeat * rows, HEAD)
                grad = grad_mixed[g * repeat : (g + 1) * repeat, at].reshape(repeat * rows, HEAD)
                logs = jnp.concatenate([r.lse[head, :, at] for head in heads_here], axis=1)
                sums = jnp.concatenate([delta[head, :, at] for head in heads_here], axis=1)
                grad_queries = jnp.zeros((repeat * rows, HEAD), F32)
                for kb in range(min(number + 2, blocks)):
                    here = slice(kb * rows, (kb + 1) * rows)
                    keys = r.k[g, here]
                    probs = jnp.exp2(nt(keys, queries) * (SCALE * LOG2E) - logs)
                    if kb >= number:
                        begin = (kb - number) * rows
                        part = mask[number, begin : begin + rows]
                        probs = probs * jnp.concatenate([part] * repeat, axis=1)
                    scores = (probs * (nt(r.v[g, here], grad) - sums)).astype(BF16)
                    grad_values[here] += nn(probs.astype(BF16), grad)
                    grad_keys[here] += nn(scores, queries)
                    grad_queries = grad_queries + tn(scores, keys)
                for i, head in enumerate(heads_here):
                    begin = g * wide + i * HEAD
                    grads[at, begin : begin + HEAD] = head_norm_back(
                        grad_queries[i * rows : (i + 1) * rows] * SCALE,
                        r.q_pre[head, at],
                        q_gain,
                        number,
                        16,
                    )
            key_columns = slice(g * wide + repeat * HEAD, g * wide + (repeat + 1) * HEAD)
            value_columns = slice(g * wide + (repeat + 1) * HEAD, (g + 1) * wide)
            for number in range(blocks):
                at = slice(number * rows, (number + 1) * rows)
                grads[at, key_columns] = head_norm_back(
                    grad_keys[at] * SCALE, r.k_pre[g, at], k_gain, number, 17
                )
                grads[at, value_columns] = grad_values[at].astype(BF16)

        def weight_grads(g):
            def body(i, _):
                chunk = lax.rem(i + 1 + p.col, width // 256)
                at = pl.ds(pl.multiple_of(chunk * 256, 256), 256)
                tokens = r.normed[:, :, at].reshape(4 * rows, 256)
                grad_wa[at, of_group[g]] = tn(tokens, grads[:, of_group[g]]).astype(BF16)
                collect_a[g].start(chunk, 256)
                return 0

            lax.fori_loop(0, width // 256, body, 0)

        def project(k):
            at = pl.ds(pl.multiple_of(home_back.block(k) * rows, rows), rows)

            def part(i):
                return lambda: nt(grads[at], r.wa_whole[i * 256 : (i + 1) * 256])

            home_back.add(k, [part(i) for i in range(width // 256)])

        for g in range(kv_heads - 1):
            group(g)
            weight_grads(g)
        collect_m[2].relay()
        group(kv_heads - 1)
        for copy in down_sends:
            copy.wait_recv()
            copy.wait_send()

        def output(at):
            r.output[at] = (r.kept[0, at] + r.down_landed[at].astype(F32)).astype(BF16)

        by_rows(rows, output)
        project(0)
        project(1)
        home_back.settle_outer(0)
        home_back.settle_outer(1)
        project(2)
        project(3)
        weight_grads(kv_heads - 1)
        home_back.settle_gate(0)
        home_back.settle_gate(1)
        home_back.settle(2)
        home_back.settle(3)
        collect_o.relay()
        for part in collect_a[:-1]:
            part.relay()
        collect_m[0].result([(r.grad_gate, 0, units, False)])
        collect_m[1].result([(r.grad_up, 0, units, False)])
        home_back.arrive()
        gain = gains_rows(r.gains[...])[0]
        r.gain_rows[...] = jnp.zeros_like(r.gain_rows)

        def norm_one_back(at):
            grad_normed = home_back.value(at)
            unit, scale = unit_of(r.x[at].astype(F32))
            r.gain_rows[...] += jnp.sum(grad_normed * unit, axis=0, keepdims=True)
            scaled = grad_normed * gain
            mean = jnp.mean(scaled * unit, axis=-1, keepdims=True)
            r.input_grad[at] += scale * (scaled - unit * mean)

        by_rows(rows, norm_one_back)
        for i in range(8):
            r.gain_pack[i : i + 1] = r.gain_rows[:, i * 128 : (i + 1) * 128]
        gains_plane.start()
        collect_a[-1].relay()
        r.plane_sum[...] = gains_plane.total()
        gains_tensor.start()
        collect_m[2].result([(r.grad_down, 0, units, turned)])
        collect_o.result([(r.grad_out, 0, nq, turned)])
        total = gains_tensor.total()
        for base, ref in (
            (0, r.grad_gain_one), (8, r.grad_gain_two), (16, r.grad_q_gain), (17, r.grad_k_gain),
        ):
            ref[...] = share(p, total, base, ref.shape[1])
        for g, part in enumerate(collect_a):
            size = repeat * HEAD
            part.result(
                [
                    (r.grad_query, g * size, size, False),
                    (r.grad_key, g * HEAD, HEAD, False),
                    (r.grad_value, g * HEAD, HEAD, False),
                ]
            )
        for part in collect_a:
            part.finish()

    pl.run_scoped(
        attention_back,
        pltpu.VMEM((4 * rows, nq + 2 * nk), BF16),
        pltpu.VMEM((heads, 4 * rows, HEAD), BF16),
        pltpu.VMEM((heads, 1, 4 * rows), F32),
        pltpu.VMEM((4, 2 * rows, rows), F32),
        pltpu.VMEM((4 * rows, HEAD), F32),
        pltpu.VMEM((4 * rows, HEAD), F32),
        pltpu.VMEM((width, nq + 2 * nk), BF16),
    )
    for part in (
        gains_out, gains_plane, gains_tensor, fan_back, quad_ct, home_back, *collect_m, collect_o,
    ):
        part.finish()


def call(dp, tensor, x, starts, gain_one, q_gain, k_gain, gain_two, wq, wk, wv, wo, wg, wu, wd, ct):
    rows, width = x.shape
    tokens = rows * tensor
    shard, nq = wq.shape
    nk, units = wk.shape[1], wg.shape[1]
    heads, kv_heads = nq // HEAD, nk // HEAD
    na, nm = nq + 2 * nk, 3 * units
    turned = shard % 128 == 0
    if not turned:
        wo, wd = wo.T, wd.T
    inputs = dict(
        x=x, starts=starts, gain_one=gain_one, q_gain=q_gain, k_gain=k_gain, gain_two=gain_two,
        wq=wq, wk=wk, wv=wv, wo=wo, wg=wg, wu=wu, wd=wd, ct=ct,
        rotary=jnp.asarray(rotary(tokens)).reshape(tensor, rows, HEAD),
    )
    outputs = dict(
        output=((rows, width), BF16),
        input_grad=((rows, width), F32),
        grad_gain_one=(gain_one.shape, F32),
        grad_q_gain=(q_gain.shape, F32),
        grad_k_gain=(k_gain.shape, F32),
        grad_query=((shard, nq), F32),
        grad_key=((shard, nk), F32),
        grad_value=((shard, nk), F32),
        grad_out=((nq, shard) if turned else (shard, nq), F32),
        grad_gain_two=(gain_two.shape, F32),
        grad_gate=((shard, units), F32),
        grad_up=((shard, units), F32),
        grad_down=((units, shard) if turned else (shard, units), F32),
    )
    scratch = dict(
        pack=((24, 128), F32),
        gain_slots=((dp, 24, 128), F32),
        gains=((24, 128), F32),
        gain_pack=((24, 128), F32),
        gain_rows=((1, width), F32),
        plane_slots=((dp, 24, 128), F32),
        plane_sum=((24, 128), F32),
        tensor_slots=((tensor, 24, 128), F32),
        tokens=((4, rows, width), BF16),
        normed=((4, rows, width), BF16),
        block=((rows, width), BF16),
        q=((heads, tokens, HEAD), BF16),
        k=((kv_heads, tokens, HEAD), BF16),
        v=((kv_heads, tokens, HEAD), BF16),
        q_pre=((heads, tokens, HEAD), F32),
        k_pre=((kv_heads, tokens, HEAD), F32),
        mixed=((tokens, nq), BF16),
        lse=((heads, 1, tokens), F32),
        normed_two=((4, rows, width), BF16),
        ct_whole=((4, rows, width), BF16),
        wa=((shard, na), BF16),
        wa_stage=((shard, na), BF16),
        wa_whole=((width, na), BF16),
        wo_shard=((shard, nq), BF16),
        wo_stage=((shard, nq), BF16),
        wo_whole=((width, nq), BF16),
        wm=((shard, nm), BF16),
        wm_stage=((shard, nm), BF16),
        wm_whole=((width, nm), BF16),
        kept=((2, rows, width), F32),
        passed=((rows, width), BF16),
        given=((2, rows, width), BF16),
        taken=((2, rows, width), BF16),
        summed=((2, rows, width), BF16),
        landed=((2, rows, width), BF16),
        down_landed=((rows, width), BF16),
        back_given=((2, rows, width), BF16),
        back_taken=((2, rows, width), BF16),
        back_summed=((rows, width), BF16),
        back_landed=((rows, width), BF16),
        cm_slots=((dp, shard, nm), BF16),
        cm_landed=((shard, nm), BF16),
        co_slots=((dp, shard, nq), BF16),
        co_landed=((shard, nq), BF16),
        ca_slots=((dp, shard, na), BF16),
        ca_landed=((shard, na), BF16),
    )
    semaphores = [
        *exchange_semaphores(dp),
        *exchange_semaphores(dp),
        *exchange_semaphores(tensor),
        *FAN_SEMAPHORES,
        *FAN_SEMAPHORES,
        *(spread_semaphores(dp) * 5),
        *QUAD_SEMAPHORES,
        *QUAD_SEMAPHORES,
        *HOME_SEMAPHORES,
        *HOME_SEMAPHORES,
        *PAIR_SEMAPHORES,
        *PAIR_SEMAPHORES,
        *(collect_semaphores(dp) * (4 + kv_heads)),
    ]
    names = [*inputs, *outputs, *scratch]

    def body(*refs):
        layer_refs = list(refs)
        layer(dp, tensor, turned, names, *layer_refs)

    in_specs = vmem(len(inputs))
    in_specs[1] = pl.BlockSpec(memory_space=pltpu.SMEM)
    return pl.pallas_call(
        body,
        out_shape=[jax.ShapeDtypeStruct(*s) for s in outputs.values()],
        in_specs=in_specs,
        out_specs=vmem(len(outputs)),
        scratch_shapes=[pltpu.VMEM(*s) for s in scratch.values()] + semaphores,
        compiler_params=params(1),
    )(*inputs.values()), turned


def copies_kernel(count, *refs):
    for source, target in zip(refs[:count], refs[count:]):
        target[...] = source[...]


def copied(arrays):
    return pl.pallas_call(
        functools.partial(copies_kernel, len(arrays)),
        out_shape=[jax.ShapeDtypeStruct(a.shape, a.dtype) for a in arrays],
        in_specs=vmem(len(arrays)),
        out_specs=vmem(len(arrays)),
    )(*arrays)


def shards(dp, tensor, *args):
    x, starts, attn_gain, q_gain, k_gain, wq, wk, wv, wo, mlp_gain, wg, wu, wd, ct = args
    outs, turned = call(
        dp, tensor, x[0], starts, attn_gain[None], q_gain[None], k_gain[None], mlp_gain[None],
        wq, wk, wv, wo, wg, wu, wd, ct[0],
    )
    outs = list(copied(outs))
    for i in (0, 1):
        outs[i] = outs[i][None]
    for i in (2, 3, 4, 9):
        outs[i] = outs[i][0]
    if not turned:
        for i in (8, 12):
            outs[i] = outs[i].T
    return tuple(outs)


def solution(mesh):
    sequence, square, turned = P("dp", "tensor", None), P("dp", "tensor"), P("tensor", "dp")
    gain = P("dp")
    in_specs = (
        sequence, P("dp", None), gain, gain, gain, square, square, square, turned, gain, square, square,
        turned, sequence,
    )
    out_specs = (
        sequence, sequence, gain, gain, gain, square, square, square, turned, gain, square, square,
        turned,
    )
    return jax.shard_map(
        functools.partial(shards, mesh.shape["dp"], mesh.shape["tensor"]),
        mesh=mesh,
        in_specs=in_specs,
        out_specs=out_specs,
        check_vma=False,
    )
```

```python
import functools
import math
import types

import jax
import jax.numpy as jnp
import numpy as np
from jax import lax
from jax.experimental import pallas as pl
from jax.experimental.pallas import tpu as pltpu
from jax.sharding import PartitionSpec as P

HEAD = 128
PIECE = 256
EPS = 1e-06
THETA = 1000000.0
SCALE = HEAD**-0.5
LOG2E = math.log2(math.e)
MESH = pl.DeviceIdType.MESH
F32 = jnp.float32
BF16 = jnp.bfloat16
VMEM_LIMIT = 62 * 2**20


def nt(x, y):
    return lax.dot_general(x, y, (((1,), (1,)), ((), ())), preferred_element_type=F32)


def nn(x, y):
    return lax.dot_general(x, y, (((1,), (0,)), ((), ())), preferred_element_type=F32)


def tn(x, y):
    return lax.dot_general(x, y, (((0,), (0,)), ((), ())), preferred_element_type=F32)


def start(copy):
    copy.start()


def wait(copy):
    copy.wait()


def wait_send(copy):
    copy.wait_send()


def by_rows(rows, act, step=64):
    def body(i, _):
        act(pl.ds(pl.multiple_of(i * step, step), step))
        return 0

    lax.fori_loop(0, rows // step, body, 0)


class Place:
    def __init__(self, dp, tensor):
        self.dp, self.tensor, self.columns = dp, tensor, dp // 2
        self.d = lax.axis_index("dp")
        self.t = lax.axis_index("tensor")
        self.col, self.c = lax.div(self.d, 2), lax.rem(self.d, 2)
        self.a, self.b = lax.div(self.t, 2), lax.rem(self.t, 2)
        self.sibling = self.d + 1 - 2 * self.c
        self.near = self.t + 1 - 2 * self.b
        self.far = self.t + 2 - 4 * self.a

    def barrier(self):
        semaphore = pltpu.get_barrier_semaphore()
        for k in range(1, self.dp):
            pl.semaphore_signal(
                semaphore, 1, device_id=(lax.rem(self.d + k, self.dp), self.t), device_id_type=MESH
            )
        for k in range(1, self.tensor):
            pl.semaphore_signal(
                semaphore,
                1,
                device_id=(self.d, lax.rem(self.t + k, self.tensor)),
                device_id_type=MESH,
            )
        pl.semaphore_wait(semaphore, self.dp + self.tensor - 2)

    def plane(self, bits_a, bits_b):
        first = self.a + bits_a - 2 * self.a * bits_a
        second = self.b + bits_b - 2 * self.b * bits_b
        return 2 * first + second


def remote(source, target, send, receive, device):
    return pltpu.make_async_remote_copy(
        src_ref=source,
        dst_ref=target,
        send_sem=send,
        recv_sem=receive,
        device_id=device,
        device_id_type=MESH,
    )


class Spread:
    def __init__(self, place, shard, stage, whole, send, receive, cross):
        self.p, self.shard, self.stage, self.whole = place, shard, stage, whole
        self.send, self.receive, self.cross = send, receive, cross
        self.rows = shard.shape[0]
        self.square = place.columns == 4
        y, x = lax.div(place.col, 2), lax.rem(place.col, 2)
        if self.square:
            self.side = [2 * y + 1 - x, 2 * (1 - y) + x]
            self.corner = 2 * (1 - y) + 1 - x

    def slot(self, index, half=None):
        size = self.rows if half is None else self.rows // 2
        begin = index * self.rows + (0 if half is None else half * size)
        return self.whole.at[pl.ds(pl.multiple_of(begin, size), size)]

    def crossing(self):
        p = self.p
        return remote(self.shard, self.stage, self.cross.at[0], self.cross.at[1], (p.d, p.far))

    def each(self, phase, act_remote, act_local):
        p = self.p
        source = self.shard if phase == 0 else self.stage
        core = p.a if phase == 0 else 1 - p.a
        columns = (
            [p.col] + self.side
            if self.square
            else [lax.rem(p.col + j, p.columns) for j in range(p.columns)]
        )
        for j, column in enumerate(columns):
            send = self.send.at[phase, j]

            def to_other():
                act_remote(
                    remote(
                        source,
                        self.slot(p.d),
                        send,
                        self.receive.at[p.d, 0],
                        (2 * column + core, p.t),
                    )
                )

            def to_self():
                act_local(pltpu.make_async_copy(source, self.slot(p.d), send))

            if j == 0 and act_local:
                pl.when(core == p.c)(to_self)
            if act_remote:
                if j:
                    to_other()
                else:
                    pl.when(core != p.c)(to_other)

    def start(self, phase):
        self.each(phase, start, start)

    def cross_start(self):
        self.crossing().start()

    def cross_wait(self):
        self.crossing().wait_recv()

    def landed(self, index, half):
        p = self.p
        part = self.slot(index, half)
        remote(
            part, part, self.send.at[0, 0], self.receive.at[index, half or 0], (p.d, p.t)
        ).wait_recv()

    def forwards(self, act):
        p = self.p
        for direction in range(2):
            for core in range(2):
                index = 2 * self.side[direction] + core
                part = self.slot(index, direction)
                act(
                    remote(
                        part,
                        part,
                        self.send.at[2 + direction, core],
                        self.receive.at[index, direction],
                        (2 * self.side[1 - direction] + p.c, p.t),
                    )
                )

    def forward(self):
        if self.square:
            for direction in range(2):
                for core in range(2):
                    self.landed(2 * self.side[direction] + core, None)
            self.forwards(start)

    def wait_whole(self):
        p = self.p
        self.each(0, None, wait)
        self.each(1, None, wait)
        if self.square:
            self.landed(p.sibling, None)
            for core in range(2):
                for half in range(2):
                    self.landed(2 * self.corner + core, half)
        else:
            for k in range(1, p.dp):
                self.landed(lax.rem(p.d + k, p.dp), None)

    def cross_sent(self):
        self.crossing().wait_send()

    def wait_sends(self):
        self.each(0, wait_send, None)
        self.each(1, wait_send, None)
        if self.square:
            self.forwards(wait_send)


def spread_semaphores(dp):
    return [
        pltpu.SemaphoreType.DMA((4, max(dp // 2, 4))),
        pltpu.SemaphoreType.DMA((dp, 2)),
        pltpu.SemaphoreType.DMA((2,)),
    ]


class Fan:
    PIECES = 4

    def __init__(self, place, block, whole, send, receive, onward):
        self.p, self.block, self.whole = place, block, whole
        self.send, self.receive, self.onward = send, receive, onward
        self.slots = [place.plane(k // 2, k % 2) for k in range(4)]
        self.rows = block.shape[0] // self.PIECES

    def first_hop(self, act, pieces):
        p = self.p
        plane = lax.select(p.a == p.c, p.near, p.c + 1)
        for piece in pieces:
            at = pl.ds(piece * self.rows, self.rows)
            act(
                remote(
                    self.block.at[at],
                    self.whole.at[p.t, at],
                    self.send.at[piece],
                    self.receive.at[p.t, piece],
                    (p.d, plane),
                )
            )

    def start(self, piece=None):
        p = self.p
        pieces = range(self.PIECES) if piece is None else [piece]
        self.first_hop(start, pieces)

        @pl.when(p.a == p.c)
        def _():
            for piece in pieces:
                at = pl.ds(piece * self.rows, self.rows)
                self.whole[p.t, at] = self.block[at]

    def hop(self, index, piece, device, row):
        part = self.whole.at[self.slots[index], pl.ds(piece * self.rows, self.rows)]
        return remote(
            part,
            part,
            self.onward.at[row, index, piece],
            self.receive.at[self.slots[index], piece],
            device,
        )

    def to_sibling(self, index, piece):
        return self.hop(index, piece, (self.p.sibling, self.p.t), 0)

    def to_near(self, index, piece):
        return self.hop(index, piece, (self.p.d, self.p.near), 1)

    def take(self, *indices):
        p = self.p
        for piece in range(self.PIECES):
            for index in indices:

                def arrived():
                    self.to_sibling(index, piece).wait_recv()

                if index == 0:
                    pl.when(p.a != p.c)(arrived)
                else:
                    arrived()

                @pl.when(p.a == p.c)
                def _():
                    if index >= 2:
                        pl.when(p.t == p.c + 1)(lambda: self.to_near(index, piece).start())
                    self.to_sibling(index, piece).start()

    def finish(self):
        p = self.p
        self.first_hop(wait_send, range(self.PIECES))

        @pl.when(p.a == p.c)
        def _():
            for index in range(4):
                for piece in range(self.PIECES):
                    self.to_sibling(index, piece).wait_send()
                    if index >= 2:
                        pl.when(p.t == p.c + 1)(lambda: self.to_near(index, piece).wait_send())


FAN_SEMAPHORES = [
    pltpu.SemaphoreType.DMA((Fan.PIECES,)),
    pltpu.SemaphoreType.DMA((4, Fan.PIECES)),
    pltpu.SemaphoreType.DMA((2, 4, Fan.PIECES)),
]


def gains_rows(total):
    one = jnp.concatenate([total[i : i + 1] for i in range(8)], axis=1)
    two = jnp.concatenate([total[i : i + 1] for i in range(8, 16)], axis=1)
    return one, two, total[16:17], total[17:18]


def unit_of(values):
    scale = lax.rsqrt(jnp.mean(values * values, axis=-1, keepdims=True) + EPS)
    return values * scale, scale


class Home:
    PIECES = 4

    def __init__(self, place, kept, given, taken, summed, landed, passed, semaphores):
        self.p = place
        self.kept, self.given, self.taken, self.summed, self.landed = kept, given, taken, summed, landed
        self.passed = passed
        self.given_send, self.taken_receive, self.summed_send, self.landed_receive, self.passing = (
            semaphores
        )
        self.rows = landed.shape[1] // self.PIECES
        self.gate = place.t == place.a + 1

    def block(self, k):
        k = 3 - k
        return self.p.plane(k // 2, k % 2)

    def mine(self, k):
        return self.p.c == (self.p.b if k % 2 else 1 - self.p.b)

    def give(self, slot):
        return remote(
            self.given.at[slot],
            self.taken.at[slot],
            self.given_send.at[slot],
            self.taken_receive.at[slot],
            (self.p.sibling, self.p.t),
        )

    def at(self, piece):
        return pl.ds(piece * self.rows, self.rows)

    def send(self, k, piece):
        p = self.p
        return remote(
            self.summed.at[k // 2, self.at(piece)],
            self.landed.at[p.b, self.at(piece)],
            self.summed_send.at[k // 2, piece],
            self.landed_receive.at[p.b, piece],
            (2 * p.col + p.a, self.block(k)),
        )

    def to_gate(self, piece):
        p = self.p
        return remote(
            self.summed.at[0, self.at(piece)],
            self.passed.at[self.at(piece)],
            self.passing.at[0, piece],
            self.passing.at[1, piece],
            (p.d, p.near),
        )

    def add(self, k, parts):
        @pl.when(self.mine(k))
        def _():
            for i, part in enumerate(parts):
                self.kept[k // 2, :, i * 256 : (i + 1) * 256] = part()

        @pl.when(jnp.logical_not(self.mine(k)))
        def _():
            for i, part in enumerate(parts):
                self.given[k // 2, :, i * 256 : (i + 1) * 256] = part().astype(BF16)
            self.give(k // 2).start()

    def total(self, k, piece):
        at = self.at(piece)
        return self.kept[k // 2, at] + self.taken[k // 2, at].astype(F32)

    def settle_outer(self, k):
        @pl.when(jnp.logical_and(self.mine(k), jnp.logical_not(self.gate)))
        def _():
            self.give(0).wait_recv()
            for piece in range(self.PIECES):
                self.summed[0, self.at(piece)] = self.total(k, piece).astype(BF16)
                self.to_gate(piece).start()

    def settle_gate(self, k):
        @pl.when(jnp.logical_and(self.mine(k), self.gate))
        def _():
            self.give(0).wait_recv()
            for piece in range(self.PIECES):
                at = self.at(piece)
                self.to_gate(piece).wait_recv()
                self.summed[0, at] = (
                    self.total(k, piece) + self.passed[at].astype(F32)
                ).astype(BF16)
                self.send(k, piece).start()

    def settle(self, k):
        p = self.p

        @pl.when(self.mine(k))
        def _():
            self.give(1).wait_recv()
            stays = jnp.logical_and(p.a == p.c, jnp.asarray(k == 3))

            @pl.when(stays)
            def _():
                for piece in range(self.PIECES):
                    self.landed[p.b, self.at(piece)] = self.total(k, piece).astype(BF16)

            @pl.when(jnp.logical_not(stays))
            def _():
                for piece in range(self.PIECES):
                    self.summed[1, self.at(piece)] = self.total(k, piece).astype(BF16)
                    self.send(k, piece).start()

    def arrive(self):
        p = self.p

        def arrived(slot):
            for piece in range(self.PIECES):
                part = self.landed.at[slot, self.at(piece)]
                remote(
                    part,
                    part,
                    self.summed_send.at[0, piece],
                    self.landed_receive.at[slot, piece],
                    (p.d, p.t),
                ).wait_recv()

        @pl.when(p.a == p.c)
        def _():
            arrived(1 - p.b)
            pl.when(p.c != p.b)(lambda: arrived(p.b))

        @pl.when(p.a != p.c)
        def _():
            self.landed[p.c] = jnp.zeros(self.landed.shape[1:], BF16)
            arrived(1 - p.c)

    def value(self, at):
        return self.landed[0, at].astype(F32) + self.landed[1, at].astype(F32)

    def finish(self):
        for k in range(4):

            @pl.when(jnp.logical_not(self.mine(k)))
            def _():
                self.give(k // 2).wait_send()

            sent = self.mine(k)
            if k == 3:
                sent = jnp.logical_and(sent, self.p.a != self.p.c)
            if k < 2:
                sent = jnp.logical_and(sent, self.gate)

                @pl.when(jnp.logical_and(self.mine(k), jnp.logical_not(self.gate)))
                def _():
                    for piece in range(self.PIECES):
                        self.to_gate(piece).wait_send()

            @pl.when(sent)
            def _():
                for piece in range(self.PIECES):
                    self.send(k, piece).wait_send()


HOME_SEMAPHORES = [
    pltpu.SemaphoreType.DMA((2,)),
    pltpu.SemaphoreType.DMA((2,)),
    *[pltpu.SemaphoreType.DMA((2, Home.PIECES))] * 3,
]


class Quad:
    def __init__(self, place, block, whole, send, receive):
        self.p, self.whole_block, self.whole, self.sent, self.receive = place, block, whole, send, receive
        b, c = place.b, place.c
        self.slots = [2 * b + c, 2 * b + 1 - c, 2 * (1 - b) + c, 2 * (1 - b) + 1 - c]

    def copy(self, index, source, slot, device):
        return remote(
            source, self.whole.at[slot], self.sent.at[index], self.receive.at[slot], device
        )

    def near(self):
        p = self.p
        return self.copy(0, self.whole_block, self.slots[0], (p.d, p.near))

    def beside(self):
        p = self.p
        return self.copy(1, self.whole_block, self.slots[0], (p.sibling, p.t))

    def onward(self):
        p = self.p
        return self.copy(2, self.whole.at[self.slots[2]], self.slots[2], (p.sibling, p.t))

    def start(self):
        self.near().start()
        self.beside().start()
        self.whole[self.slots[0]] = self.whole_block[...]

    def take(self, index):
        slot = self.slots[index]
        self.copy(0, self.whole_block, slot, (self.p.d, self.p.near)).wait_recv()
        if index == 2:
            self.onward().start()

    def finish(self):
        self.near().wait_send()
        self.beside().wait_send()
        self.onward().wait_send()


QUAD_SEMAPHORES = [pltpu.SemaphoreType.DMA((3,)), pltpu.SemaphoreType.DMA((4,))]


class PairSum:
    def __init__(self, place, kept, given, taken, summed, landed, given_send, taken_receive, across):
        self.p = place
        self.kept, self.given, self.taken, self.summed, self.landed = kept, given, taken, summed, landed
        self.given_send, self.taken_receive, self.across = given_send, taken_receive, across

    def give(self, half):
        return remote(
            self.given.at[half],
            self.taken.at[half],
            self.given_send.at[half],
            self.taken_receive.at[half],
            (self.p.sibling, self.p.t),
        )

    PIECES = 4

    def at(self, piece):
        size = self.summed.shape[0] // self.PIECES
        return pl.ds(piece * size, size)

    def send(self, piece):
        p = self.p
        return remote(
            self.summed.at[self.at(piece)],
            self.landed.at[self.at(piece)],
            self.across.at[0, piece],
            self.across.at[1, piece],
            (p.d, p.near),
        )

    def add_far(self, send):
        self.give(1).wait_recv()
        for piece in range(self.PIECES):
            at = self.at(piece)
            self.summed[at] = (self.kept[1, at] + self.taken[1, at].astype(F32)).astype(BF16)
            if send:
                self.send(piece).start()

    def take_own(self):
        self.give(0).wait_recv()

    def own(self, at):
        return self.kept[0, at] + self.taken[0, at].astype(F32)

    def finish(self):
        self.give(0).wait_send()
        self.give(1).wait_send()


PAIR_SEMAPHORES = [
    pltpu.SemaphoreType.DMA((2,)),
    pltpu.SemaphoreType.DMA((2,)),
    pltpu.SemaphoreType.DMA((2, PairSum.PIECES)),
]


class Collect:
    def __init__(self, place, source, slots, summed, landed, send, receive, across):
        self.p, self.source, self.slots, self.summed, self.landed = place, source, slots, summed, landed
        self.send, self.receive, self.across = send, receive, across
        self.rows = slots.shape[1]

    def part(self, index):
        return self.source.at[pl.ds(pl.multiple_of(index * self.rows, self.rows), self.rows)]

    def own(self):
        p = self.p
        return pltpu.make_async_copy(self.part(p.d), self.slots.at[p.d], self.send.at[0, p.d])

    def other(self, target):
        p = self.p
        return remote(
            self.part(target),
            self.slots.at[p.d],
            self.send.at[0, target],
            self.receive.at[0, p.d],
            (target, p.t),
        )

    def start(self, chunk, size):
        count = size // self.rows

        def body(i, _):
            target = chunk * count + i
            pl.when(target == self.p.d)(lambda: self.own().start())
            pl.when(target != self.p.d)(lambda: self.other(target).start())
            return 0

        lax.fori_loop(0, count, body, 0)

    def cross(self):
        p = self.p
        return remote(self.summed, self.landed, self.across.at[0], self.across.at[1], (p.d, p.far))

    def total(self, core, here):
        return lax.fori_loop(
            1,
            self.p.columns,
            lambda i, s: s + self.slots[2 * i + core, :, here].astype(F32),
            self.slots[core, :, here].astype(F32),
        )

    def gathered(self):
        p = self.p
        self.own().wait()
        for k in range(1, p.dp):
            source = lax.rem(p.d + k, p.dp)
            remote(
                self.part(source),
                self.slots.at[source],
                self.send.at[0, source],
                self.receive.at[0, source],
                (p.d, p.t),
            ).wait_recv()

    def relay(self):
        self.gathered()
        for begin in range(0, self.summed.shape[1], 256):
            here = slice(begin, begin + 256)
            self.summed[:, here] = self.total(1 - self.p.a, here).astype(BF16)
        self.cross().start()

    def result(self, targets):
        self.cross().wait_recv()
        begin = 0
        for target, first, count, turned in targets:
            for offset in range(0, count, min(count, 256)):
                size = min(count, 256)
                here = slice(begin, begin + size)
                there = slice(first + offset, first + offset + size)
                value = self.total(self.p.a, here) + self.landed[:, here].astype(F32)
                if turned:
                    target[there] = value.T
                else:
                    target[:, there] = value
                begin += size

    def order(self, i):
        count = self.source.shape[0] // 256
        return lax.rem(i + 1 + self.p.col, count)

    def halfway(self):
        pass

    def finish(self):
        p = self.p
        for k in range(1, p.dp):
            self.other(lax.rem(p.d + k, p.dp)).wait_send()
        self.cross().wait_send()


class SquareCollect(Collect):
    def __init__(self, place, *refs):
        super().__init__(place, *refs)
        y, x = lax.div(place.col, 2), lax.rem(place.col, 2)
        self.side = [2 * y + 1 - x, 2 * (1 - y) + x]
        self.corner = 2 * (1 - y) + 1 - x
        self.half = self.rows // 2

    def order(self, i):
        columns = [self.corner, self.side[0], self.side[1], self.p.col]
        result = columns[3]
        for k in range(3):
            result = lax.select(i == k, columns[k], result)
        return result

    def rows_of(self, column, core, direction):
        begin = (2 * column + core) * self.rows + direction * self.half
        return self.source.at[pl.ds(pl.multiple_of(begin, self.half), self.half)]

    def first(self, column, direction, beyond, core):
        p = self.p
        number = 4 * direction + 2 * beyond + core
        return remote(
            self.rows_of(column, core, direction),
            self.slots.at[4 + 2 * beyond + core, pl.ds(direction * self.half, self.half)],
            self.send.at[0, number],
            self.receive.at[0, number],
            (2 * self.side[direction] + p.c, p.t),
        )

    def firsts(self, column, kind, act):
        for direction in range(2):
            for core in range(2):
                if kind == 0:
                    act(self.first(column, direction, 1, core))
                elif kind == direction + 1:
                    act(self.first(column, direction, 0, core))

    def start(self, chunk, size):
        p = self.p
        pl.when(chunk == self.corner)(lambda: self.firsts(chunk, 0, start))
        for direction in range(2):
            pl.when(chunk == self.side[direction])(
                functools.partial(self.firsts, chunk, direction + 1, start)
            )

    def seconds(self, act):
        p = self.p
        for direction in range(2):
            here = pl.ds(direction * self.half, self.half)
            for core in range(2):
                act(
                    remote(
                        self.rows_of(self.side[1 - direction], core, direction),
                        self.slots.at[2 * p.c + 1, here],
                        self.send.at[1, 2 + 2 * direction + core],
                        self.receive.at[1, 2 + 2 * direction + p.c],
                        (2 * self.side[1 - direction] + core, p.t),
                    )
                )
        act(
            remote(
                self.part(p.sibling),
                self.slots.at[2 * p.c],
                self.send.at[1, 1],
                self.receive.at[1, p.c],
                (p.sibling, p.t),
            )
        )

    def own(self):
        p = self.p
        return pltpu.make_async_copy(self.part(p.d), self.slots.at[2 * p.c], self.send.at[1, 0])

    def halfway(self):
        p = self.p
        for direction in range(2):
            here = pl.ds(direction * self.half, self.half)
            for beyond in range(2):
                for core in range(2):
                    number = 4 * direction + 2 * beyond + core
                    slot = self.slots.at[4 + 2 * beyond + core, here]
                    remote(
                        slot,
                        slot,
                        self.send.at[0, number],
                        self.receive.at[0, number],
                        (p.d, p.t),
                    ).wait_recv()
                    column = self.side[1 - direction] if beyond else p.col
                    target = self.rows_of(column, core, direction)
                    total = target[...].astype(F32) + slot[...].astype(F32)
                    target[...] = total.astype(BF16)
        self.seconds(start)
        self.own().start()

    def gathered(self):
        p = self.p
        self.own().wait()

        def arrived(slot, number):
            remote(
                slot, slot, self.send.at[1, 0], self.receive.at[1, number], (p.d, p.t)
            ).wait_recv()

        arrived(self.slots.at[2 * (1 - p.c)], 1 - p.c)
        for direction in range(2):
            here = pl.ds(direction * self.half, self.half)
            for core in range(2):
                arrived(self.slots.at[2 * core + 1, here], 2 + 2 * direction + core)

    def total(self, core, here):
        return self.slots[2 * core, :, here].astype(F32) + self.slots[2 * core + 1, :, here].astype(
            F32
        )

    def finish(self):
        self.firsts(self.corner, 0, wait_send)
        for direction in range(2):
            self.firsts(self.side[direction], direction + 1, wait_send)
        self.seconds(wait_send)
        self.cross().wait_send()


def collect_semaphores(dp):
    return [
        pltpu.SemaphoreType.DMA((2, max(dp, 8))),
        pltpu.SemaphoreType.DMA((2, max(dp, 8))),
        pltpu.SemaphoreType.DMA((2,)),
    ]


def vmem(count):
    return [pl.BlockSpec(memory_space=pltpu.VMEM)] * count


def params(identity):
    return pltpu.CompilerParams(
        collective_id=identity, has_side_effects=True, vmem_limit_bytes=VMEM_LIMIT
    )


def rotary(tokens):
    frequency = np.float32(THETA) ** (
        -(np.arange(HEAD // 2, dtype=np.float32) * np.float32(2.0)) / np.float32(HEAD)
    )
    angles = np.arange(tokens, dtype=np.float32)[:, None] * frequency.astype(np.float32)[None, :]
    return np.concatenate([np.cos(angles), np.sin(angles)], axis=1).astype(np.float32)


def rotary_rows(table):
    other = pltpu.roll(table, HEAD // 2, 1)
    low = lax.broadcasted_iota(jnp.int32, (1, HEAD), 1) < HEAD // 2
    return jnp.where(low, table, other), jnp.where(low, -other, table)


def allowed_mask(place, gains, base, rows, keys, transposed):
    lane = lax.broadcasted_iota(jnp.int32, (1, 128), 1)
    chosen = (lane == 2 * place.col + place.a).astype(F32)
    shape = (keys, rows) if transposed else (rows, keys)
    query_dim, key_dim = (1, 0) if transposed else (0, 1)
    line = lambda dim: tuple(n if i == dim else 1 for i, n in enumerate(shape))
    query = lax.broadcasted_iota(jnp.int32, shape, query_dim)
    key = lax.broadcasted_iota(jnp.int32, shape, key_dim)
    mask = (key <= query).astype(F32)
    for piece in range(2):
        numbers = gains[18 + piece : 19 + piece]
        first_position = jnp.sum(numbers * chosen, axis=1, keepdims=True) - base.astype(F32)

        def inside(position):
            position = position.astype(F32)
            return jnp.logical_and(
                position >= first_position, position < first_position + PIECE
            ).astype(F32)

        in_query = inside(lax.broadcasted_iota(jnp.int32, line(query_dim), query_dim))
        in_key = inside(lax.broadcasted_iota(jnp.int32, line(key_dim), key_dim))
        mask = jnp.maximum(mask, in_query * in_key)
    return mask


def placed(place, values, base):
    size = values.shape[1]
    begin = place.d * size
    if size < 128:
        values = jnp.concatenate([values, jnp.zeros((1, 128 - size), F32)], axis=1)
        values = pltpu.roll(values, lax.rem(begin, 128), 1)
    row = lax.broadcasted_iota(jnp.int32, (24, 128), 0)
    return jnp.where(row == base + lax.div(begin, 128), values, 0.0)


def share(place, tile, base, size):
    begin = place.d * size
    row = lax.broadcasted_iota(jnp.int32, (24, 128), 0)
    chosen = jnp.where(row == base + lax.div(begin, 128), tile, 0.0)
    values = jnp.sum(chosen, axis=0, keepdims=True)
    if size < 128:
        values = pltpu.roll(values, lax.rem(128 - lax.rem(begin, 128), 128), 1)
    return values[:, :size]


class Exchange:
    def __init__(self, place, tile, slots, send, receive, in_plane):
        self.p, self.tile, self.slots, self.in_plane = place, tile, slots, in_plane
        self.sent, self.receive = send, receive
        self.count = place.dp if in_plane else place.tensor
        self.me = place.d if in_plane else place.t

    def copy(self, k, slot):
        p = self.p
        other = lax.rem(self.me + k, self.count)
        device = (other, p.t) if self.in_plane else (p.d, other)
        return remote(
            self.tile, self.slots.at[slot], self.sent.at[k], self.receive.at[slot], device
        )

    def start(self):
        for k in range(1, self.count):
            self.copy(k, self.me).start()
        self.slots[self.me] = self.tile[...]

    def total(self):
        for k in range(1, self.count):
            self.copy(k, lax.rem(self.me + k, self.count)).wait_recv()
        return lax.fori_loop(1, self.count, lambda i, s: s + self.slots[i], self.slots[0])

    def finish(self):
        for k in range(1, self.count):
            self.copy(k, self.me).wait_send()


def exchange_semaphores(count):
    return [pltpu.SemaphoreType.DMA((count,)), pltpu.SemaphoreType.DMA((count,))]


def layer(dp, tensor, turned, names, *refs):
    r = types.SimpleNamespace(**dict(zip(names, refs)))
    rest = list(refs[len(names) :])

    def take(count):
        head, rest[:] = rest[:count], rest[count:]
        return head

    p = Place(dp, tensor)
    gains_out = Exchange(p, r.pack, r.gain_slots, *take(2), True)
    gains_plane = Exchange(p, r.gain_pack, r.plane_slots, *take(2), True)
    gains_tensor = Exchange(p, r.plane_sum, r.tensor_slots, *take(2), False)
    fan = Fan(p, r.x, r.tokens, *take(3))
    fan_back = Fan(p, r.block, r.tokens, *take(3))
    spread_a = Spread(p, r.wa, r.wa_stage, r.wa_whole, *take(3))
    spread_o = Spread(p, r.wo_shard, r.wo_stage, r.wo_whole, *take(3))
    units = r.wg.shape[1]
    thirds = [slice(i * units, (i + 1) * units) for i in range(3)]
    spread_m = [
        Spread(p, r.wm.at[:, c], r.wm_stage.at[:, c], r.wm_whole.at[:, c], *take(3)) for c in thirds
    ]
    quad_ct = Quad(p, r.ct, r.ct_whole, *take(2))
    quad = Quad(p, r.block, r.normed_two, *take(2))
    home_buffers = (r.kept, r.given, r.taken, r.summed, r.landed, r.passed)
    home = Home(p, *home_buffers, take(5))
    home_back = Home(p, *home_buffers, take(5))
    down_semaphores, back_semaphores = take(3), take(3)
    collect = SquareCollect if dp == 8 else Collect
    collect_m = [
        collect(
            p, r.wm_whole.at[:, c], r.cm_slots.at[:, :, c], r.wm.at[:, c], r.cm_landed.at[:, c], *take(3)
        )
        for c in thirds
    ]
    collect_o = collect(p, r.wo_whole, r.co_slots, r.wo_shard, r.co_landed, *take(3))
    rows, width = r.x.shape
    nq, nk = r.wq.shape[1], r.wk.shape[1]
    heads, kv_heads, blocks = nq // HEAD, nk // HEAD, 4
    repeat = heads // kv_heads
    wide = (repeat + 2) * HEAD
    of_group = [slice(g * wide, (g + 1) * wide) for g in range(kv_heads)]
    collect_a_semaphores = [take(3) for _ in of_group]

    tile = jnp.zeros((24, 128), F32)
    for base, ref in ((0, r.gain_one), (8, r.gain_two), (16, r.q_gain), (17, r.k_gain)):
        tile = tile + placed(p, ref[...].astype(F32), base)
    row = lax.broadcasted_iota(jnp.int32, (24, 128), 0)
    lane = lax.broadcasted_iota(jnp.int32, (24, 128), 1)
    for piece in range(2):
        here = jnp.logical_and(row == 18 + piece, lane == p.d)
        tile = tile + jnp.where(here, r.starts[0, piece], 0).astype(F32)
    r.pack[...] = tile
    for g in range(kv_heads):
        begin = g * wide
        for ref, size in ((r.wq, repeat * HEAD), (r.wk, HEAD), (r.wv, HEAD)):
            r.wa[:, begin : begin + size] = ref[:, g * size : (g + 1) * size]
            begin += size
    p.barrier()
    gains_out.start()
    spread_a.cross_start()
    pl.when(p.a == p.c)(fan.start)
    spread_a.start(0)

    def turn(target, source, begin):
        if source.shape[0] == target.shape[0]:
            target[:, begin : begin + source.shape[1]] = source[...]
        else:
            for i in range(0, source.shape[0], 128):
                target[:, begin + i : begin + i + 128] = source[i : i + 128].T

    turn(r.wo_shard, r.wo, 0)
    r.wm[:, :units] = r.wg[...]
    r.wm[:, units : 2 * units] = r.wu[...]
    turn(r.wm, r.wd, 2 * units)
    total = gains_out.total()
    r.gains[...] = total
    gain_one, gain_two, q_gain, k_gain = gains_rows(total)
    def normalize(slot):
        def act(at):
            unit, _ = unit_of(r.tokens[slot, at].astype(F32))
            r.normed[slot, at] = (unit * gain_one).astype(BF16)

        by_rows(rows, act)

    fan.take(0)
    spread_a.cross_sent()
    pl.when(p.a != p.c)(fan.start)
    spread_a.cross_wait()
    spread_a.start(1)
    spread_o.start(0)
    fan.take(1)
    spread_a.forward()
    normalize(fan.slots[0])
    normalize(fan.slots[1])
    fan.take(2, 3)
    spread_o.cross_start()
    quad_ct.start()
    for part in spread_m:
        part.start(0)
    normalize(fan.slots[2])
    normalize(fan.slots[3])
    spread_a.wait_whole()
    fan.finish()
    spread_a.wait_sends()

    def attention(v_wide, mask):
        v_wide[:, :, HEAD:] = jnp.ones((kv_heads, rows * 4, HEAD), BF16)

        def qkv(slot, _):
            at = pl.ds(pl.multiple_of(slot * rows, rows), rows)
            cosine, sine = rotary_rows(r.rotary[slot])

            def rotated(values, gain):
                unit_values, _ = unit_of(values)
                scaled = unit_values * gain
                return (scaled * cosine + pltpu.roll(scaled, 64, 1) * sine).astype(BF16)

            for g in range(kv_heads):
                for i in range(0, repeat + 2, 2):
                    begin = g * wide + i * HEAD
                    product = nn(r.normed[slot], r.wa_whole[:, begin : begin + 2 * HEAD])
                    for j in range(2):
                        values = product[:, j * HEAD : (j + 1) * HEAD]
                        if i + j < repeat:
                            r.q_pre[g * repeat + i + j, at] = values
                            r.q[g * repeat + i + j, at] = rotated(values, q_gain)
                        elif i + j == repeat:
                            r.k_pre[g, at] = values
                            r.k[g, at] = rotated(values, k_gain)
                        else:
                            v_wide[g, at, :HEAD] = values.astype(BF16)
            return 0

        lax.fori_loop(0, 4, qkv, 0)

        def attend(k):
            block = home.block(k)
            mask[...] = allowed_mask(p, r.gains[...], block * rows, rows, 2 * rows, False)
            for number in range(blocks):

                @pl.when(block == number)
                def _():
                    at = slice(number * rows, (number + 1) * rows)

                    def group(g, _):
                        queries = r.q[pl.ds(g * repeat, repeat), at].reshape(repeat * rows, HEAD)
                        total = jnp.zeros((repeat * rows, 2 * HEAD), F32)
                        for kb in range(min(number + 2, blocks)):
                            keys = slice(kb * rows, (kb + 1) * rows)
                            weight = jnp.exp2(nt(queries, r.k[g, keys]) * (SCALE * LOG2E))
                            if kb >= number:
                                part = mask[:, (kb - number) * rows : (kb - number + 1) * rows]
                                weight = weight * jnp.concatenate([part] * repeat, axis=0)
                            total = total + nn(weight.astype(BF16), v_wide[g, keys])
                        summed = total[:, HEAD:]
                        result = (total[:, :HEAD] / summed).astype(BF16)
                        result = jnp.concatenate(
                            [result[i * rows : (i + 1) * rows] for i in range(repeat)], axis=1
                        )
                        size = repeat * HEAD
                        r.mixed[at, pl.ds(pl.multiple_of(g * size, size), size)] = result
                        logs = jnp.log2(summed)
                        for i in range(repeat):
                            across = logs[i * rows : (i + 1) * rows].T
                            r.lse[g * repeat + i, :, at] = across[0:1]
                        return 0

                    lax.fori_loop(0, kv_heads, group, 0)

        def project(k):
            at = pl.ds(pl.multiple_of(home.block(k) * rows, rows), rows)

            def part(i):
                return lambda: nt(r.mixed[at], r.wo_whole[i * 256 : (i + 1) * 256])

            home.add(k, [part(i) for i in range(width // 256)])

        spread_o.cross_wait()
        spread_o.start(1)
        spread_m[0].cross_start()
        attend(0)
        attend(1)
        spread_m[1].cross_start()
        spread_o.forward()
        spread_o.wait_whole()
        project(0)
        project(1)
        home.settle_outer(0)
        home.settle_outer(1)
        attend(2)
        project(2)
        spread_m[0].cross_wait()
        spread_m[0].start(1)
        spread_m[2].cross_start()
        attend(3)
        project(3)
        home.settle_gate(0)
        home.settle_gate(1)
        home.settle(2)
        home.settle(3)
        r.v[...] = v_wide[:, :, :HEAD]

    pl.run_scoped(
        attention,
        pltpu.VMEM((kv_heads, 4 * rows, 2 * HEAD), BF16),
        pltpu.VMEM((rows, 2 * rows), F32),
    )
    spread_m[0].forward()
    spread_m[1].cross_wait()
    spread_m[1].start(1)
    quad_ct.take(1)
    quad_ct.take(2)
    home.arrive()

    def norm_two(at):
        hidden = r.x[at].astype(F32) + home.value(at)
        r.kept[0, at] = hidden
        unit, _ = unit_of(hidden)
        r.block[at] = (unit * gain_two).astype(BF16)

    by_rows(rows, norm_two)
    quad.start()
    spread_m[2].cross_wait()
    spread_m[2].start(1)
    spread_m[1].forward()
    quad_ct.take(3)
    quad.take(1)
    quad.take(2)
    quad.take(3)
    spread_m[2].forward()
    quad.finish()
    home.finish()
    spread_o.cross_sent()
    spread_o.wait_sends()
    for part in spread_m:
        part.wait_whole()
    for part in spread_m:
        part.cross_sent()
        part.wait_sends()

    def feed_forward(active, grad_gate, grad_up, down_kept, back_kept):
        down = PairSum(
            p, down_kept, r.given, r.taken, r.summed.at[0], r.down_landed, *down_semaphores
        )
        back = PairSum(
            p, back_kept, r.back_given, r.back_taken, r.back_summed, r.back_landed, *back_semaphores
        )
        wm = r.wm_whole

        def work(slot, keep, half):
            tokens, cotangent = r.normed_two[slot], r.ct_whole[slot]
            at = pl.ds(pl.multiple_of(slot * rows, rows), rows)
            for i in range(units // 256):
                here = slice(i * 256, (i + 1) * 256)
                gate = nn(tokens, wm[:, i * 256 : (i + 1) * 256])
                upward = nn(tokens, wm[:, units + i * 256 : units + (i + 1) * 256])
                grad = nn(cotangent, wm[:, 2 * units + i * 256 : 2 * units + (i + 1) * 256])
                sigmoid = 1.0 / (1.0 + jnp.exp2(gate * -LOG2E))
                silu = gate * sigmoid
                active[at, here] = (silu * upward).astype(BF16)
                grad_gate[at, here] = (
                    grad * upward * sigmoid * (1.0 + gate * (1.0 - sigmoid))
                ).astype(BF16)
                grad_up[at, here] = (grad * silu).astype(BF16)
            for i in range(width // 256):
                here = slice(i * 256, (i + 1) * 256)
                out = nt(grad_gate[at], wm[here, :units]) + nt(
                    grad_up[at], wm[here, units : 2 * units]
                )
                if keep:
                    back.kept[half, :, here] = out
                else:
                    back.given[half, :, here] = out.astype(BF16)
            if not keep:
                back.give(half).start()
            for i in range(width // 256):
                here = slice(i * 256, (i + 1) * 256)
                out = nt(active[at], wm[here, 2 * units :])
                if keep:
                    down.kept[half, :, here] = out
                else:
                    down.given[half, :, here] = out.astype(BF16)
            if not keep:
                down.give(half).start()

        def both(step, _):
            half = 1 - step
            other = lax.select(half == 1, 1 - p.b, p.b)
            work(2 * other + p.c, True, half)
            work(2 * other + 1 - p.c, False, half)

            @pl.when(half == 1)
            def _():
                back.add_far(True)

            return 0

        lax.fori_loop(0, 2, both, 0)

        def weight_grads(third, tokens_ref, grad):
            def body(i, _):
                chunk = collect_m[third].order(i)
                at = pl.ds(pl.multiple_of(chunk * 256, 256), 256)
                tokens = tokens_ref[:, :, at].reshape(4 * rows, 256)
                wm[at, thirds[third]] = tn(tokens, grad[...]).astype(BF16)
                collect_m[third].start(chunk, 256)
                return 0

            lax.fori_loop(0, width // 256, body, 0)

        weight_grads(0, r.normed_two, grad_gate)
        down.add_far(False)
        down.take_own()
        back.take_own()
        gain = gains_rows(r.gains[...])[1]
        r.gain_rows[...] = jnp.zeros_like(r.gain_rows)

        def norm_two_back(at):
            grad_normed = back.own(at) + back.landed[at].astype(F32)
            unit, scale = unit_of(r.kept[0, at])
            r.gain_rows[...] += jnp.sum(grad_normed * unit, axis=0, keepdims=True)
            scaled = grad_normed * gain
            mean = jnp.mean(scaled * unit, axis=-1, keepdims=True)
            grad = r.ct[at].astype(F32) + scale * (scaled - unit * mean)
            r.input_grad[at] = grad
            r.block[at] = grad.astype(BF16)

        for piece in range(back.PIECES):
            back.send(piece).wait_recv()
            norm_two_back(back.at(piece))
            fan_back.start(piece)
        fan_back.take(0)

        def hidden_sum(at):
            r.kept[0, at] += down.own(at)

        by_rows(rows, hidden_sum)
        weight_grads(1, r.normed_two, grad_up)
        fan_back.take(1)
        weight_grads(2, r.ct_whole, active)
        for i in range(8):
            r.gain_pack[8 + i : 9 + i] = r.gain_rows[:, i * 128 : (i + 1) * 128]
        collect_m[0].halfway()
        fan_back.take(2, 3)
        collect_m[1].halfway()
        collect_m[0].relay()
        for piece in range(back.PIECES):
            back.send(piece).wait_send()
        back.finish()
        down.finish()

    r.gain_pack[16:24] = jnp.zeros((8, 128), F32)
    pl.run_scoped(
        feed_forward,
        *[pltpu.VMEM((4 * rows, units), BF16)] * 3,
        *[pltpu.VMEM((2, rows, width), F32)] * 2,
    )

    def attention_back(grads, grad_mixed, delta, mask, grad_keys, grad_values, grad_wa):
        collect_a = [
            collect(
                p, grad_wa.at[:, c], r.ca_slots.at[:, :, c], r.wa.at[:, c], r.ca_landed.at[:, c],
                *semaphores,
            )
            for c, semaphores in zip(of_group, collect_a_semaphores)
        ]
        down_sends = [
            remote(
                r.summed.at[0, at],
                r.down_landed.at[at],
                down_semaphores[2].at[0, i],
                down_semaphores[2].at[1, i],
                (p.d, p.near),
            )
            for i, at in enumerate(pl.ds(j * (rows // 4), rows // 4) for j in range(4))
        ]
        for number in range(blocks):
            base = jnp.int32(number * rows)
            mask[number] = allowed_mask(p, r.gains[...], base, rows, 2 * rows, True)
        for copy in down_sends:
            copy.start()

        def mixed_back(slot, _):
            at = pl.ds(pl.multiple_of(slot * rows, rows), rows)
            for i in range(heads * HEAD // 256):
                grad = nn(r.tokens[slot], r.wo_whole[:, i * 256 : (i + 1) * 256]).astype(BF16)
                for j in range(256 // HEAD):
                    head = i * (256 // HEAD) + j
                    one = grad[:, j * HEAD : (j + 1) * HEAD]
                    grad_mixed[head, at] = one
                    mixed = r.mixed[at, head * HEAD : (head + 1) * HEAD]
                    row = lax.dot_general(
                        jnp.ones((8, HEAD), F32),
                        one.astype(F32) * mixed.astype(F32),
                        (((1,), (1,)), ((), ())),
                        precision=lax.Precision.HIGHEST,
                        preferred_element_type=F32,
                    )
                    delta[head, :, at] = row[0:1]
            return 0

        lax.fori_loop(0, 4, mixed_back, 0)

        def out_grads(i, _):
            chunk = collect_o.order(i)
            at = pl.ds(pl.multiple_of(chunk * 256, 256), 256)
            tokens = r.tokens[:, :, at].reshape(4 * rows, 256)
            r.wo_whole[at] = tn(tokens, r.mixed[...]).astype(BF16)
            collect_o.start(chunk, 256)
            return 0

        lax.fori_loop(0, width // 256, out_grads, 0)
        collect_m[2].halfway()
        collect_m[1].relay()
        _, _, q_gain, k_gain = gains_rows(r.gains[...])

        def head_norm_back(grad, before, gain, number, row):
            unit, scale = unit_of(before)
            cosine, sine = rotary_rows(r.rotary[number])
            back = grad * cosine - pltpu.roll(grad, 64, 1) * sine
            r.gain_pack[row : row + 1] += jnp.sum(back * unit, axis=0, keepdims=True)
            scaled = back * gain
            mean = jnp.mean(scaled * unit, axis=-1, keepdims=True)
            return (scale * (scaled - unit * mean)).astype(BF16)

        def group(g):
            grad_keys[...] = jnp.zeros_like(grad_keys)
            grad_values[...] = jnp.zeros_like(grad_values)

            for number in range(blocks):
                at = slice(number * rows, (number + 1) * rows)
                heads_here = range(g * repeat, (g + 1) * repeat)
                queries = r.q[g * repeat : (g + 1) * repeat, at].reshape(repeat * rows, HEAD)
                grad = grad_mixed[g * repeat : (g + 1) * repeat, at].reshape(repeat * rows, HEAD)
                logs = jnp.concatenate([r.lse[head, :, at] for head in heads_here], axis=1)
                sums = jnp.concatenate([delta[head, :, at] for head in heads_here], axis=1)
                grad_queries = jnp.zeros((repeat * rows, HEAD), F32)
                for kb in range(min(number + 2, blocks)):
                    here = slice(kb * rows, (kb + 1) * rows)
                    keys = r.k[g, here]
                    probs = jnp.exp2(nt(keys, queries) * (SCALE * LOG2E) - logs)
                    if kb >= number:
                        begin = (kb - number) * rows
                        part = mask[number, begin : begin + rows]
                        probs = probs * jnp.concatenate([part] * repeat, axis=1)
                    scores = (probs * (nt(r.v[g, here], grad) - sums)).astype(BF16)
                    grad_values[here] += nn(probs.astype(BF16), grad)
                    grad_keys[here] += nn(scores, queries)
                    grad_queries = grad_queries + tn(scores, keys)
                for i, head in enumerate(heads_here):
                    begin = g * wide + i * HEAD
                    grads[at, begin : begin + HEAD] = head_norm_back(
                        grad_queries[i * rows : (i + 1) * rows] * SCALE,
                        r.q_pre[head, at],
                        q_gain,
                        number,
                        16,
                    )
            key_columns = slice(g * wide + repeat * HEAD, g * wide + (repeat + 1) * HEAD)
            value_columns = slice(g * wide + (repeat + 1) * HEAD, (g + 1) * wide)
            for number in range(blocks):
                at = slice(number * rows, (number + 1) * rows)
                grads[at, key_columns] = head_norm_back(
                    grad_keys[at] * SCALE, r.k_pre[g, at], k_gain, number, 17
                )
                grads[at, value_columns] = grad_values[at].astype(BF16)

        def weight_grads(g):
            def body(i, _):
                chunk = collect_a[g].order(i)
                at = pl.ds(pl.multiple_of(chunk * 256, 256), 256)
                tokens = r.normed[:, :, at].reshape(4 * rows, 256)
                grad_wa[at, of_group[g]] = tn(tokens, grads[:, of_group[g]]).astype(BF16)
                collect_a[g].start(chunk, 256)
                return 0

            lax.fori_loop(0, width // 256, body, 0)

        def project(k):
            at = pl.ds(pl.multiple_of(home_back.block(k) * rows, rows), rows)

            def part(i):
                return lambda: nt(grads[at], r.wa_whole[i * 256 : (i + 1) * 256])

            home_back.add(k, [part(i) for i in range(width // 256)])

        for g in range(kv_heads - 1):
            group(g)
            weight_grads(g)
        collect_o.halfway()
        collect_m[2].relay()
        group(kv_heads - 1)
        weight_grads(kv_heads - 1)
        for copy in down_sends:
            copy.wait_recv()
            copy.wait_send()

        def output(at):
            r.output[at] = (r.kept[0, at] + r.down_landed[at].astype(F32)).astype(BF16)

        by_rows(rows, output)
        project(0)
        project(1)
        home_back.settle_outer(0)
        home_back.settle_outer(1)
        project(2)
        project(3)
        for part in collect_a[:-1]:
            part.halfway()
        collect_o.relay()
        home_back.settle_gate(0)
        home_back.settle_gate(1)
        home_back.settle(2)
        home_back.settle(3)
        collect_a[-1].halfway()
        for part in collect_a[:-1]:
            part.relay()
        collect_m[0].result([(r.grad_gate, 0, units, False)])
        collect_m[1].result([(r.grad_up, 0, units, False)])
        home_back.arrive()
        gain = gains_rows(r.gains[...])[0]
        r.gain_rows[...] = jnp.zeros_like(r.gain_rows)

        def norm_one_back(at):
            grad_normed = home_back.value(at)
            unit, scale = unit_of(r.x[at].astype(F32))
            r.gain_rows[...] += jnp.sum(grad_normed * unit, axis=0, keepdims=True)
            scaled = grad_normed * gain
            mean = jnp.mean(scaled * unit, axis=-1, keepdims=True)
            r.input_grad[at] += scale * (scaled - unit * mean)

        by_rows(rows, norm_one_back)
        for i in range(8):
            r.gain_pack[i : i + 1] = r.gain_rows[:, i * 128 : (i + 1) * 128]
        gains_plane.start()
        collect_a[-1].relay()
        r.plane_sum[...] = gains_plane.total()
        gains_tensor.start()
        collect_m[2].result([(r.grad_down, 0, units, turned)])
        collect_o.result([(r.grad_out, 0, nq, turned)])
        total = gains_tensor.total()
        for base, ref in (
            (0, r.grad_gain_one), (8, r.grad_gain_two), (16, r.grad_q_gain), (17, r.grad_k_gain),
        ):
            ref[...] = share(p, total, base, ref.shape[1])
        for g, part in enumerate(collect_a):
            size = repeat * HEAD
            part.result(
                [
                    (r.grad_query, g * size, size, False),
                    (r.grad_key, g * HEAD, HEAD, False),
                    (r.grad_value, g * HEAD, HEAD, False),
                ]
            )
        for part in collect_a:
            part.finish()

    pl.run_scoped(
        attention_back,
        pltpu.VMEM((4 * rows, nq + 2 * nk), BF16),
        pltpu.VMEM((heads, 4 * rows, HEAD), BF16),
        pltpu.VMEM((heads, 1, 4 * rows), F32),
        pltpu.VMEM((4, 2 * rows, rows), F32),
        pltpu.VMEM((4 * rows, HEAD), F32),
        pltpu.VMEM((4 * rows, HEAD), F32),
        pltpu.VMEM((width, nq + 2 * nk), BF16),
    )
    for part in (
        gains_out, gains_plane, gains_tensor, fan_back, quad_ct, home_back, *collect_m, collect_o,
    ):
        part.finish()


def call(dp, tensor, x, starts, gain_one, q_gain, k_gain, gain_two, wq, wk, wv, wo, wg, wu, wd, ct):
    rows, width = x.shape
    tokens = rows * tensor
    shard, nq = wq.shape
    nk, units = wk.shape[1], wg.shape[1]
    heads, kv_heads = nq // HEAD, nk // HEAD
    na, nm = nq + 2 * nk, 3 * units
    turned = shard % 128 == 0
    if not turned:
        wo, wd = wo.T, wd.T
    inputs = dict(
        x=x, starts=starts, gain_one=gain_one, q_gain=q_gain, k_gain=k_gain, gain_two=gain_two,
        wq=wq, wk=wk, wv=wv, wo=wo, wg=wg, wu=wu, wd=wd, ct=ct,
        rotary=jnp.asarray(rotary(tokens)).reshape(tensor, rows, HEAD),
    )
    outputs = dict(
        output=((rows, width), BF16),
        input_grad=((rows, width), F32),
        grad_gain_one=(gain_one.shape, F32),
        grad_q_gain=(q_gain.shape, F32),
        grad_k_gain=(k_gain.shape, F32),
        grad_query=((shard, nq), F32),
        grad_key=((shard, nk), F32),
        grad_value=((shard, nk), F32),
        grad_out=((nq, shard) if turned else (shard, nq), F32),
        grad_gain_two=(gain_two.shape, F32),
        grad_gate=((shard, units), F32),
        grad_up=((shard, units), F32),
        grad_down=((units, shard) if turned else (shard, units), F32),
    )
    scratch = dict(
        pack=((24, 128), F32),
        gain_slots=((dp, 24, 128), F32),
        gains=((24, 128), F32),
        gain_pack=((24, 128), F32),
        gain_rows=((1, width), F32),
        plane_slots=((dp, 24, 128), F32),
        plane_sum=((24, 128), F32),
        tensor_slots=((tensor, 24, 128), F32),
        tokens=((4, rows, width), BF16),
        normed=((4, rows, width), BF16),
        block=((rows, width), BF16),
        q=((heads, tokens, HEAD), BF16),
        k=((kv_heads, tokens, HEAD), BF16),
        v=((kv_heads, tokens, HEAD), BF16),
        q_pre=((heads, tokens, HEAD), F32),
        k_pre=((kv_heads, tokens, HEAD), F32),
        mixed=((tokens, nq), BF16),
        lse=((heads, 1, tokens), F32),
        normed_two=((4, rows, width), BF16),
        ct_whole=((4, rows, width), BF16),
        wa=((shard, na), BF16),
        wa_stage=((shard, na), BF16),
        wa_whole=((width, na), BF16),
        wo_shard=((shard, nq), BF16),
        wo_stage=((shard, nq), BF16),
        wo_whole=((width, nq), BF16),
        wm=((shard, nm), BF16),
        wm_stage=((shard, nm), BF16),
        wm_whole=((width, nm), BF16),
        kept=((2, rows, width), F32),
        passed=((rows, width), BF16),
        given=((2, rows, width), BF16),
        taken=((2, rows, width), BF16),
        summed=((2, rows, width), BF16),
        landed=((2, rows, width), BF16),
        down_landed=((rows, width), BF16),
        back_given=((2, rows, width), BF16),
        back_taken=((2, rows, width), BF16),
        back_summed=((rows, width), BF16),
        back_landed=((rows, width), BF16),
        cm_slots=((dp, shard, nm), BF16),
        cm_landed=((shard, nm), BF16),
        co_slots=((dp, shard, nq), BF16),
        co_landed=((shard, nq), BF16),
        ca_slots=((dp, shard, na), BF16),
        ca_landed=((shard, na), BF16),
    )
    semaphores = [
        *exchange_semaphores(dp),
        *exchange_semaphores(dp),
        *exchange_semaphores(tensor),
        *FAN_SEMAPHORES,
        *FAN_SEMAPHORES,
        *(spread_semaphores(dp) * 5),
        *QUAD_SEMAPHORES,
        *QUAD_SEMAPHORES,
        *HOME_SEMAPHORES,
        *HOME_SEMAPHORES,
        *PAIR_SEMAPHORES,
        *PAIR_SEMAPHORES,
        *(collect_semaphores(dp) * (4 + kv_heads)),
    ]
    names = [*inputs, *outputs, *scratch]

    def body(*refs):
        layer_refs = list(refs)
        layer(dp, tensor, turned, names, *layer_refs)

    in_specs = vmem(len(inputs))
    in_specs[1] = pl.BlockSpec(memory_space=pltpu.SMEM)
    return pl.pallas_call(
        body,
        out_shape=[jax.ShapeDtypeStruct(*s) for s in outputs.values()],
        in_specs=in_specs,
        out_specs=vmem(len(outputs)),
        scratch_shapes=[pltpu.VMEM(*s) for s in scratch.values()] + semaphores,
        compiler_params=params(1),
    )(*inputs.values()), turned


def copies_kernel(count, *refs):
    for source, target in zip(refs[:count], refs[count:]):
        target[...] = source[...]


def copied(arrays):
    return pl.pallas_call(
        functools.partial(copies_kernel, len(arrays)),
        out_shape=[jax.ShapeDtypeStruct(a.shape, a.dtype) for a in arrays],
        in_specs=vmem(len(arrays)),
        out_specs=vmem(len(arrays)),
    )(*arrays)


def shards(dp, tensor, *args):
    x, starts, attn_gain, q_gain, k_gain, wq, wk, wv, wo, mlp_gain, wg, wu, wd, ct = args
    outs, turned = call(
        dp, tensor, x[0], starts, attn_gain[None], q_gain[None], k_gain[None], mlp_gain[None],
        wq, wk, wv, wo, wg, wu, wd, ct[0],
    )
    outs = list(copied(outs))
    for i in (0, 1):
        outs[i] = outs[i][None]
    for i in (2, 3, 4, 9):
        outs[i] = outs[i][0]
    if not turned:
        for i in (8, 12):
            outs[i] = outs[i].T
    return tuple(outs)


def solution(mesh):
    sequence, square, turned = P("dp", "tensor", None), P("dp", "tensor"), P("tensor", "dp")
    gain = P("dp")
    in_specs = (
        sequence, P("dp", None), gain, gain, gain, square, square, square, turned, gain, square, square,
        turned, sequence,
    )
    out_specs = (
        sequence, sequence, gain, gain, gain, square, square, square, turned, gain, square, square,
        turned,
    )
    return jax.shard_map(
        functools.partial(shards, mesh.shape["dp"], mesh.shape["tensor"]),
        mesh=mesh,
        in_specs=in_specs,
        out_specs=out_specs,
        check_vma=False,
    )
```

```python
import functools
import math
import types

import jax
import jax.numpy as jnp
import numpy as np
from jax import lax
from jax.experimental import pallas as pl
from jax.experimental.pallas import tpu as pltpu
from jax.sharding import PartitionSpec as P

HEAD = 128
PIECE = 256
EPS = 1e-06
THETA = 1000000.0
SCALE = HEAD**-0.5
LOG2E = math.log2(math.e)
MESH = pl.DeviceIdType.MESH
F32 = jnp.float32
BF16 = jnp.bfloat16
VMEM_LIMIT = 62 * 2**20


def nt(x, y):
    return lax.dot_general(x, y, (((1,), (1,)), ((), ())), preferred_element_type=F32)


def nn(x, y):
    return lax.dot_general(x, y, (((1,), (0,)), ((), ())), preferred_element_type=F32)


def tn(x, y):
    return lax.dot_general(x, y, (((0,), (0,)), ((), ())), preferred_element_type=F32)


def start(copy):
    copy.start()


def wait(copy):
    copy.wait()


def wait_send(copy):
    copy.wait_send()


def by_rows(rows, act, step=64):
    def body(i, _):
        act(pl.ds(pl.multiple_of(i * step, step), step))
        return 0

    lax.fori_loop(0, rows // step, body, 0)


class Place:
    def __init__(self, dp, tensor):
        self.dp, self.tensor, self.columns = dp, tensor, dp // 2
        self.d = lax.axis_index("dp")
        self.t = lax.axis_index("tensor")
        self.col, self.c = lax.div(self.d, 2), lax.rem(self.d, 2)
        self.a, self.b = lax.div(self.t, 2), lax.rem(self.t, 2)
        self.sibling = self.d + 1 - 2 * self.c
        self.near = self.t + 1 - 2 * self.b
        self.far = self.t + 2 - 4 * self.a

    def barrier(self):
        semaphore = pltpu.get_barrier_semaphore()
        for k in range(1, self.dp):
            pl.semaphore_signal(
                semaphore, 1, device_id=(lax.rem(self.d + k, self.dp), self.t), device_id_type=MESH
            )
        for k in range(1, self.tensor):
            pl.semaphore_signal(
                semaphore,
                1,
                device_id=(self.d, lax.rem(self.t + k, self.tensor)),
                device_id_type=MESH,
            )
        pl.semaphore_wait(semaphore, self.dp + self.tensor - 2)

    def plane(self, bits_a, bits_b):
        first = self.a + bits_a - 2 * self.a * bits_a
        second = self.b + bits_b - 2 * self.b * bits_b
        return 2 * first + second


def remote(source, target, send, receive, device):
    return pltpu.make_async_remote_copy(
        src_ref=source,
        dst_ref=target,
        send_sem=send,
        recv_sem=receive,
        device_id=device,
        device_id_type=MESH,
    )


class Spread:
    def __init__(self, place, shard, stage, whole, send, receive, cross):
        self.p, self.shard, self.stage, self.whole = place, shard, stage, whole
        self.send, self.receive, self.cross = send, receive, cross
        self.rows = shard.shape[0]
        self.square = place.columns == 4
        y, x = lax.div(place.col, 2), lax.rem(place.col, 2)
        if self.square:
            self.side = [2 * y + 1 - x, 2 * (1 - y) + x]
            self.corner = 2 * (1 - y) + 1 - x

    def slot(self, index, half=None):
        size = self.rows if half is None else self.rows // 2
        begin = index * self.rows + (0 if half is None else half * size)
        return self.whole.at[pl.ds(pl.multiple_of(begin, size), size)]

    def crossing(self):
        p = self.p
        return remote(self.shard, self.stage, self.cross.at[0], self.cross.at[1], (p.d, p.far))

    def each(self, phase, act_remote, act_local):
        p = self.p
        source = self.shard if phase == 0 else self.stage
        core = p.a if phase == 0 else 1 - p.a
        columns = (
            [p.col] + self.side
            if self.square
            else [lax.rem(p.col + j, p.columns) for j in range(p.columns)]
        )
        for j, column in enumerate(columns):
            send = self.send.at[phase, j]

            def to_other():
                act_remote(
                    remote(
                        source,
                        self.slot(p.d),
                        send,
                        self.receive.at[p.d, 0],
                        (2 * column + core, p.t),
                    )
                )

            def to_self():
                act_local(pltpu.make_async_copy(source, self.slot(p.d), send))

            if j == 0 and act_local:
                pl.when(core == p.c)(to_self)
            if act_remote:
                if j:
                    to_other()
                else:
                    pl.when(core != p.c)(to_other)

    def start(self, phase):
        self.each(phase, start, start)

    def cross_start(self):
        self.crossing().start()

    def cross_wait(self):
        self.crossing().wait_recv()

    def landed(self, index, half):
        p = self.p
        part = self.slot(index, half)
        remote(
            part, part, self.send.at[0, 0], self.receive.at[index, half or 0], (p.d, p.t)
        ).wait_recv()

    def forwards(self, act):
        p = self.p
        for direction in range(2):
            for core in range(2):
                index = 2 * self.side[direction] + core
                part = self.slot(index, direction)
                act(
                    remote(
                        part,
                        part,
                        self.send.at[2 + direction, core],
                        self.receive.at[index, direction],
                        (2 * self.side[1 - direction] + p.c, p.t),
                    )
                )

    def forward(self):
        if self.square:
            for direction in range(2):
                for core in range(2):
                    self.landed(2 * self.side[direction] + core, None)
            self.forwards(start)

    def wait_whole(self):
        p = self.p
        self.each(0, None, wait)
        self.each(1, None, wait)
        if self.square:
            self.landed(p.sibling, None)
            for core in range(2):
                for half in range(2):
                    self.landed(2 * self.corner + core, half)
        else:
            for k in range(1, p.dp):
                self.landed(lax.rem(p.d + k, p.dp), None)

    def cross_sent(self):
        self.crossing().wait_send()

    def wait_sends(self):
        self.each(0, wait_send, None)
        self.each(1, wait_send, None)
        if self.square:
            self.forwards(wait_send)


def spread_semaphores(dp):
    return [
        pltpu.SemaphoreType.DMA((4, max(dp // 2, 4))),
        pltpu.SemaphoreType.DMA((dp, 2)),
        pltpu.SemaphoreType.DMA((2,)),
    ]


class Fan:
    PIECES = 4

    def __init__(self, place, block, whole, send, receive, onward):
        self.p, self.block, self.whole = place, block, whole
        self.send, self.receive, self.onward = send, receive, onward
        self.slots = [place.plane(k // 2, k % 2) for k in range(4)]
        self.rows = block.shape[0] // self.PIECES

    def first_hop(self, act, pieces):
        p = self.p
        plane = lax.select(p.a == p.c, p.near, p.c + 1)
        for piece in pieces:
            at = pl.ds(piece * self.rows, self.rows)
            act(
                remote(
                    self.block.at[at],
                    self.whole.at[p.t, at],
                    self.send.at[piece],
                    self.receive.at[p.t, piece],
                    (p.d, plane),
                )
            )

    def start(self, piece=None):
        p = self.p
        pieces = range(self.PIECES) if piece is None else [piece]
        self.first_hop(start, pieces)

        @pl.when(p.a == p.c)
        def _():
            for piece in pieces:
                at = pl.ds(piece * self.rows, self.rows)
                self.whole[p.t, at] = self.block[at]

    def hop(self, index, piece, device, row):
        part = self.whole.at[self.slots[index], pl.ds(piece * self.rows, self.rows)]
        return remote(
            part,
            part,
            self.onward.at[row, index, piece],
            self.receive.at[self.slots[index], piece],
            device,
        )

    def to_sibling(self, index, piece):
        return self.hop(index, piece, (self.p.sibling, self.p.t), 0)

    def to_near(self, index, piece):
        return self.hop(index, piece, (self.p.d, self.p.near), 1)

    def take(self, *indices):
        p = self.p
        for piece in range(self.PIECES):
            for index in indices:

                def arrived():
                    self.to_sibling(index, piece).wait_recv()

                if index == 0:
                    pl.when(p.a != p.c)(arrived)
                else:
                    arrived()

                @pl.when(p.a == p.c)
                def _():
                    if index >= 2:
                        pl.when(p.t == p.c + 1)(lambda: self.to_near(index, piece).start())
                    self.to_sibling(index, piece).start()

    def finish(self):
        p = self.p
        self.first_hop(wait_send, range(self.PIECES))

        @pl.when(p.a == p.c)
        def _():
            for index in range(4):
                for piece in range(self.PIECES):
                    self.to_sibling(index, piece).wait_send()
                    if index >= 2:
                        pl.when(p.t == p.c + 1)(lambda: self.to_near(index, piece).wait_send())


FAN_SEMAPHORES = [
    pltpu.SemaphoreType.DMA((Fan.PIECES,)),
    pltpu.SemaphoreType.DMA((4, Fan.PIECES)),
    pltpu.SemaphoreType.DMA((2, 4, Fan.PIECES)),
]


def gains_rows(total):
    one = jnp.concatenate([total[i : i + 1] for i in range(8)], axis=1)
    two = jnp.concatenate([total[i : i + 1] for i in range(8, 16)], axis=1)
    return one, two, total[16:17], total[17:18]


def unit_of(values):
    scale = lax.rsqrt(jnp.mean(values * values, axis=-1, keepdims=True) + EPS)
    return values * scale, scale


class Home:
    PIECES = 4

    def __init__(self, place, kept, given, taken, summed, landed, passed, semaphores):
        self.p = place
        self.kept, self.given, self.taken, self.summed, self.landed = kept, given, taken, summed, landed
        self.passed = passed
        self.given_send, self.taken_receive, self.summed_send, self.landed_receive, self.passing = (
            semaphores
        )
        self.rows = landed.shape[1] // self.PIECES
        self.gate = place.t == place.a + 1

    def block(self, k):
        k = 3 - k
        return self.p.plane(k // 2, k % 2)

    def mine(self, k):
        return self.p.c == (self.p.b if k % 2 else 1 - self.p.b)

    def give(self, slot):
        return remote(
            self.given.at[slot],
            self.taken.at[slot],
            self.given_send.at[slot],
            self.taken_receive.at[slot],
            (self.p.sibling, self.p.t),
        )

    def at(self, piece):
        return pl.ds(piece * self.rows, self.rows)

    def send(self, k, piece):
        p = self.p
        return remote(
            self.summed.at[k // 2, self.at(piece)],
            self.landed.at[p.b, self.at(piece)],
            self.summed_send.at[k // 2, piece],
            self.landed_receive.at[p.b, piece],
            (2 * p.col + p.a, self.block(k)),
        )

    def to_gate(self, piece):
        p = self.p
        return remote(
            self.summed.at[0, self.at(piece)],
            self.passed.at[self.at(piece)],
            self.passing.at[0, piece],
            self.passing.at[1, piece],
            (p.d, p.near),
        )

    def add(self, k, parts):
        @pl.when(self.mine(k))
        def _():
            for i, part in enumerate(parts):
                self.kept[k // 2, :, i * 256 : (i + 1) * 256] = part()

        @pl.when(jnp.logical_not(self.mine(k)))
        def _():
            for i, part in enumerate(parts):
                self.given[k // 2, :, i * 256 : (i + 1) * 256] = part().astype(BF16)
            self.give(k // 2).start()

    def total(self, k, piece):
        at = self.at(piece)
        return self.kept[k // 2, at] + self.taken[k // 2, at].astype(F32)

    def settle_outer(self, k):
        @pl.when(jnp.logical_and(self.mine(k), jnp.logical_not(self.gate)))
        def _():
            self.give(0).wait_recv()
            for piece in range(self.PIECES):
                self.summed[0, self.at(piece)] = self.total(k, piece).astype(BF16)
                self.to_gate(piece).start()

    def settle_gate(self, k):
        @pl.when(jnp.logical_and(self.mine(k), self.gate))
        def _():
            self.give(0).wait_recv()
            for piece in range(self.PIECES):
                at = self.at(piece)
                self.to_gate(piece).wait_recv()
                self.summed[0, at] = (
                    self.total(k, piece) + self.passed[at].astype(F32)
                ).astype(BF16)
                self.send(k, piece).start()

    def settle(self, k):
        p = self.p

        @pl.when(self.mine(k))
        def _():
            self.give(1).wait_recv()
            stays = jnp.logical_and(p.a == p.c, jnp.asarray(k == 3))

            @pl.when(stays)
            def _():
                for piece in range(self.PIECES):
                    self.landed[p.b, self.at(piece)] = self.total(k, piece).astype(BF16)

            @pl.when(jnp.logical_not(stays))
            def _():
                for piece in range(self.PIECES):
                    self.summed[1, self.at(piece)] = self.total(k, piece).astype(BF16)
                    self.send(k, piece).start()

    def arrive(self):
        p = self.p

        def arrived(slot):
            for piece in range(self.PIECES):
                part = self.landed.at[slot, self.at(piece)]
                remote(
                    part,
                    part,
                    self.summed_send.at[0, piece],
                    self.landed_receive.at[slot, piece],
                    (p.d, p.t),
                ).wait_recv()

        @pl.when(p.a == p.c)
        def _():
            arrived(1 - p.b)
            pl.when(p.c != p.b)(lambda: arrived(p.b))

        @pl.when(p.a != p.c)
        def _():
            self.landed[p.c] = jnp.zeros(self.landed.shape[1:], BF16)
            arrived(1 - p.c)

    def value(self, at):
        return self.landed[0, at].astype(F32) + self.landed[1, at].astype(F32)

    def finish(self):
        for k in range(4):

            @pl.when(jnp.logical_not(self.mine(k)))
            def _():
                self.give(k // 2).wait_send()

            sent = self.mine(k)
            if k == 3:
                sent = jnp.logical_and(sent, self.p.a != self.p.c)
            if k < 2:
                sent = jnp.logical_and(sent, self.gate)

                @pl.when(jnp.logical_and(self.mine(k), jnp.logical_not(self.gate)))
                def _():
                    for piece in range(self.PIECES):
                        self.to_gate(piece).wait_send()

            @pl.when(sent)
            def _():
                for piece in range(self.PIECES):
                    self.send(k, piece).wait_send()


HOME_SEMAPHORES = [
    pltpu.SemaphoreType.DMA((2,)),
    pltpu.SemaphoreType.DMA((2,)),
    *[pltpu.SemaphoreType.DMA((2, Home.PIECES))] * 3,
]


class Quad:
    def __init__(self, place, block, whole, send, receive):
        self.p, self.whole_block, self.whole, self.sent, self.receive = place, block, whole, send, receive
        b, c = place.b, place.c
        self.slots = [2 * b + c, 2 * b + 1 - c, 2 * (1 - b) + c, 2 * (1 - b) + 1 - c]

    def copy(self, index, source, slot, device):
        return remote(
            source, self.whole.at[slot], self.sent.at[index], self.receive.at[slot], device
        )

    def near(self):
        p = self.p
        return self.copy(0, self.whole_block, self.slots[0], (p.d, p.near))

    def beside(self):
        p = self.p
        return self.copy(1, self.whole_block, self.slots[0], (p.sibling, p.t))

    def onward(self):
        p = self.p
        return self.copy(2, self.whole.at[self.slots[2]], self.slots[2], (p.sibling, p.t))

    def start(self):
        self.near().start()
        self.beside().start()
        self.whole[self.slots[0]] = self.whole_block[...]

    def take(self, index):
        slot = self.slots[index]
        self.copy(0, self.whole_block, slot, (self.p.d, self.p.near)).wait_recv()
        if index == 2:
            self.onward().start()

    def finish(self):
        self.near().wait_send()
        self.beside().wait_send()
        self.onward().wait_send()


QUAD_SEMAPHORES = [pltpu.SemaphoreType.DMA((3,)), pltpu.SemaphoreType.DMA((4,))]


class PairSum:
    def __init__(self, place, kept, given, taken, summed, landed, given_send, taken_receive, across):
        self.p = place
        self.kept, self.given, self.taken, self.summed, self.landed = kept, given, taken, summed, landed
        self.given_send, self.taken_receive, self.across = given_send, taken_receive, across

    def give(self, half):
        return remote(
            self.given.at[half],
            self.taken.at[half],
            self.given_send.at[half],
            self.taken_receive.at[half],
            (self.p.sibling, self.p.t),
        )

    PIECES = 4

    def at(self, piece):
        size = self.summed.shape[0] // self.PIECES
        return pl.ds(piece * size, size)

    def send(self, piece):
        p = self.p
        return remote(
            self.summed.at[self.at(piece)],
            self.landed.at[self.at(piece)],
            self.across.at[0, piece],
            self.across.at[1, piece],
            (p.d, p.near),
        )

    def add_far(self, send):
        self.give(1).wait_recv()
        for piece in range(self.PIECES):
            at = self.at(piece)
            self.summed[at] = (self.kept[1, at] + self.taken[1, at].astype(F32)).astype(BF16)
            if send:
                self.send(piece).start()

    def take_own(self):
        self.give(0).wait_recv()

    def own(self, at):
        return self.kept[0, at] + self.taken[0, at].astype(F32)

    def finish(self):
        self.give(0).wait_send()
        self.give(1).wait_send()


PAIR_SEMAPHORES = [
    pltpu.SemaphoreType.DMA((2,)),
    pltpu.SemaphoreType.DMA((2,)),
    pltpu.SemaphoreType.DMA((2, PairSum.PIECES)),
]


class Collect:
    def __init__(self, place, source, slots, summed, landed, send, receive, across):
        self.p, self.source, self.slots, self.summed, self.landed = place, source, slots, summed, landed
        self.send, self.receive, self.across = send, receive, across
        self.rows = slots.shape[1]

    def part(self, index):
        return self.source.at[pl.ds(pl.multiple_of(index * self.rows, self.rows), self.rows)]

    def own(self):
        p = self.p
        return pltpu.make_async_copy(self.part(p.d), self.slots.at[p.d], self.send.at[0, p.d])

    def other(self, target):
        p = self.p
        return remote(
            self.part(target),
            self.slots.at[p.d],
            self.send.at[0, target],
            self.receive.at[0, p.d],
            (target, p.t),
        )

    def start(self, chunk, size):
        count = size // self.rows

        def body(i, _):
            target = chunk * count + i
            pl.when(target == self.p.d)(lambda: self.own().start())
            pl.when(target != self.p.d)(lambda: self.other(target).start())
            return 0

        lax.fori_loop(0, count, body, 0)

    def cross(self):
        p = self.p
        return remote(self.summed, self.landed, self.across.at[0], self.across.at[1], (p.d, p.far))

    def total(self, core, here):
        return lax.fori_loop(
            1,
            self.p.columns,
            lambda i, s: s + self.slots[2 * i + core, :, here].astype(F32),
            self.slots[core, :, here].astype(F32),
        )

    def gathered(self):
        p = self.p
        self.own().wait()
        for k in range(1, p.dp):
            source = lax.rem(p.d + k, p.dp)
            remote(
                self.part(source),
                self.slots.at[source],
                self.send.at[0, source],
                self.receive.at[0, source],
                (p.d, p.t),
            ).wait_recv()

    def relay(self):
        self.gathered()
        for begin in range(0, self.summed.shape[1], 256):
            here = slice(begin, begin + 256)
            self.summed[:, here] = self.total(1 - self.p.a, here).astype(BF16)
        self.cross().start()

    def result(self, targets):
        self.cross().wait_recv()
        begin = 0
        for target, first, count, turned in targets:
            for offset in range(0, count, min(count, 256)):
                size = min(count, 256)
                here = slice(begin, begin + size)
                there = slice(first + offset, first + offset + size)
                value = self.total(self.p.a, here) + self.landed[:, here].astype(F32)
                if turned:
                    target[there] = value.T
                else:
                    target[:, there] = value
                begin += size

    def order(self, i):
        count = self.source.shape[0] // 256
        return lax.rem(i + 1 + self.p.col, count)

    def halfway(self):
        pass

    def finish(self):
        p = self.p
        for k in range(1, p.dp):
            self.other(lax.rem(p.d + k, p.dp)).wait_send()
        self.cross().wait_send()


class SquareCollect(Collect):
    def __init__(self, place, *refs):
        super().__init__(place, *refs)
        y, x = lax.div(place.col, 2), lax.rem(place.col, 2)
        self.side = [2 * y + 1 - x, 2 * (1 - y) + x]
        self.corner = 2 * (1 - y) + 1 - x
        self.half = self.rows // 2

    def order(self, i):
        columns = [self.corner, self.side[0], self.side[1], self.p.col]
        result = columns[3]
        for k in range(3):
            result = lax.select(i == k, columns[k], result)
        return result

    def rows_of(self, column, core, direction):
        begin = (2 * column + core) * self.rows + direction * self.half
        return self.source.at[pl.ds(pl.multiple_of(begin, self.half), self.half)]

    def first(self, column, direction, beyond, core):
        p = self.p
        number = 4 * direction + 2 * beyond + core
        return remote(
            self.rows_of(column, core, direction),
            self.slots.at[4 + 2 * beyond + core, pl.ds(direction * self.half, self.half)],
            self.send.at[0, number],
            self.receive.at[0, number],
            (2 * self.side[direction] + p.c, p.t),
        )

    def firsts(self, column, kind, act):
        for direction in range(2):
            for core in range(2):
                if kind == 0:
                    act(self.first(column, direction, 1, core))
                elif kind == direction + 1:
                    act(self.first(column, direction, 0, core))

    def start(self, chunk, size):
        p = self.p
        pl.when(chunk == self.corner)(lambda: self.firsts(chunk, 0, start))
        for direction in range(2):
            pl.when(chunk == self.side[direction])(
                functools.partial(self.firsts, chunk, direction + 1, start)
            )

    def seconds(self, act):
        p = self.p
        for direction in range(2):
            here = pl.ds(direction * self.half, self.half)
            for core in range(2):
                act(
                    remote(
                        self.rows_of(self.side[1 - direction], core, direction),
                        self.slots.at[2 * p.c + 1, here],
                        self.send.at[1, 2 + 2 * direction + core],
                        self.receive.at[1, 2 + 2 * direction + p.c],
                        (2 * self.side[1 - direction] + core, p.t),
                    )
                )
        act(
            remote(
                self.part(p.sibling),
                self.slots.at[2 * p.c],
                self.send.at[1, 1],
                self.receive.at[1, p.c],
                (p.sibling, p.t),
            )
        )

    def own(self):
        p = self.p
        return pltpu.make_async_copy(self.part(p.d), self.slots.at[2 * p.c], self.send.at[1, 0])

    def halfway(self):
        p = self.p
        for direction in range(2):
            here = pl.ds(direction * self.half, self.half)
            for beyond in range(2):
                for core in range(2):
                    number = 4 * direction + 2 * beyond + core
                    slot = self.slots.at[4 + 2 * beyond + core, here]
                    remote(
                        slot,
                        slot,
                        self.send.at[0, number],
                        self.receive.at[0, number],
                        (p.d, p.t),
                    ).wait_recv()
                    column = self.side[1 - direction] if beyond else p.col
                    target = self.rows_of(column, core, direction)
                    total = target[...].astype(F32) + slot[...].astype(F32)
                    target[...] = total.astype(BF16)
        self.seconds(start)
        self.own().start()

    def gathered(self):
        p = self.p
        self.own().wait()

        def arrived(slot, number):
            remote(
                slot, slot, self.send.at[1, 0], self.receive.at[1, number], (p.d, p.t)
            ).wait_recv()

        arrived(self.slots.at[2 * (1 - p.c)], 1 - p.c)
        for direction in range(2):
            here = pl.ds(direction * self.half, self.half)
            for core in range(2):
                arrived(self.slots.at[2 * core + 1, here], 2 + 2 * direction + core)

    def total(self, core, here):
        return self.slots[2 * core, :, here].astype(F32) + self.slots[2 * core + 1, :, here].astype(
            F32
        )

    def finish(self):
        self.firsts(self.corner, 0, wait_send)
        for direction in range(2):
            self.firsts(self.side[direction], direction + 1, wait_send)
        self.seconds(wait_send)
        self.cross().wait_send()


def collect_semaphores(dp):
    return [
        pltpu.SemaphoreType.DMA((2, max(dp, 8))),
        pltpu.SemaphoreType.DMA((2, max(dp, 8))),
        pltpu.SemaphoreType.DMA((2,)),
    ]


def vmem(count):
    return [pl.BlockSpec(memory_space=pltpu.VMEM)] * count


def params(identity):
    return pltpu.CompilerParams(
        collective_id=identity, has_side_effects=True, vmem_limit_bytes=VMEM_LIMIT
    )


def rotary(tokens):
    frequency = np.float32(THETA) ** (
        -(np.arange(HEAD // 2, dtype=np.float32) * np.float32(2.0)) / np.float32(HEAD)
    )
    angles = np.arange(tokens, dtype=np.float32)[:, None] * frequency.astype(np.float32)[None, :]
    return np.concatenate([np.cos(angles), np.sin(angles)], axis=1).astype(np.float32)


def rotary_rows(table):
    other = pltpu.roll(table, HEAD // 2, 1)
    low = lax.broadcasted_iota(jnp.int32, (1, HEAD), 1) < HEAD // 2
    return jnp.where(low, table, other), jnp.where(low, -other, table)


def allowed_mask(place, gains, base, rows, keys, transposed):
    lane = lax.broadcasted_iota(jnp.int32, (1, 128), 1)
    chosen = (lane == 2 * place.col + place.a).astype(F32)
    shape = (keys, rows) if transposed else (rows, keys)
    query_dim, key_dim = (1, 0) if transposed else (0, 1)
    line = lambda dim: tuple(n if i == dim else 1 for i, n in enumerate(shape))
    query = lax.broadcasted_iota(jnp.int32, shape, query_dim)
    key = lax.broadcasted_iota(jnp.int32, shape, key_dim)
    mask = (key <= query).astype(F32)
    for piece in range(2):
        numbers = gains[18 + piece : 19 + piece]
        first_position = jnp.sum(numbers * chosen, axis=1, keepdims=True) - base.astype(F32)

        def inside(position):
            position = position.astype(F32)
            return jnp.logical_and(
                position >= first_position, position < first_position + PIECE
            ).astype(F32)

        in_query = inside(lax.broadcasted_iota(jnp.int32, line(query_dim), query_dim))
        in_key = inside(lax.broadcasted_iota(jnp.int32, line(key_dim), key_dim))
        mask = jnp.maximum(mask, in_query * in_key)
    return mask


def placed(place, values, base):
    size = values.shape[1]
    begin = place.d * size
    if size < 128:
        values = jnp.concatenate([values, jnp.zeros((1, 128 - size), F32)], axis=1)
        values = pltpu.roll(values, lax.rem(begin, 128), 1)
    row = lax.broadcasted_iota(jnp.int32, (24, 128), 0)
    return jnp.where(row == base + lax.div(begin, 128), values, 0.0)


def share(place, tile, base, size):
    begin = place.d * size
    row = lax.broadcasted_iota(jnp.int32, (24, 128), 0)
    chosen = jnp.where(row == base + lax.div(begin, 128), tile, 0.0)
    values = jnp.sum(chosen, axis=0, keepdims=True)
    if size < 128:
        values = pltpu.roll(values, lax.rem(128 - lax.rem(begin, 128), 128), 1)
    return values[:, :size]


class Exchange:
    def __init__(self, place, tile, slots, send, receive, in_plane):
        self.p, self.tile, self.slots, self.in_plane = place, tile, slots, in_plane
        self.sent, self.receive = send, receive
        self.count = place.dp if in_plane else place.tensor
        self.me = place.d if in_plane else place.t

    def copy(self, k, slot):
        p = self.p
        other = lax.rem(self.me + k, self.count)
        device = (other, p.t) if self.in_plane else (p.d, other)
        return remote(
            self.tile, self.slots.at[slot], self.sent.at[k], self.receive.at[slot], device
        )

    def start(self):
        for k in range(1, self.count):
            self.copy(k, self.me).start()
        self.slots[self.me] = self.tile[...]

    def total(self):
        for k in range(1, self.count):
            self.copy(k, lax.rem(self.me + k, self.count)).wait_recv()
        return lax.fori_loop(1, self.count, lambda i, s: s + self.slots[i], self.slots[0])

    def finish(self):
        for k in range(1, self.count):
            self.copy(k, self.me).wait_send()


def exchange_semaphores(count):
    return [pltpu.SemaphoreType.DMA((count,)), pltpu.SemaphoreType.DMA((count,))]


def layer(dp, tensor, turned, names, *refs):
    r = types.SimpleNamespace(**dict(zip(names, refs)))
    rest = list(refs[len(names) :])

    def take(count):
        head, rest[:] = rest[:count], rest[count:]
        return head

    p = Place(dp, tensor)
    gains_out = Exchange(p, r.pack, r.gain_slots, *take(2), True)
    gains_plane = Exchange(p, r.gain_pack, r.plane_slots, *take(2), True)
    gains_tensor = Exchange(p, r.plane_sum, r.tensor_slots, *take(2), False)
    fan = Fan(p, r.x, r.tokens, *take(3))
    fan_back = Fan(p, r.block, r.tokens, *take(3))
    spread_a = Spread(p, r.wa, r.wa_stage, r.wa_whole, *take(3))
    spread_o = Spread(p, r.wo_shard, r.wo_stage, r.wo_whole, *take(3))
    units = r.wg.shape[1]
    thirds = [slice(i * units, (i + 1) * units) for i in range(3)]
    spread_m = [
        Spread(p, r.wm.at[:, c], r.wm_stage.at[:, c], r.wm_whole.at[:, c], *take(3)) for c in thirds
    ]
    quad_ct = Quad(p, r.ct, r.ct_whole, *take(2))
    quad = Quad(p, r.block, r.normed_two, *take(2))
    home_buffers = (r.kept, r.given, r.taken, r.summed, r.landed, r.passed)
    home = Home(p, *home_buffers, take(5))
    home_back = Home(p, *home_buffers, take(5))
    down_semaphores, back_semaphores = take(3), take(3)
    collect = SquareCollect if dp == 8 else Collect
    collect_m = [
        collect(
            p, r.wm_whole.at[:, c], r.cm_slots.at[:, :, c], r.wm.at[:, c], r.cm_landed.at[:, c], *take(3)
        )
        for c in thirds
    ]
    collect_o = collect(p, r.wo_whole, r.co_slots, r.wo_shard, r.co_landed, *take(3))
    rows, width = r.x.shape
    nq, nk = r.wq.shape[1], r.wk.shape[1]
    heads, kv_heads, blocks = nq // HEAD, nk // HEAD, 4
    repeat = heads // kv_heads
    wide = (repeat + 2) * HEAD
    of_group = [slice(g * wide, (g + 1) * wide) for g in range(kv_heads)]
    collect_a_semaphores = [take(3) for _ in of_group]

    tile = jnp.zeros((24, 128), F32)
    for base, ref in ((0, r.gain_one), (8, r.gain_two), (16, r.q_gain), (17, r.k_gain)):
        tile = tile + placed(p, ref[...].astype(F32), base)
    row = lax.broadcasted_iota(jnp.int32, (24, 128), 0)
    lane = lax.broadcasted_iota(jnp.int32, (24, 128), 1)
    for piece in range(2):
        here = jnp.logical_and(row == 18 + piece, lane == p.d)
        tile = tile + jnp.where(here, r.starts[0, piece], 0).astype(F32)
    r.pack[...] = tile
    for g in range(kv_heads):
        begin = g * wide
        for ref, size in ((r.wq, repeat * HEAD), (r.wk, HEAD), (r.wv, HEAD)):
            r.wa[:, begin : begin + size] = ref[:, g * size : (g + 1) * size]
            begin += size
    p.barrier()
    gains_out.start()
    spread_a.cross_start()
    pl.when(p.a == p.c)(fan.start)
    spread_a.start(0)

    def turn(target, source, begin):
        if source.shape[0] == target.shape[0]:
            target[:, begin : begin + source.shape[1]] = source[...]
        else:
            for i in range(0, source.shape[0], 128):
                target[:, begin + i : begin + i + 128] = source[i : i + 128].T

    turn(r.wo_shard, r.wo, 0)
    r.wm[:, :units] = r.wg[...]
    r.wm[:, units : 2 * units] = r.wu[...]
    turn(r.wm, r.wd, 2 * units)
    total = gains_out.total()
    r.gains[...] = total
    gain_one, gain_two, q_gain, k_gain = gains_rows(total)
    def normalize(slot):
        def act(at):
            unit, _ = unit_of(r.tokens[slot, at].astype(F32))
            r.normed[slot, at] = (unit * gain_one).astype(BF16)

        by_rows(rows, act)

    fan.take(0)
    spread_a.cross_sent()
    pl.when(p.a != p.c)(fan.start)
    spread_a.cross_wait()
    spread_a.start(1)
    spread_o.start(0)
    fan.take(1)
    spread_a.forward()
    normalize(fan.slots[0])
    normalize(fan.slots[1])
    fan.take(2, 3)
    spread_o.cross_start()
    quad_ct.start()
    for part in spread_m:
        part.start(0)
    normalize(fan.slots[2])
    normalize(fan.slots[3])
    spread_a.wait_whole()
    fan.finish()
    spread_a.wait_sends()

    def attention(v_wide, mask):
        v_wide[:, :, HEAD:] = jnp.ones((kv_heads, rows * 4, HEAD), BF16)

        def qkv(slot, _):
            at = pl.ds(pl.multiple_of(slot * rows, rows), rows)
            cosine, sine = rotary_rows(r.rotary[slot])

            def rotated(values, gain):
                unit_values, _ = unit_of(values)
                scaled = unit_values * gain
                return (scaled * cosine + pltpu.roll(scaled, 64, 1) * sine).astype(BF16)

            for g in range(kv_heads):
                for i in range(0, repeat + 2, 2):
                    begin = g * wide + i * HEAD
                    product = nn(r.normed[slot], r.wa_whole[:, begin : begin + 2 * HEAD])
                    for j in range(2):
                        values = product[:, j * HEAD : (j + 1) * HEAD]
                        if i + j < repeat:
                            r.q_pre[g * repeat + i + j, at] = values
                            r.q[g * repeat + i + j, at] = rotated(values, q_gain)
                        elif i + j == repeat:
                            r.k_pre[g, at] = values
                            r.k[g, at] = rotated(values, k_gain)
                        else:
                            v_wide[g, at, :HEAD] = values.astype(BF16)
            return 0

        lax.fori_loop(0, 4, qkv, 0)

        def attend(k):
            block = home.block(k)
            mask[...] = allowed_mask(p, r.gains[...], block * rows, rows, 2 * rows, False)
            for number in range(blocks):

                @pl.when(block == number)
                def _():
                    at = slice(number * rows, (number + 1) * rows)

                    def group(g, _):
                        queries = r.q[pl.ds(g * repeat, repeat), at].reshape(repeat * rows, HEAD)
                        total = jnp.zeros((repeat * rows, 2 * HEAD), F32)
                        for kb in range(min(number + 2, blocks)):
                            keys = slice(kb * rows, (kb + 1) * rows)
                            weight = jnp.exp2(nt(queries, r.k[g, keys]) * (SCALE * LOG2E))
                            if kb >= number:
                                part = mask[:, (kb - number) * rows : (kb - number + 1) * rows]
                                weight = weight * jnp.concatenate([part] * repeat, axis=0)
                            total = total + nn(weight.astype(BF16), v_wide[g, keys])
                        summed = total[:, HEAD:]
                        result = (total[:, :HEAD] / summed).astype(BF16)
                        result = jnp.concatenate(
                            [result[i * rows : (i + 1) * rows] for i in range(repeat)], axis=1
                        )
                        size = repeat * HEAD
                        r.mixed[at, pl.ds(pl.multiple_of(g * size, size), size)] = result
                        logs = jnp.log2(summed)
                        for i in range(repeat):
                            across = logs[i * rows : (i + 1) * rows].T
                            r.lse[g * repeat + i, :, at] = across[0:1]
                        return 0

                    lax.fori_loop(0, kv_heads, group, 0)

        def project(k):
            at = pl.ds(pl.multiple_of(home.block(k) * rows, rows), rows)

            def part(i):
                return lambda: nt(r.mixed[at], r.wo_whole[i * 256 : (i + 1) * 256])

            home.add(k, [part(i) for i in range(width // 256)])

        spread_o.cross_wait()
        spread_o.start(1)
        spread_m[0].cross_start()
        attend(0)
        attend(1)
        spread_m[1].cross_start()
        spread_o.forward()
        spread_o.wait_whole()
        project(0)
        project(1)
        home.settle_outer(0)
        home.settle_outer(1)
        attend(2)
        project(2)
        spread_m[0].cross_wait()
        spread_m[0].start(1)
        spread_m[2].cross_start()
        attend(3)
        project(3)
        home.settle_gate(0)
        home.settle_gate(1)
        home.settle(2)
        home.settle(3)
        r.v[...] = v_wide[:, :, :HEAD]

    pl.run_scoped(
        attention,
        pltpu.VMEM((kv_heads, 4 * rows, 2 * HEAD), BF16),
        pltpu.VMEM((rows, 2 * rows), F32),
    )
    spread_m[0].forward()
    spread_m[1].cross_wait()
    spread_m[1].start(1)
    quad_ct.take(1)
    quad_ct.take(2)
    spread_m[2].cross_wait()
    spread_m[2].start(1)
    home.arrive()

    def norm_two(at):
        hidden = r.x[at].astype(F32) + home.value(at)
        r.kept[0, at] = hidden
        unit, _ = unit_of(hidden)
        r.block[at] = (unit * gain_two).astype(BF16)

    by_rows(rows, norm_two)
    quad.start()
    spread_m[1].forward()
    quad_ct.take(3)
    quad.take(1)
    quad.take(2)
    quad.take(3)
    spread_m[2].forward()
    quad.finish()
    home.finish()
    spread_o.cross_sent()
    spread_o.wait_sends()
    for part in spread_m:
        part.wait_whole()
    for part in spread_m:
        part.cross_sent()
        part.wait_sends()

    def feed_forward(active, grad_gate, grad_up, down_kept, back_kept):
        down = PairSum(
            p, down_kept, r.given, r.taken, r.summed.at[0], r.down_landed, *down_semaphores
        )
        back = PairSum(
            p, back_kept, r.back_given, r.back_taken, r.back_summed, r.back_landed, *back_semaphores
        )
        wm = r.wm_whole

        def work(slot, keep, half):
            tokens, cotangent = r.normed_two[slot], r.ct_whole[slot]
            at = pl.ds(pl.multiple_of(slot * rows, rows), rows)
            for i in range(units // 256):
                here = slice(i * 256, (i + 1) * 256)
                gate = nn(tokens, wm[:, i * 256 : (i + 1) * 256])
                upward = nn(tokens, wm[:, units + i * 256 : units + (i + 1) * 256])
                grad = nn(cotangent, wm[:, 2 * units + i * 256 : 2 * units + (i + 1) * 256])
                sigmoid = 1.0 / (1.0 + jnp.exp2(gate * -LOG2E))
                silu = gate * sigmoid
                active[at, here] = (silu * upward).astype(BF16)
                grad_gate[at, here] = (
                    grad * upward * sigmoid * (1.0 + gate * (1.0 - sigmoid))
                ).astype(BF16)
                grad_up[at, here] = (grad * silu).astype(BF16)
            for i in range(width // 256):
                here = slice(i * 256, (i + 1) * 256)
                out = nt(grad_gate[at], wm[here, :units]) + nt(
                    grad_up[at], wm[here, units : 2 * units]
                )
                if keep:
                    back.kept[half, :, here] = out
                else:
                    back.given[half, :, here] = out.astype(BF16)
            if not keep:
                back.give(half).start()
            for i in range(width // 256):
                here = slice(i * 256, (i + 1) * 256)
                out = nt(active[at], wm[here, 2 * units :])
                if keep:
                    down.kept[half, :, here] = out
                else:
                    down.given[half, :, here] = out.astype(BF16)
            if not keep:
                down.give(half).start()

        def both(step, _):
            half = 1 - step
            other = lax.select(half == 1, 1 - p.b, p.b)
            work(2 * other + p.c, True, half)
            work(2 * other + 1 - p.c, False, half)

            @pl.when(half == 1)
            def _():
                back.add_far(True)

            return 0

        lax.fori_loop(0, 2, both, 0)

        def weight_grads(third, tokens_ref, grad):
            def body(i, _):
                chunk = collect_m[third].order(i)
                at = pl.ds(pl.multiple_of(chunk * 256, 256), 256)
                tokens = tokens_ref[:, :, at].reshape(4 * rows, 256)
                wm[at, thirds[third]] = tn(tokens, grad[...]).astype(BF16)
                collect_m[third].start(chunk, 256)
                return 0

            lax.fori_loop(0, width // 256, body, 0)

        weight_grads(0, r.normed_two, grad_gate)
        down.add_far(False)
        down.take_own()
        back.take_own()
        gain = gains_rows(r.gains[...])[1]
        r.gain_rows[...] = jnp.zeros_like(r.gain_rows)

        def norm_two_back(at):
            grad_normed = back.own(at) + back.landed[at].astype(F32)
            unit, scale = unit_of(r.kept[0, at])
            r.gain_rows[...] += jnp.sum(grad_normed * unit, axis=0, keepdims=True)
            scaled = grad_normed * gain
            mean = jnp.mean(scaled * unit, axis=-1, keepdims=True)
            grad = r.ct[at].astype(F32) + scale * (scaled - unit * mean)
            r.input_grad[at] = grad
            r.block[at] = grad.astype(BF16)

        for piece in range(back.PIECES):
            back.send(piece).wait_recv()
            norm_two_back(back.at(piece))
            fan_back.start(piece)
        fan_back.take(0)

        def hidden_sum(at):
            r.kept[0, at] += down.own(at)

        by_rows(rows, hidden_sum)
        weight_grads(1, r.normed_two, grad_up)
        fan_back.take(1)
        weight_grads(2, r.ct_whole, active)
        for i in range(8):
            r.gain_pack[8 + i : 9 + i] = r.gain_rows[:, i * 128 : (i + 1) * 128]
        collect_m[0].halfway()
        fan_back.take(2, 3)
        collect_m[1].halfway()
        collect_m[0].relay()
        for piece in range(back.PIECES):
            back.send(piece).wait_send()
        back.finish()
        down.finish()

    r.gain_pack[16:24] = jnp.zeros((8, 128), F32)
    pl.run_scoped(
        feed_forward,
        *[pltpu.VMEM((4 * rows, units), BF16)] * 3,
        *[pltpu.VMEM((2, rows, width), F32)] * 2,
    )

    def attention_back(grads, grad_mixed, delta, mask, grad_keys, grad_values, grad_wa):
        collect_a = [
            collect(
                p, grad_wa.at[:, c], r.ca_slots.at[:, :, c], r.wa.at[:, c], r.ca_landed.at[:, c],
                *semaphores,
            )
            for c, semaphores in zip(of_group, collect_a_semaphores)
        ]
        down_sends = [
            remote(
                r.summed.at[0, at],
                r.down_landed.at[at],
                down_semaphores[2].at[0, i],
                down_semaphores[2].at[1, i],
                (p.d, p.near),
            )
            for i, at in enumerate(pl.ds(j * (rows // 4), rows // 4) for j in range(4))
        ]
        for number in range(blocks):
            base = jnp.int32(number * rows)
            mask[number] = allowed_mask(p, r.gains[...], base, rows, 2 * rows, True)
        for copy in down_sends:
            copy.start()

        def mixed_back(slot, _):
            at = pl.ds(pl.multiple_of(slot * rows, rows), rows)
            for i in range(heads * HEAD // 256):
                grad = nn(r.tokens[slot], r.wo_whole[:, i * 256 : (i + 1) * 256]).astype(BF16)
                for j in range(256 // HEAD):
                    head = i * (256 // HEAD) + j
                    one = grad[:, j * HEAD : (j + 1) * HEAD]
                    grad_mixed[head, at] = one
                    mixed = r.mixed[at, head * HEAD : (head + 1) * HEAD]
                    row = lax.dot_general(
                        jnp.ones((8, HEAD), F32),
                        one.astype(F32) * mixed.astype(F32),
                        (((1,), (1,)), ((), ())),
                        precision=lax.Precision.HIGHEST,
                        preferred_element_type=F32,
                    )
                    delta[head, :, at] = row[0:1]
            return 0

        lax.fori_loop(0, 4, mixed_back, 0)

        def out_grads(i, _):
            chunk = collect_o.order(i)
            at = pl.ds(pl.multiple_of(chunk * 256, 256), 256)
            tokens = r.tokens[:, :, at].reshape(4 * rows, 256)
            r.wo_whole[at] = tn(tokens, r.mixed[...]).astype(BF16)
            collect_o.start(chunk, 256)
            return 0

        lax.fori_loop(0, width // 256, out_grads, 0)
        collect_m[2].halfway()
        collect_m[1].relay()
        _, _, q_gain, k_gain = gains_rows(r.gains[...])

        def head_norm_back(grad, before, gain, number, row):
            unit, scale = unit_of(before)
            cosine, sine = rotary_rows(r.rotary[number])
            back = grad * cosine - pltpu.roll(grad, 64, 1) * sine
            r.gain_pack[row : row + 1] += jnp.sum(back * unit, axis=0, keepdims=True)
            scaled = back * gain
            mean = jnp.mean(scaled * unit, axis=-1, keepdims=True)
            return (scale * (scaled - unit * mean)).astype(BF16)

        def group(g):
            grad_keys[...] = jnp.zeros_like(grad_keys)
            grad_values[...] = jnp.zeros_like(grad_values)

            for number in range(blocks):
                at = slice(number * rows, (number + 1) * rows)
                heads_here = range(g * repeat, (g + 1) * repeat)
                queries = r.q[g * repeat : (g + 1) * repeat, at].reshape(repeat * rows, HEAD)
                grad = grad_mixed[g * repeat : (g + 1) * repeat, at].reshape(repeat * rows, HEAD)
                logs = jnp.concatenate([r.lse[head, :, at] for head in heads_here], axis=1)
                sums = jnp.concatenate([delta[head, :, at] for head in heads_here], axis=1)
                grad_queries = jnp.zeros((repeat * rows, HEAD), F32)
                for kb in range(min(number + 2, blocks)):
                    here = slice(kb * rows, (kb + 1) * rows)
                    keys = r.k[g, here]
                    probs = jnp.exp2(nt(keys, queries) * (SCALE * LOG2E) - logs)
                    if kb >= number:
                        begin = (kb - number) * rows
                        part = mask[number, begin : begin + rows]
                        probs = probs * jnp.concatenate([part] * repeat, axis=1)
                    scores = (probs * (nt(r.v[g, here], grad) - sums)).astype(BF16)
                    grad_values[here] += nn(probs.astype(BF16), grad)
                    grad_keys[here] += nn(scores, queries)
                    grad_queries = grad_queries + tn(scores, keys)
                for i, head in enumerate(heads_here):
                    begin = g * wide + i * HEAD
                    grads[at, begin : begin + HEAD] = head_norm_back(
                        grad_queries[i * rows : (i + 1) * rows] * SCALE,
                        r.q_pre[head, at],
                        q_gain,
                        number,
                        16,
                    )
            key_columns = slice(g * wide + repeat * HEAD, g * wide + (repeat + 1) * HEAD)
            value_columns = slice(g * wide + (repeat + 1) * HEAD, (g + 1) * wide)
            for number in range(blocks):
                at = slice(number * rows, (number + 1) * rows)
                grads[at, key_columns] = head_norm_back(
                    grad_keys[at] * SCALE, r.k_pre[g, at], k_gain, number, 17
                )
                grads[at, value_columns] = grad_values[at].astype(BF16)

        def weight_grads(g):
            def body(i, _):
                chunk = collect_a[g].order(i)
                at = pl.ds(pl.multiple_of(chunk * 256, 256), 256)
                tokens = r.normed[:, :, at].reshape(4 * rows, 256)
                grad_wa[at, of_group[g]] = tn(tokens, grads[:, of_group[g]]).astype(BF16)
                collect_a[g].start(chunk, 256)
                return 0

            lax.fori_loop(0, width // 256, body, 0)

        def project(k):
            at = pl.ds(pl.multiple_of(home_back.block(k) * rows, rows), rows)

            def part(i):
                return lambda: nt(grads[at], r.wa_whole[i * 256 : (i + 1) * 256])

            home_back.add(k, [part(i) for i in range(width // 256)])

        for g in range(kv_heads - 1):
            group(g)
            weight_grads(g)
        collect_o.halfway()
        collect_m[2].relay()
        group(kv_heads - 1)
        for copy in down_sends:
            copy.wait_recv()
            copy.wait_send()

        def output(at):
            r.output[at] = (r.kept[0, at] + r.down_landed[at].astype(F32)).astype(BF16)

        by_rows(rows, output)
        project(0)
        project(1)
        home_back.settle_outer(0)
        home_back.settle_outer(1)
        weight_grads(kv_heads - 1)
        project(2)
        project(3)
        for part in collect_a[:-1]:
            part.halfway()
        collect_o.relay()
        home_back.settle_gate(0)
        home_back.settle_gate(1)
        home_back.settle(2)
        home_back.settle(3)
        collect_a[-1].halfway()
        for part in collect_a[:-1]:
            part.relay()
        collect_m[0].result([(r.grad_gate, 0, units, False)])
        collect_m[1].result([(r.grad_up, 0, units, False)])
        home_back.arrive()
        gain = gains_rows(r.gains[...])[0]
        r.gain_rows[...] = jnp.zeros_like(r.gain_rows)

        def norm_one_back(at):
            grad_normed = home_back.value(at)
            unit, scale = unit_of(r.x[at].astype(F32))
            r.gain_rows[...] += jnp.sum(grad_normed * unit, axis=0, keepdims=True)
            scaled = grad_normed * gain
            mean = jnp.mean(scaled * unit, axis=-1, keepdims=True)
            r.input_grad[at] += scale * (scaled - unit * mean)

        by_rows(rows, norm_one_back)
        for i in range(8):
            r.gain_pack[i : i + 1] = r.gain_rows[:, i * 128 : (i + 1) * 128]
        gains_plane.start()
        collect_a[-1].relay()
        r.plane_sum[...] = gains_plane.total()
        gains_tensor.start()
        collect_m[2].result([(r.grad_down, 0, units, turned)])
        collect_o.result([(r.grad_out, 0, nq, turned)])
        total = gains_tensor.total()
        for base, ref in (
            (0, r.grad_gain_one), (8, r.grad_gain_two), (16, r.grad_q_gain), (17, r.grad_k_gain),
        ):
            ref[...] = share(p, total, base, ref.shape[1])
        for g, part in enumerate(collect_a):
            size = repeat * HEAD
            part.result(
                [
                    (r.grad_query, g * size, size, False),
                    (r.grad_key, g * HEAD, HEAD, False),
                    (r.grad_value, g * HEAD, HEAD, False),
                ]
            )
        for part in collect_a:
            part.finish()

    pl.run_scoped(
        attention_back,
        pltpu.VMEM((4 * rows, nq + 2 * nk), BF16),
        pltpu.VMEM((heads, 4 * rows, HEAD), BF16),
        pltpu.VMEM((heads, 1, 4 * rows), F32),
        pltpu.VMEM((4, 2 * rows, rows), F32),
        pltpu.VMEM((4 * rows, HEAD), F32),
        pltpu.VMEM((4 * rows, HEAD), F32),
        pltpu.VMEM((width, nq + 2 * nk), BF16),
    )
    for part in (
        gains_out, gains_plane, gains_tensor, fan_back, quad_ct, home_back, *collect_m, collect_o,
    ):
        part.finish()


def call(dp, tensor, x, starts, gain_one, q_gain, k_gain, gain_two, wq, wk, wv, wo, wg, wu, wd, ct):
    rows, width = x.shape
    tokens = rows * tensor
    shard, nq = wq.shape
    nk, units = wk.shape[1], wg.shape[1]
    heads, kv_heads = nq // HEAD, nk // HEAD
    na, nm = nq + 2 * nk, 3 * units
    turned = shard % 128 == 0
    if not turned:
        wo, wd = wo.T, wd.T
    inputs = dict(
        x=x, starts=starts, gain_one=gain_one, q_gain=q_gain, k_gain=k_gain, gain_two=gain_two,
        wq=wq, wk=wk, wv=wv, wo=wo, wg=wg, wu=wu, wd=wd, ct=ct,
        rotary=jnp.asarray(rotary(tokens)).reshape(tensor, rows, HEAD),
    )
    outputs = dict(
        output=((rows, width), BF16),
        input_grad=((rows, width), F32),
        grad_gain_one=(gain_one.shape, F32),
        grad_q_gain=(q_gain.shape, F32),
        grad_k_gain=(k_gain.shape, F32),
        grad_query=((shard, nq), F32),
        grad_key=((shard, nk), F32),
        grad_value=((shard, nk), F32),
        grad_out=((nq, shard) if turned else (shard, nq), F32),
        grad_gain_two=(gain_two.shape, F32),
        grad_gate=((shard, units), F32),
        grad_up=((shard, units), F32),
        grad_down=((units, shard) if turned else (shard, units), F32),
    )
    scratch = dict(
        pack=((24, 128), F32),
        gain_slots=((dp, 24, 128), F32),
        gains=((24, 128), F32),
        gain_pack=((24, 128), F32),
        gain_rows=((1, width), F32),
        plane_slots=((dp, 24, 128), F32),
        plane_sum=((24, 128), F32),
        tensor_slots=((tensor, 24, 128), F32),
        tokens=((4, rows, width), BF16),
        normed=((4, rows, width), BF16),
        block=((rows, width), BF16),
        q=((heads, tokens, HEAD), BF16),
        k=((kv_heads, tokens, HEAD), BF16),
        v=((kv_heads, tokens, HEAD), BF16),
        q_pre=((heads, tokens, HEAD), F32),
        k_pre=((kv_heads, tokens, HEAD), F32),
        mixed=((tokens, nq), BF16),
        lse=((heads, 1, tokens), F32),
        normed_two=((4, rows, width), BF16),
        ct_whole=((4, rows, width), BF16),
        wa=((shard, na), BF16),
        wa_stage=((shard, na), BF16),
        wa_whole=((width, na), BF16),
        wo_shard=((shard, nq), BF16),
        wo_stage=((shard, nq), BF16),
        wo_whole=((width, nq), BF16),
        wm=((shard, nm), BF16),
        wm_stage=((shard, nm), BF16),
        wm_whole=((width, nm), BF16),
        kept=((2, rows, width), F32),
        passed=((rows, width), BF16),
        given=((2, rows, width), BF16),
        taken=((2, rows, width), BF16),
        summed=((2, rows, width), BF16),
        landed=((2, rows, width), BF16),
        down_landed=((rows, width), BF16),
        back_given=((2, rows, width), BF16),
        back_taken=((2, rows, width), BF16),
        back_summed=((rows, width), BF16),
        back_landed=((rows, width), BF16),
        cm_slots=((dp, shard, nm), BF16),
        cm_landed=((shard, nm), BF16),
        co_slots=((dp, shard, nq), BF16),
        co_landed=((shard, nq), BF16),
        ca_slots=((dp, shard, na), BF16),
        ca_landed=((shard, na), BF16),
    )
    semaphores = [
        *exchange_semaphores(dp),
        *exchange_semaphores(dp),
        *exchange_semaphores(tensor),
        *FAN_SEMAPHORES,
        *FAN_SEMAPHORES,
        *(spread_semaphores(dp) * 5),
        *QUAD_SEMAPHORES,
        *QUAD_SEMAPHORES,
        *HOME_SEMAPHORES,
        *HOME_SEMAPHORES,
        *PAIR_SEMAPHORES,
        *PAIR_SEMAPHORES,
        *(collect_semaphores(dp) * (4 + kv_heads)),
    ]
    names = [*inputs, *outputs, *scratch]

    def body(*refs):
        layer_refs = list(refs)
        layer(dp, tensor, turned, names, *layer_refs)

    in_specs = vmem(len(inputs))
    in_specs[1] = pl.BlockSpec(memory_space=pltpu.SMEM)
    return pl.pallas_call(
        body,
        out_shape=[jax.ShapeDtypeStruct(*s) for s in outputs.values()],
        in_specs=in_specs,
        out_specs=vmem(len(outputs)),
        scratch_shapes=[pltpu.VMEM(*s) for s in scratch.values()] + semaphores,
        compiler_params=params(1),
    )(*inputs.values()), turned


def copies_kernel(count, *refs):
    for source, target in zip(refs[:count], refs[count:]):
        target[...] = source[...]


def copied(arrays):
    return pl.pallas_call(
        functools.partial(copies_kernel, len(arrays)),
        out_shape=[jax.ShapeDtypeStruct(a.shape, a.dtype) for a in arrays],
        in_specs=vmem(len(arrays)),
        out_specs=vmem(len(arrays)),
    )(*arrays)


def shards(dp, tensor, *args):
    x, starts, attn_gain, q_gain, k_gain, wq, wk, wv, wo, mlp_gain, wg, wu, wd, ct = args
    outs, turned = call(
        dp, tensor, x[0], starts, attn_gain[None], q_gain[None], k_gain[None], mlp_gain[None],
        wq, wk, wv, wo, wg, wu, wd, ct[0],
    )
    outs = list(copied(outs))
    for i in (0, 1):
        outs[i] = outs[i][None]
    for i in (2, 3, 4, 9):
        outs[i] = outs[i][0]
    if not turned:
        for i in (8, 12):
            outs[i] = outs[i].T
    return tuple(outs)


def solution(mesh):
    sequence, square, turned = P("dp", "tensor", None), P("dp", "tensor"), P("tensor", "dp")
    gain = P("dp")
    in_specs = (
        sequence, P("dp", None), gain, gain, gain, square, square, square, turned, gain, square, square,
        turned, sequence,
    )
    out_specs = (
        sequence, sequence, gain, gain, gain, square, square, square, turned, gain, square, square,
        turned,
    )
    return jax.shard_map(
        functools.partial(shards, mesh.shape["dp"], mesh.shape["tensor"]),
        mesh=mesh,
        in_specs=in_specs,
        out_specs=out_specs,
        check_vma=False,
    )
```
